128 devices in a mesh: group: 4 (over z), dev: 32 (over y, x, core).
Axes of the slice: x: 4, y: 4, z: 4, core: 2. Of those that a mesh axis runs over, the one named last changes fastest.
Arguments:
- store_states: bfloat16 [8192, 8, 2048], P(('group', 'dev')), may hold values from -6 to 6
- store_keys: bfloat16 [8192, 768], P(('group', 'dev')), may hold values from -6 to 6
- passage_ids: int32 [128, 32], replicated, may hold values from 0 to 8191, as said below
- store_slot: int32 [8192], replicated, may hold values from 0 to 8191, as said below
- row_question: int32 [4, 32], P('group'), may hold values from 0 to 31, each once within a row
- queries: bfloat16 [128, 8, 2048], P(('group', 'dev')), may hold values from -480 to 480
- question_emb: bfloat16 [128, 768], P(('group', 'dev')), may hold values from -6 to 6
- enc_gain: float32 [2048], replicated, may hold values from 0.5 to 1.5
- key_weight: bfloat16 [2048, 2048], replicated, may hold values from -0.125 to 0.125
- value_weight: bfloat16 [2048, 2048], replicated, may hold values from -0.125 to 0.125
Outputs:
- context: bfloat16 [128, 8, 2048], P(('group', 'dev'))
- distill_loss: float32 [128], P(('group', 'dev'))
- key_grad: float32 [8192, 768], P(('group', 'dev'))
The draws below stay inside these ranges and needn't reach their ends.
Inputs may be any that keep to these rules, and one draw needn't show every extreme that they name: `passage_ids`: call the passages in slots k with k % (size of dev) = d of questions g * 32 to (g + 1) * 32 - 1 the requests of device (g, d); store row r lies on device r // 64 in group+dev order. All requests of one device lie on store devices of one group index; at most 2 of them lie on store devices of any one dev index; one store device holds at most 16 requests of the devices of one group. Both bounds are reached in every draw. `store_slot`: A permutation of the store rows. `row_question`: each row is a permutation of the questions of the group.
All inputs are finite; a program needn't handle non-finite values.
Results may differ from the reference program's by a relative error of at most 0.017.
The reference program's roundings to bfloat16 on the way (of `normed`, `weights` and `grad_rows`) count: a program that leaves them out, or rounds other values in their place, can miss the bound.
Values may be sent and summed in bfloat16 or wider, within the bound.
A program may use at most 128 MiB of HBM per device.

```python
import math
import jax
import jax.numpy as jnp
from jax import lax

D = 2048
HEADS = 32
HEAD_DIM = 64
E = 768
K = 32
PLEN = 8
A = 8
P_DEV = 64
QG = 32
QUESTIONS = 128
K_DEV = 1
R = 32
C2 = 2
N_STORE = 8192
N_GROUP = 4
N_DEV = 32


def request_layout(key):
    subkeys = jax.random.split(key, 8)
    readers = N_GROUP * N_DEV
    pair_count = N_DEV // 2
    first_part = jax.random.randint(subkeys[0], (readers, pair_count), 0, C2 + 1)
    forced_column = jax.random.randint(subkeys[1], (), 0, N_DEV)
    forced_group = jax.random.randint(subkeys[2], (), 0, N_GROUP)
    forced_residue = jax.random.randint(subkeys[3], (), 0, N_GROUP)
    row_shift = jax.random.randint(subkeys[4], (), 0, N_GROUP)
    reader_index = jnp.arange(readers, dtype=jnp.int32)
    reader_group = reader_index // N_DEV
    reader_device = reader_index % N_DEV
    forced = (reader_group == forced_group) & (reader_device % N_GROUP == forced_residue)
    forced_value = jnp.where(forced_column % 2 == 0, C2, 0)
    pair_index = jnp.arange(pair_count, dtype=jnp.int32)
    forced_pair = forced[:, None] & (pair_index[None, :] == forced_column // 2)
    first_part = jnp.where(forced_pair, forced_value, first_part)
    counts = jnp.stack([first_part, C2 - first_part], axis=2).reshape(readers, N_DEV)
    run_ends = jnp.cumsum(counts, axis=1)
    positions = jnp.arange(R, dtype=jnp.int32)
    column = jnp.sum((run_ends[:, None, :] <= positions[None, :, None]).astype(jnp.int32), axis=2)
    scores = jax.random.randint(subkeys[5], (readers, R), 0, 1 << 20) * R + positions[None, :]
    shuffle = jnp.argsort(scores, axis=1)
    column = jnp.take_along_axis(column, shuffle, axis=1)
    local_row = jax.random.randint(subkeys[6], (readers, R), 0, P_DEV)
    owner_row = (reader_group + reader_device + row_shift) % N_GROUP
    owner_index = owner_row[:, None] * N_DEV + column
    store_rows = owner_index * P_DEV + local_row
    store_rows = store_rows.reshape(N_GROUP, N_DEV, QG, K_DEV).transpose(0, 2, 3, 1).reshape(QUESTIONS, K)
    slot_table = jax.random.permutation(subkeys[7], N_STORE).astype(jnp.int32)
    return (store_rows.astype(jnp.int32), slot_table)


def draw_passage_ids(key, part):
    store_rows, slot_table = request_layout(key)
    passage_table = jnp.zeros((N_STORE,), jnp.int32).at[slot_table].set(jnp.arange(N_STORE, dtype=jnp.int32))
    return passage_table[store_rows]


def draw_store_slot(key, part):
    store_rows, slot_table = request_layout(key)
    return slot_table


def draw_queries(key, part):
    key = jax.random.fold_in(key, 3)
    subkeys = jax.random.split(key, 3)
    shape_full = (QUESTIONS, A, HEADS, HEAD_DIM)
    shape_head = (QUESTIONS, A, HEADS, 1)
    base = jnp.clip(jax.random.normal(subkeys[0], shape_full, jnp.float32), -6.0, 6.0)
    lower = 4.0
    upper = 80.0
    sharp = jax.random.bernoulli(subkeys[1], 0.5, shape_head)
    level = jnp.exp(jax.random.uniform(subkeys[2], shape_head, jnp.float32, math.log(lower), math.log(upper)))
    factor = jnp.where(sharp, level, 1.0)
    return (base * factor).reshape(QUESTIONS, A, HEADS * HEAD_DIM).astype(jnp.bfloat16)


def levels(key, dims, cuts, smallest, high):
    gain = 1.0
    for dim, blocks in cuts:
        steps = jax.random.uniform(jax.random.fold_in(jax.random.fold_in(key, 6), dim), (blocks,), jnp.float32, smallest / len(cuts), high / len(cuts))
        gain = gain * jnp.repeat(jnp.exp(steps), dims[dim] // blocks).reshape((-1,) + (1,) * (len(dims) - 1 - dim))
    return gain


def normal_values(own_key, dims, deviation, reach, cuts=(), kind=jnp.bfloat16):
    result = jax.random.normal(own_key, dims, jnp.float32) * deviation
    if len(cuts) > 0:
        result = levels(own_key, dims, cuts, -0.22, 0.18) * result
    return jnp.clip(result, min=-reach, max=reach).astype(kind)


def setup_inputs(seed: int = 0) -> dict:
    arg_keys = jax.random.split(jax.random.key(seed), 11)
    return {
        "store_states": normal_values(arg_keys[0], (N_STORE, PLEN, D), 1.0, 6.0, ((0, 128),)),
        "store_keys": normal_values(arg_keys[1], (N_STORE, E), 1.0, 6.0, ((0, 128),)),
        "passage_ids": draw_passage_ids(jax.random.fold_in(arg_keys[10], 71), 0),
        "store_slot": draw_store_slot(jax.random.fold_in(arg_keys[10], 71), 0),
        "row_question": jax.vmap(lambda own: jax.random.permutation(own, QG))(jax.random.split(arg_keys[4], N_GROUP)).reshape((N_GROUP, QG)).astype(jnp.int32),
        "queries": draw_queries(jax.random.fold_in(arg_keys[10], 71), 0),
        "question_emb": normal_values(arg_keys[6], (QUESTIONS, E), 1.0, 6.0, ((0, 128),)),
        "enc_gain": jnp.clip(1.0 + 0.1 * jax.random.normal(arg_keys[7], (D,), jnp.float32), 0.5, 1.5),
        "key_weight": normal_values(arg_keys[8], (D, D), D ** -0.5, 0.125),
        "value_weight": normal_values(arg_keys[9], (D, D), D ** -0.5, 0.125),
    }


epsilon = 1e-06
loss_weight = 256.0

def rms_scale(states, enc_gain):
    values = states.astype(jnp.float32)
    mean_square = lax.optimization_barrier(jnp.mean(values * values, axis=-1, keepdims=True))
    return (values * lax.rsqrt(mean_square + epsilon) * enc_gain).astype(jnp.bfloat16)

def reference(store_states, store_keys, passage_ids, store_slot, row_question, queries, question_emb, enc_gain, key_weight, value_weight):
    store_rows = store_slot[passage_ids]
    question_of = (jnp.arange(N_GROUP, dtype=jnp.int32)[:, None] * QG + row_question).reshape(-1).astype(jnp.int32)
    attn_scale = HEAD_DIM ** (-0.5)
    retrieval_scale = E ** (-0.5)

    def decode_row(row_index):
        listed = store_rows[question_of[row_index]]
        normed = rms_scale(store_states[listed], enc_gain).reshape(K * PLEN, D)
        key_cross = jnp.dot(normed, key_weight, preferred_element_type=jnp.float32).astype(jnp.bfloat16)
        value_cross = jnp.dot(normed, value_weight, preferred_element_type=jnp.float32).astype(jnp.bfloat16)
        query_heads = queries[row_index].reshape(A, HEADS, HEAD_DIM).astype(jnp.float32)
        key_heads = key_cross.reshape(K * PLEN, HEADS, HEAD_DIM).astype(jnp.float32)
        value_heads = value_cross.reshape(K * PLEN, HEADS, HEAD_DIM).astype(jnp.float32)
        scores = jnp.einsum('ahe,lhe->hal', query_heads, key_heads) * attn_scale
        peak_score = lax.optimization_barrier(jnp.max(scores, axis=-1, keepdims=True))
        exp_scores = jnp.exp(scores - peak_score)
        totals = lax.optimization_barrier(jnp.sum(exp_scores, axis=-1, keepdims=True))
        weights = lax.optimization_barrier(exp_scores.astype(jnp.bfloat16)).astype(jnp.float32)
        context = jnp.einsum('hal,lhe->ahe', weights, value_heads) / jnp.transpose(totals, (1, 0, 2))
        context = context.reshape(A, D).astype(jnp.bfloat16)
        passage_mass = lax.optimization_barrier(jnp.sum((exp_scores / totals).reshape(HEADS, A, K, PLEN), axis=(0, 1, 3))) / (HEADS * A)
        passage_key = store_keys[listed]
        retrieval = jnp.dot(passage_key, question_emb[row_index], preferred_element_type=jnp.float32) * retrieval_scale
        log_prob = jax.nn.log_softmax(retrieval)
        distill_loss = jnp.sum(passage_mass * (jnp.log(passage_mass) - log_prob))
        coefficient = loss_weight * retrieval_scale * (jnp.exp(log_prob) - passage_mass)
        grad_rows = (coefficient[:, None] * question_emb[row_index].astype(jnp.float32)[None, :]).astype(jnp.bfloat16)
        return (context, distill_loss, grad_rows)
    contexts, losses, grad_rows = lax.map(decode_row, jnp.arange(QUESTIONS, dtype=jnp.int32))
    targets = store_rows[question_of].reshape(-1)
    key_grad = jnp.zeros((N_STORE, E), jnp.float32).at[targets].add(grad_rows.reshape(-1, E).astype(jnp.float32))
    return (contexts, losses, key_grad)
```

```python
import functools

import jax
import jax.numpy as jnp
from jax import lax
from jax.experimental import pallas as pl
from jax.experimental.pallas import tpu as pltpu
from jax.sharding import PartitionSpec as P

MESH = pl.DeviceIdType.MESH
F32 = jnp.float32
BF16 = jnp.bfloat16
HIGHEST = lax.Precision.HIGHEST

D = 2048
E = 768
GROUPS = 4
PER_GROUP = 32
SLOTS = 16
LANES = 128
STORE = 64
EPS = 1e-06
LOSS_WEIGHT = 256.0
ABSENT = -1e30

ORDERS = (("x", "y", "z"), ("y", "z", "x"), ("z", "x", "y"))
AG, AG_SIB, RQ, AR, RS = 0, 27, 39, 42, 75
SEMS = 105


def nt(a, b, precision=None):
    return lax.dot_general(
        a, b, (((1,), (1,)), ((), ())), preferred_element_type=F32, precision=precision
    )


def nn(a, b, precision=None):
    return jnp.dot(a, b, preferred_element_type=F32, precision=precision)


def iota(shape, dim):
    return lax.broadcasted_iota(jnp.int32, shape, dim)


def block_of(part, g, j):
    y, x, core = j // 8, (j // 2) % 4, j % 2
    at = {"x": x, "y": y, "z": g}
    first, second, third = ORDERS[part]
    return core * 64 + at[third] * 16 + at[second] * 4 + at[first]


def add_blocks(part, blocks):
    total = blocks[0].astype(F32)
    for block in blocks[1:]:
        total = total + block.astype(F32)
    if part < 2:
        return total, total.astype(BF16)
    loss = total[0:8, 256:384] + total[8:16, 256:384]
    high = loss.astype(BF16).astype(F32)
    tile = jnp.concatenate([high, loss - high], axis=0)
    return total, jnp.concatenate([total[:, 0:256], tile], axis=1).astype(BF16)


def kernel(
    rows_ref,
    lane_ref,
    col_ref,
    own_rq_ref,
    states_ref,
    keys_ref,
    queries_ref,
    emb_ref,
    gain_ref,
    kw_ref,
    vw_ref,
    ctx_ref,
    loss_ref,
    grad_ref,
    st,
    w,
    nrm,
    kv,
    q0,
    q1,
    q2,
    c0,
    c1,
    c2,
    rc0,
    rc1,
    rc2,
    ra0,
    ra1,
    ra2,
    rb0,
    rb1,
    rb2,
    rd0,
    rd1,
    rd2,
    s_buf,
    p_buf,
    t0,
    t1,
    t2,
    ac0,
    ac1,
    ac2,
    ar0,
    ar1,
    ar2,
    acc0,
    acc1,
    acc2,
    l0,
    l1,
    l2,
    rqt,
    ir_ref,
    loss_t,
    send_sem,
    recv_sem,
    local_sem,
):
    qs, cs, rcs = (q0, q1, q2), (c0, c1, c2), (rc0, rc1, rc2)
    rstage = ((ra0, ra1, ra2), (rb0, rb1, rb2), (rd0, rd1, rd2))
    ts, acs, ars, accs, ls = (
        (t0, t1, t2),
        (ac0, ac1, ac2),
        (ar0, ar1, ar2),
        (acc0, acc1, acc2),
        (l0, l1, l2),
    )
    my_group = lax.axis_index("group")
    my_dev = lax.axis_index("dev")
    core = my_dev % 2
    at = {"x": (my_dev // 2) % 4, "y": my_dev // 8, "z": my_group}
    sibling = (my_group, my_dev + 1 - 2 * core)

    def peer(axis, step):
        to = (at[axis] + step) % 4
        if axis == "z":
            return (to, my_dev)
        if axis == "y":
            return (my_group, to * 8 + at["x"] * 2 + core)
        return (my_group, at["y"] * 8 + to * 2 + core)

    started = []

    def remote(src, dst, number, device):
        copy = pltpu.make_async_remote_copy(
            src_ref=src,
            dst_ref=dst,
            send_sem=send_sem.at[number],
            recv_sem=recv_sem.at[number],
            device_id=device,
            device_id_type=MESH,
        )
        return copy

    def start(src, dst, number, device):
        copy = remote(src, dst, number, device)
        copy.start()
        started.append(copy)

    def arrived(dst, number):
        remote(dst, dst, number, sibling).wait_recv()

    states_copy = pltpu.make_async_copy(states_ref, st, local_sem.at[8])
    states_copy.start()
    w_copies = []
    for n in range(8):
        src = kw_ref if n < 4 else vw_ref
        copy = pltpu.make_async_copy(
            src.at[:, pl.ds((n % 4) * 512, 512)],
            w.at[:, pl.ds(n * 512, 512)],
            local_sem.at[n],
        )
        copy.start()
        w_copies.append(copy)

    mine = [
        core * 64 + at[ORDERS[p][2]] * 16 + at[ORDERS[p][1]] * 4 + at[ORDERS[p][0]]
        for p in range(3)
    ]
    for c in range(8):
        tile = jnp.concatenate(
            [
                queries_ref[0, :, c * 128 : c * 128 + 128].astype(F32),
                queries_ref[0, :, 1024 + c * 128 : 1152 + c * 128].astype(F32),
            ],
            axis=0,
        )
        qs[c // 3][mine[c // 3], :, (c % 3) * 128 : (c % 3) * 128 + 128] = tile.astype(BF16)
    emb_rows = [emb_ref[:, c * 128 : c * 128 + 128].astype(F32) for c in range(6)]
    emb_tile = jnp.concatenate(emb_rows + [jnp.zeros((10, 128), F32)], axis=0)
    q2[mine[2], :, 256:384] = emb_tile.astype(BF16)
    rqt[my_group] = own_rq_ref[...]

    barrier = pltpu.get_barrier_semaphore()
    pl.semaphore_signal(barrier, inc=1, device_id=sibling, device_id_type=MESH)
    for axis in ("x", "y", "z"):
        for step in (1, 2, 3):
            pl.semaphore_signal(barrier, inc=1, device_id=peer(axis, step), device_id_type=MESH)
    pl.semaphore_wait(barrier, 10)

    def span(p, stage, back):
        first, second, third = ORDERS[p]
        digit = (at[ORDERS[p][stage]] + 4 - back) % 4
        if stage == 0:
            return core * 64 + at[third] * 16 + at[second] * 4 + digit, 1
        if stage == 1:
            return core * 64 + at[third] * 16 + digit * 4, 4
        return core * 64 + digit * 16, 16

    def gather_start(stage):
        for p in range(3):
            begin, size = span(p, stage, 0)
            for step in (1, 2, 3):
                ref = qs[p].at[pl.ds(begin, size)]
                start(ref, ref, AG + (p * 3 + stage) * 3 + step - 1, peer(ORDERS[p][stage], step))

    def gather_wait(p, stage, step):
        begin, size = span(p, stage, step)
        arrived(qs[p].at[pl.ds(begin, size)], AG + (p * 3 + stage) * 3 + step - 1)

    def forward(p, back):
        begin, size = span(p, 2, back)
        ref = qs[p].at[pl.ds(begin, size)]
        start(ref, ref, AG_SIB + p * 4 + back, sibling)

    gather_start(0)
    for step in (1, 2, 3):
        start(own_rq_ref, rqt.at[my_group], RQ + step - 1, peer("z", step))

    states_copy.wait()

    def norm_pair(pair, carry):
        both = []
        for half in range(2):
            values = st[rows_ref[pair * 2 + half]].astype(F32)
            mean_square = jnp.mean(values * values, axis=-1, keepdims=True)
            both.append(values * lax.rsqrt(mean_square + EPS) * gain_ref[...])
        nrm[pl.ds(pl.multiple_of(pair * 16, 16), 16), :] = jnp.concatenate(both, axis=0).astype(BF16)
        return carry

    lax.fori_loop(0, 32, norm_pair, 0)

    def project(begin, end):
        def step(n, carry):
            offset = pl.multiple_of(n * 256, 256)
            kv[:, pl.ds(offset, 256)] = nn(nrm[...], w[:, pl.ds(offset, 256)]).astype(BF16)
            return carry

        for n in range(begin, end):
            w_copies[n].wait()
        lax.fori_loop(begin * 2, end * 2, step, 0)

    for p in range(3):
        for step in (1, 2, 3):
            gather_wait(p, 0, step)
    gather_start(1)
    project(0, 2)
    for p in range(3):
        for step in (1, 2, 3):
            gather_wait(p, 1, step)
    gather_start(2)
    for p in range(3):
        forward(p, 0)
    project(2, 6)
    for step in (1, 3, 2):
        for p in range(3):
            gather_wait(p, 2, step)
            forward(p, step)
    project(6, 8)

    for step in (1, 2, 3):
        arrived(rqt.at[(my_group + 4 - step) % 4], RQ + step - 1)
    for g in range(4):
        match = rqt[g, 0:32, :] == lane_ref[g : g + 1, :]
        row = jnp.sum(jnp.where(match, iota((32, 128), 0) + (g * 32 + 1), 0), axis=0, keepdims=True)
        ir_ref[g : g + 1, :] = row - 1

    for p in range(3):
        for back in range(4):
            first, second, third = ORDERS[p]
            begin = (1 - core) * 64 + ((at[third] + 4 - back) % 4) * 16
            arrived(qs[p].at[pl.ds(begin, 16)], AG_SIB + p * 4 + back)

    lane = iota((1, 128), 1)
    low = (lane < 64).astype(F32).astype(BF16)
    high = (lane >= 64).astype(F32).astype(BF16)

    def scores_of(p, tiles):
        def step(n, carry):
            g, cc = n // tiles, n % tiles
            inner = pl.multiple_of(cc * 128, 128)
            outer = pl.multiple_of((3 * p + cc) * 128, 128)
            slots = pl.ds(pl.multiple_of(g * 128, 128), 128)
            right = jnp.concatenate(
                [kv[slots, pl.ds(outer, 128)], kv[slots, pl.ds(outer + 1024, 128)]], axis=0
            )
            row = ir_ref[pl.ds(g, 1), :] - g * 32
            total = [jnp.zeros((8, 128), F32) for _ in range(4)]
            for jb in range(2):
                left = []
                for jj in range(16):
                    block = qs[p][block_of(p, g, jb * 16 + jj), :, pl.ds(inner, 128)]
                    left += [block * low, block * high]
                out = nt(jnp.concatenate(left, axis=0), right)
                for jj in range(16):
                    keep = jnp.broadcast_to(row == jb * 16 + jj, (8, 128))
                    for tile in range(4):
                        half = tile % 2
                        begin = jj * 32 + tile * 8
                        piece = out[begin : begin + 8, half * 128 : half * 128 + 128]
                        total[tile] = jnp.where(keep, piece, total[tile])
            rows = pl.ds(pl.multiple_of((3 * p + cc) * 32, 32), 32)
            s_buf[g, rows, :] = jnp.concatenate(total, axis=0) * (64 ** (-0.5))
            return carry

        lax.fori_loop(0, 4 * tiles, step, 0)

    scores_of(0, 3)
    scores_of(1, 3)
    scores_of(2, 2)

    sub = iota((128, 128), 0)
    lanes = iota((128, 128), 1)
    peak_i = jnp.zeros((256, 128), F32)
    total_i = jnp.zeros((256, 128), F32)
    present = jnp.zeros((8, 128), F32)
    for g in range(4):
        scores = s_buf[g]
        u_row = lane_ref[g : g + 1, :]
        peak = scores
        for s in (1, 2, 4):
            bit = jnp.broadcast_to((lane // s) % 2 == 1, (256, 128))
            other = jnp.where(bit, pltpu.roll(peak, s, 1), pltpu.roll(peak, 128 - s, 1))
            peak = jnp.maximum(peak, other)
        u_rows = jnp.broadcast_to(u_row, (8, 128))
        before = pltpu.roll(u_rows, 8, 1)[0:1, :]
        for s in (8, 16, 32, 64):
            same = (pltpu.roll(u_rows, s, 1)[0:1, :] == u_row) & (lane >= s)
            other = jnp.where(jnp.broadcast_to(same, (256, 128)), pltpu.roll(peak, s, 1), ABSENT)
            peak = jnp.maximum(peak, other)
        for s in (8, 16, 32, 64):
            same = (pltpu.roll(u_rows, 128 - s, 1)[0:1, :] == u_row) & (lane < 128 - s)
            other = jnp.where(
                jnp.broadcast_to(same, (256, 128)), pltpu.roll(peak, 128 - s, 1), ABSENT
            )
            peak = jnp.maximum(peak, other)
        chosen = sub == ir_ref[g : g + 1, :]
        first = ((before != u_row) | (lane < 8)) & (lane % 8 == 0)
        lead = jnp.where(chosen & jnp.broadcast_to(first, (128, 128)), 1.0, 0.0)
        peak_i = peak_i + nt(peak, lead, HIGHEST)
        total_i = total_i + nt(jnp.exp(scores - peak), jnp.where(chosen, 1.0, 0.0), HIGHEST)
        present = present + nt(jnp.ones((8, 128), F32), lead)
    table = jnp.where(
        jnp.broadcast_to(present[0:1, :] > 0.5, (256, 128)),
        peak_i + jnp.log(jnp.maximum(total_i, 1e-30)),
        ABSENT,
    )
    t0[...] = table[0:128, :]
    t1[...] = table[128:256, :]

    u_col = jnp.concatenate([col_ref[:, 0:1]], axis=0)
    k_col = col_ref[:, 1:2]
    row_col = col_ref[:, 2:3]
    valid = u_col >= 0
    lane64 = iota((64, 128), 1)
    slot_group = iota((64, 128), 0) // 16
    row_question = jnp.concatenate(
        [jnp.broadcast_to(rqt[g, 32:33, :], (16, 128)) for g in range(4)], axis=0
    )
    one_hot_i = (row_question == u_col) & (lane64 // 32 == slot_group)
    hot_i = jnp.where(one_hot_i, 1.0, 0.0)
    j_col = jnp.sum(jnp.where(one_hot_i, lane64 % 32, 0), axis=1, keepdims=True)
    place = block_of(2, slot_group[:, 0:1], j_col) * 16
    flat = q2[:, :, 256:384].reshape(2048, 128)
    wide = iota((64, 2048), 1)
    emb = jnp.concatenate(
        [nn(jnp.where(wide == place + c, 1.0, 0.0).astype(BF16), flat) for c in range(6)], axis=1
    )
    hot_row = jnp.where(iota((64, 64), 1) == row_col, 1.0, 0.0).astype(BF16)
    keys = nn(hot_row, keys_ref[...])
    retrieval = jnp.sum(emb * keys, axis=1, keepdims=True) * (E ** (-0.5))
    square = iota((64, 64), 0) == iota((64, 64), 1)
    retrieval_row = jnp.sum(jnp.where(square, retrieval, 0.0), axis=0, keepdims=True)
    k_row = lane_ref[4:5, 0:64]
    by_k = jnp.where(iota((32, 64), 0) == k_row, retrieval_row, 0.0)
    t2[...] = nn(by_k, hot_i, HIGHEST)

    size = (64, 64, 16)

    def combine(p, values):
        if p == 2:
            total = values[0]
            for value in values[1:]:
                total = total + value
            return total
        top = values[0]
        for value in values[1:]:
            top = jnp.maximum(top, value)
        total = jnp.exp(values[0] - top)
        for value in values[1:]:
            total = total + jnp.exp(value - top)
        return top + jnp.log(total)

    for p in range(3):
        other = pl.ds(pl.multiple_of((1 - core) * size[p], size[p]), size[p])
        start(ts[p].at[other], acs[p], AR + p * 11, sibling)
    for p in range(3):
        own = pl.ds(pl.multiple_of(core * size[p], size[p]), size[p])
        arrived(acs[p], AR + p * 11)
        accs[p][0] = combine(p, [ts[p][own, :], acs[p][...]])
        for step in (1, 2, 3):
            start(
                accs[p].at[0],
                ars[p].at[step - 1],
                AR + p * 11 + step,
                peer(ORDERS[p][0], step),
            )
    for stage in range(3):
        for p in range(3):
            values = [accs[p][stage]]
            for step in (1, 2, 3):
                arrived(ars[p].at[stage * 3 + step - 1], AR + p * 11 + stage * 3 + step)
                values.append(ars[p][stage * 3 + step - 1])
            total = combine(p, values)
            own = pl.ds(pl.multiple_of(core * size[p], size[p]), size[p])
            if stage == 2:
                ls[p][own, :] = total
                ref = ls[p].at[own]
                start(ref, ref, AR + p * 11 + 10, sibling)
            else:
                accs[p][stage + 1] = total
                for step in (1, 2, 3):
                    start(
                        accs[p].at[stage + 1],
                        ars[p].at[(stage + 1) * 3 + step - 1],
                        AR + p * 11 + (stage + 1) * 3 + step,
                        peer(ORDERS[p][stage + 1], step),
                    )
    for p in range(3):
        other = pl.ds(pl.multiple_of((1 - core) * size[p], size[p]), size[p])
        arrived(ls[p].at[other], AR + p * 11 + 10)

    log_sum = jnp.concatenate([l0[...], l1[...]], axis=0)
    targets = []
    for g in range(4):
        chosen = jnp.where(sub == ir_ref[g : g + 1, :], 1.0, 0.0)
        weights = jnp.exp(s_buf[g] - nn(log_sum, chosen, HIGHEST))
        p_buf[g] = weights.astype(BF16)
        mass = jnp.sum(weights, axis=0, keepdims=True)
        own = iota((16, 128), 1) // 8 == iota((16, 128), 0)
        targets.append(jnp.sum(jnp.where(own, mass, 0.0), axis=1, keepdims=True))
    target = jnp.concatenate(targets, axis=0) * (1.0 / 256.0)
    raw = l2[...]
    top = jnp.max(raw, axis=0, keepdims=True)
    log_prob_all = raw - top - jnp.log(jnp.sum(jnp.exp(raw - top), axis=0, keepdims=True))
    hot_k = jnp.where(iota((64, 32), 1) == k_col, 1.0, 0.0)
    log_prob = jnp.sum(
        jnp.where(one_hot_i, nn(hot_k, log_prob_all, HIGHEST), 0.0), axis=1, keepdims=True
    )
    term = jnp.where(valid, target * (jnp.log(target) - log_prob), 0.0)
    loss_row = jnp.sum(jnp.where(one_hot_i, term, 0.0), axis=0, keepdims=True)
    loss_col = jnp.sum(jnp.where(sub == lanes, loss_row, 0.0), axis=1, keepdims=True)
    loss_t[...] = jnp.broadcast_to(loss_col, (128, 128))

    def loss_block(j, carry):
        for g in range(4):
            value = jnp.broadcast_to(loss_t[pl.ds(g * 32 + j, 1), :], (8, 128))
            top_half = value.astype(BF16).astype(F32)
            tile = jnp.concatenate([top_half, value - top_half], axis=0)
            c2[block_of(2, g, j), :, 256:384] = tile.astype(BF16)
        return carry

    lax.fori_loop(0, 32, loss_block, 0)

    keep_low = jnp.broadcast_to(lane < 64, (8, 128))

    def context_of(p, tiles):
        def step(n, carry):
            g, cc = n // tiles, n % tiles
            inner = pl.multiple_of(cc * 128, 128)
            outer = pl.multiple_of(D + (3 * p + cc) * 128, 128)
            slots = pl.ds(pl.multiple_of(g * 128, 128), 128)
            right = jnp.concatenate(
                [kv[slots, pl.ds(outer, 128)], kv[slots, pl.ds(outer + 1024, 128)]], axis=1
            )
            row = ir_ref[pl.ds(g, 1), :] - g * 32
            rows = pl.ds(pl.multiple_of((3 * p + cc) * 32, 32), 32)
            weights = p_buf[g, rows, :]
            for jb in range(2):
                left = []
                for jj in range(16):
                    keep = jnp.where(row == jb * 16 + jj, 1.0, 0.0).astype(BF16)
                    left.append(weights * keep)
                out = nn(jnp.concatenate(left, axis=0), right)
                for jj in range(16):
                    halves = []
                    for half in range(2):
                        cols = slice(half * 128, half * 128 + 128)
                        begin = jj * 32 + half * 8
                        halves.append(
                            jnp.where(
                                keep_low,
                                out[begin : begin + 8, cols],
                                out[begin + 16 : begin + 24, cols],
                            )
                        )
                    tile = jnp.concatenate(halves, axis=0).astype(BF16)
                    cs[p][block_of(p, g, jb * 16 + jj), :, pl.ds(inner, 128)] = tile
            return carry

        lax.fori_loop(0, 4 * tiles, step, 0)

    def swap_start(p):
        start(cs[p].at[pl.ds((1 - core) * 64, 64)], rcs[p], RS + p * 10, sibling)

    def reach(p, stage, to):
        first, second, third = ORDERS[p]
        if stage == 0:
            return core * 64 + to * 16, 16
        if stage == 1:
            return core * 64 + at[third] * 16 + to * 4, 4
        return core * 64 + at[third] * 16 + at[second] * 4 + to, 1

    def scatter_start(p, stage):
        axis = ORDERS[p][2 - stage]
        for step in (1, 2, 3):
            begin, count = reach(p, stage, (at[axis] + step) % 4)
            start(
                cs[p].at[pl.ds(begin, count)],
                rstage[stage][p].at[pl.ds((step - 1) * count, count)],
                RS + p * 10 + 1 + stage * 3 + step - 1,
                peer(axis, step),
            )

    def swap_finish(p):
        arrived(rcs[p], RS + p * 10)

        def step(b, carry):
            _, block = add_blocks(p, [cs[p][core * 64 + b], rcs[p][b]])
            cs[p][core * 64 + b] = block
            return carry

        lax.fori_loop(0, 64, step, 0)

    def scatter_wait(p, stage):
        count = (16, 4, 1)[stage]
        for step in (1, 2, 3):
            arrived(
                rstage[stage][p].at[pl.ds((step - 1) * count, count)],
                RS + p * 10 + 1 + stage * 3 + step - 1,
            )

    def scatter_add(p, stage):
        axis = ORDERS[p][2 - stage]
        begin, count = reach(p, stage, at[axis])
        scatter_wait(p, stage)

        def step(b, carry):
            parts = [rstage[stage][p][n * count + b] for n in range(3)]
            _, block = add_blocks(p, [cs[p][begin + b]] + parts)
            cs[p][begin + b] = block
            return carry

        lax.fori_loop(0, count, step, 0)

    context_of(0, 3)
    swap_start(0)
    context_of(1, 3)
    swap_start(1)
    swap_finish(0)
    scatter_start(0, 0)
    context_of(2, 2)
    swap_start(2)
    swap_finish(1)
    scatter_start(1, 0)
    swap_finish(2)
    scatter_start(2, 0)

    coefficient = (LOSS_WEIGHT * E ** (-0.5)) * (jnp.exp(log_prob) - target)
    grads = jnp.where(valid, coefficient * emb, 0.0).astype(BF16)
    hot_row_t = jnp.where(iota((64, 64), 0) == lane_ref[5:6, 0:64], 1.0, 0.0).astype(BF16)
    grad_ref[...] = nn(hot_row_t, grads)

    for p in range(3):
        scatter_add(p, 0)
        scatter_start(p, 1)
    for p in range(3):
        scatter_add(p, 1)
        scatter_start(p, 2)
    for p in range(3):
        begin, _ = reach(p, 2, at[ORDERS[p][0]])
        scatter_wait(p, 2)
        total, _ = add_blocks(p, [cs[p][begin]] + [rstage[2][p][n] for n in range(3)])
        for cc in range(2 if p == 2 else 3):
            c = 3 * p + cc
            cols = total[:, cc * 128 : cc * 128 + 128].astype(BF16)
            ctx_ref[0, :, c * 128 : c * 128 + 128] = total[0:8, cc * 128 : cc * 128 + 128].astype(BF16)
            ctx_ref[0, :, 1024 + c * 128 : 1152 + c * 128] = total[
                8:16, cc * 128 : cc * 128 + 128
            ].astype(BF16)
        if p == 2:
            loss_ref[...] = total[0:8, 256:384] + total[8:16, 256:384]

    for copy in started:
        copy.wait_send()


def body(
    store_states,
    store_keys,
    passage_ids,
    store_slot,
    row_question,
    queries,
    question_emb,
    enc_gain,
    key_weight,
    value_weight,
):
    me = lax.axis_index("group") * lax.axis_size("dev") + lax.axis_index("dev")
    rows = store_slot[passage_ids].reshape(GROUPS, 1024)
    mine = rows // STORE == me
    earlier = iota((1024, 1024), 0) <= iota((1024, 1024), 1)
    rank = jnp.dot(mine.astype(BF16), earlier.astype(BF16), preferred_element_type=F32)
    rank = rank.astype(jnp.int32) - 1
    hit = mine[:, None, :] & (rank[:, None, :] == jnp.arange(SLOTS)[None, :, None])
    code = iota((GROUPS, 1024), 1) * STORE + rows % STORE + 1
    code = jnp.sum(jnp.where(hit, code[:, None, :], 0), axis=2).reshape(64) - 1
    valid = code >= 0
    u = jnp.where(valid, code // (32 * STORE), -1)
    k = jnp.where(valid, (code // STORE) % 32, 0)
    row = jnp.where(valid, code % STORE, -1)
    rows_of = jnp.maximum(row, 0)
    u_lanes = jnp.repeat(u.reshape(4, 16), 8, axis=1)
    pad = jnp.zeros((64,), jnp.int32)
    lane_tab = jnp.concatenate(
        [
            u_lanes,
            jnp.concatenate([k, pad])[None],
            jnp.concatenate([row, pad])[None],
            jnp.zeros((2, 128), jnp.int32),
        ]
    )
    col_tab = jnp.pad(jnp.stack([u, k, row], axis=1), ((0, 0), (0, 125)))
    rq = row_question[0]
    rq_tab = jnp.concatenate(
        [
            jnp.broadcast_to(rq[:, None], (32, 128)),
            jnp.broadcast_to(jnp.tile(rq, 4)[None, :], (8, 128)),
        ]
    )
    vmem = pl.BlockSpec(memory_space=pltpu.VMEM)
    anywhere = pl.BlockSpec(memory_space=pl.ANY)
    scratch = [
        pltpu.VMEM((64, 8, D), BF16),
        pltpu.VMEM((D, 2 * D), BF16),
        pltpu.VMEM((512, D), BF16),
        pltpu.VMEM((512, 2 * D), BF16),
    ]
    scratch += [pltpu.VMEM((128, 16, 384), BF16)] * 6
    scratch += [pltpu.VMEM((64, 16, 384), BF16)] * 3
    scratch += [pltpu.VMEM((48, 16, 384), BF16)] * 3
    scratch += [pltpu.VMEM((12, 16, 384), BF16)] * 3
    scratch += [pltpu.VMEM((3, 16, 384), BF16)] * 3
    scratch += [pltpu.VMEM((4, 256, 128), F32), pltpu.VMEM((4, 256, 128), BF16)]
    sizes = (64, 64, 16)
    scratch += [pltpu.VMEM((2 * n, 128), F32) for n in sizes]
    scratch += [pltpu.VMEM((n, 128), F32) for n in sizes]
    scratch += [pltpu.VMEM((9, n, 128), F32) for n in sizes]
    scratch += [pltpu.VMEM((3, n, 128), F32) for n in sizes]
    scratch += [pltpu.VMEM((2 * n, 128), F32) for n in sizes]
    scratch += [
        pltpu.VMEM((4, 40, 128), jnp.int32),
        pltpu.VMEM((8, 128), jnp.int32),
        pltpu.VMEM((128, 128), F32),
        pltpu.SemaphoreType.DMA((SEMS,)),
        pltpu.SemaphoreType.DMA((SEMS,)),
        pltpu.SemaphoreType.DMA((9,)),
    ]
    context, loss, grad = pl.pallas_call(
        kernel,
        out_shape=(
            jax.ShapeDtypeStruct((1, 8, D), BF16),
            jax.ShapeDtypeStruct((8, 128), F32),
            jax.ShapeDtypeStruct((STORE, E), F32),
        ),
        in_specs=[
            pl.BlockSpec(memory_space=pltpu.SMEM),
            vmem,
            vmem,
            vmem,
            anywhere,
            vmem,
            vmem,
            vmem,
            vmem,
            anywhere,
            anywhere,
        ],
        out_specs=(vmem, vmem, vmem),
        scratch_shapes=scratch,
        compiler_params=pltpu.CompilerParams(
            collective_id=0, has_side_effects=True, vmem_limit_bytes=60 * 1024 * 1024
        ),
        cost_estimate=pl.CostEstimate(
            flops=12 * 10**9, bytes_accessed=20 * 10**6, transcendentals=10**6
        ),
    )(
        rows_of,
        lane_tab,
        col_tab,
        rq_tab,
        store_states,
        store_keys,
        queries,
        question_emb,
        enc_gain.reshape(1, D),
        key_weight,
        value_weight,
    )
    return context, loss[0, 0:1], grad


def solution(mesh):
    in_specs = (
        P(("group", "dev"), None, None),
        P(("group", "dev"), None),
        P(),
        P(),
        P("group", None),
        P(("group", "dev"), None, None),
        P(("group", "dev"), None),
        P(),
        P(),
        P(),
    )
    out_specs = (P(("group", "dev"), None, None), P(("group", "dev")), P(("group", "dev"), None))
    return jax.shard_map(body, mesh=mesh, in_specs=in_specs, out_specs=out_specs, check_vma=False)
```

```python
import functools

import jax
import jax.numpy as jnp
from jax import lax
from jax.experimental import pallas as pl
from jax.experimental.pallas import tpu as pltpu
from jax.sharding import PartitionSpec as P

MESH = pl.DeviceIdType.MESH
F32 = jnp.float32
BF16 = jnp.bfloat16
HIGHEST = lax.Precision.HIGHEST

D = 2048
E = 768
GROUPS = 4
PER_GROUP = 32
SLOTS = 16
LANES = 128
STORE = 64
EPS = 1e-06
LOSS_WEIGHT = 256.0
ABSENT = -1e30

ORDERS = (("x", "y", "z"), ("y", "z", "x"), ("z", "x", "y"))
AG, AG_SIB, RQ, AR, RS = 0, 27, 39, 42, 75
SEMS = 105


def nt(a, b, precision=None):
    return lax.dot_general(
        a, b, (((1,), (1,)), ((), ())), preferred_element_type=F32, precision=precision
    )


def nn(a, b, precision=None):
    return jnp.dot(a, b, preferred_element_type=F32, precision=precision)


def iota(shape, dim):
    return lax.broadcasted_iota(jnp.int32, shape, dim)


def block_of(part, g, j):
    y, x, core = j // 8, (j // 2) % 4, j % 2
    at = {"x": x, "y": y, "z": g}
    first, second, third = ORDERS[part]
    return core * 64 + at[third] * 16 + at[second] * 4 + at[first]


def add_blocks(part, blocks):
    total = blocks[0].astype(F32)
    for block in blocks[1:]:
        total = total + block.astype(F32)
    if part < 2:
        return total, total.astype(BF16)
    loss = total[0:8, 256:384] + total[8:16, 256:384]
    high = loss.astype(BF16).astype(F32)
    tile = jnp.concatenate([high, loss - high], axis=0)
    return total, jnp.concatenate([total[:, 0:256], tile], axis=1).astype(BF16)


def kernel(
    ids_ref,
    slot_ref,
    rq_ref,
    states_ref,
    keys_ref,
    queries_ref,
    emb_ref,
    gain_ref,
    kw_ref,
    vw_ref,
    ctx_ref,
    loss_ref,
    grad_ref,
    st,
    w,
    stored,
    pick,
    nrm,
    kv,
    q0,
    q1,
    q2,
    c0,
    c1,
    c2,
    rc0,
    rc1,
    rc2,
    ra0,
    ra1,
    ra2,
    rb0,
    rb1,
    rb2,
    rd0,
    rd1,
    rd2,
    s_buf,
    p_buf,
    t0,
    t1,
    t2,
    ac0,
    ac1,
    ac2,
    ar0,
    ar1,
    ar2,
    acc0,
    acc1,
    acc2,
    l0,
    l1,
    l2,
    rqt,
    lane_ref,
    ir_ref,
    loss_t,
    send_sem,
    recv_sem,
    local_sem,
):
    qs, cs, rcs = (q0, q1, q2), (c0, c1, c2), (rc0, rc1, rc2)
    rstage = ((ra0, ra1, ra2), (rb0, rb1, rb2), (rd0, rd1, rd2))
    ts, acs, ars, accs, ls = (
        (t0, t1, t2),
        (ac0, ac1, ac2),
        (ar0, ar1, ar2),
        (acc0, acc1, acc2),
        (l0, l1, l2),
    )
    my_group = lax.axis_index("group")
    my_dev = lax.axis_index("dev")
    core = my_dev % 2
    at = {"x": (my_dev // 2) % 4, "y": my_dev // 8, "z": my_group}
    sibling = (my_group, my_dev + 1 - 2 * core)

    def peer(axis, step):
        to = (at[axis] + step) % 4
        if axis == "z":
            return (to, my_dev)
        if axis == "y":
            return (my_group, to * 8 + at["x"] * 2 + core)
        return (my_group, at["y"] * 8 + to * 2 + core)

    started = []

    def remote(src, dst, number, device):
        copy = pltpu.make_async_remote_copy(
            src_ref=src,
            dst_ref=dst,
            send_sem=send_sem.at[number],
            recv_sem=recv_sem.at[number],
            device_id=device,
            device_id_type=MESH,
        )
        return copy

    def start(src, dst, number, device):
        copy = remote(src, dst, number, device)
        copy.start()
        started.append(copy)

    def arrived(dst, number):
        remote(dst, dst, number, sibling).wait_recv()

    states_copy = pltpu.make_async_copy(states_ref, st, local_sem.at[8])
    states_copy.start()
    w_copies = []
    for n in range(8):
        src = kw_ref if n < 4 else vw_ref
        copy = pltpu.make_async_copy(
            src.at[:, pl.ds((n % 4) * 512, 512)],
            w.at[:, pl.ds(n * 512, 512)],
            local_sem.at[n],
        )
        copy.start()
        w_copies.append(copy)

    mine = [
        core * 64 + at[ORDERS[p][2]] * 16 + at[ORDERS[p][1]] * 4 + at[ORDERS[p][0]]
        for p in range(3)
    ]
    for c in range(8):
        tile = jnp.concatenate(
            [
                queries_ref[0, :, c * 128 : c * 128 + 128].astype(F32),
                queries_ref[0, :, 1024 + c * 128 : 1152 + c * 128].astype(F32),
            ],
            axis=0,
        )
        qs[c // 3][mine[c // 3], :, (c % 3) * 128 : (c % 3) * 128 + 128] = tile.astype(BF16)
    emb_rows = [emb_ref[:, c * 128 : c * 128 + 128].astype(F32) for c in range(6)]
    emb_tile = jnp.concatenate(emb_rows + [jnp.zeros((10, 128), F32)], axis=0)
    q2[mine[2], :, 256:384] = emb_tile.astype(BF16)
    diagonal = iota((32, 32), 0) == iota((32, 32), 1)
    rq_col = jnp.sum(jnp.where(diagonal, rq_ref[...], 0), axis=1, keepdims=True)
    rqt[my_group] = jnp.broadcast_to(rq_col, (32, 128))

    barrier = pltpu.get_barrier_semaphore()
    pl.semaphore_signal(barrier, inc=1, device_id=sibling, device_id_type=MESH)
    for axis in ("x", "y", "z"):
        for step in (1, 2, 3):
            pl.semaphore_signal(barrier, inc=1, device_id=peer(axis, step), device_id_type=MESH)
    pl.semaphore_wait(barrier, 10)

    def span(p, stage, back):
        first, second, third = ORDERS[p]
        digit = (at[ORDERS[p][stage]] + 4 - back) % 4
        if stage == 0:
            return core * 64 + at[third] * 16 + at[second] * 4 + digit, 1
        if stage == 1:
            return core * 64 + at[third] * 16 + digit * 4, 4
        return core * 64 + digit * 16, 16

    def gather_start(stage):
        for p in range(3):
            begin, size = span(p, stage, 0)
            for step in (1, 2, 3):
                ref = qs[p].at[pl.ds(begin, size)]
                start(ref, ref, AG + (p * 3 + stage) * 3 + step - 1, peer(ORDERS[p][stage], step))

    def gather_wait(p, stage, step):
        begin, size = span(p, stage, step)
        arrived(qs[p].at[pl.ds(begin, size)], AG + (p * 3 + stage) * 3 + step - 1)

    def forward(p, back):
        begin, size = span(p, 2, back)
        ref = qs[p].at[pl.ds(begin, size)]
        start(ref, ref, AG_SIB + p * 4 + back, sibling)

    gather_start(0)
    for step in (1, 2, 3):
        start(rqt.at[my_group], rqt.at[my_group], RQ + step - 1, peer("z", step))

    lane = iota((1, 128), 1)
    sub = iota((128, 128), 0)
    lanes = iota((128, 128), 1)
    first_row = (my_group * PER_GROUP + my_dev) * STORE
    local = slot_ref[...] - first_row
    local = jnp.where((local >= 0) & (local < STORE), local + 1, 0).astype(F32)
    local_t = jnp.transpose(local).astype(BF16)
    ids_high = ids_ref[...] // 128
    ids_low = ids_ref[...] % 128
    high_sub = iota((64, 128), 0)
    lane32 = iota((128, 32), 1)
    held_rows = []
    for k in range(32):
        hot = jnp.where(high_sub == ids_high[k : k + 1, :], 1.0, 0.0).astype(BF16)
        found = jnp.where(sub == ids_low[k : k + 1, :], nn(local_t, hot), 0.0)
        held_rows.append(jnp.sum(found, axis=0, keepdims=True))
    held = jnp.transpose(jnp.concatenate(held_rows, axis=0))
    held_int = held.astype(jnp.int32)
    mine_f = jnp.where(held_int > 0, 1.0, 0.0)
    mine_b = mine_f.astype(BF16)
    in_row = nn(mine_b, jnp.ones((32, 32), BF16))
    above = jnp.where((sub // 32 == lanes // 32) & (lanes < sub), 1.0, 0.0).astype(BF16)
    upto = jnp.where(iota((32, 32), 0) <= iota((32, 32), 1), 1.0, 0.0).astype(BF16)
    rank = nn(above, in_row.astype(BF16)) + nn(mine_b, upto)
    rank = jnp.where(held_int > 0, rank.astype(jnp.int32), 0)
    code = (iota((128, 32), 0) % 32) * 4096 + lane32 * 128 + held_int
    spread = jnp.zeros((128, 128), jnp.int32)
    for n in range(SLOTS):
        here = jnp.sum(jnp.where(rank == n + 1, code, 0), axis=1, keepdims=True)
        spread = jnp.where(lanes // 8 == n, here, spread)
    code_cols = []
    slot16 = iota((16, 128), 1) == iota((16, 128), 0) * 8
    for g in range(4):
        code_row = jnp.sum(spread[g * 32 : g * 32 + 32], axis=0, keepdims=True)
        lane_ref[g : g + 1, :] = jnp.where(code_row > 0, code_row // 4096, -1)
        code_cols.append(jnp.sum(jnp.where(slot16, code_row, 0), axis=1, keepdims=True))
        long_col = jnp.sum(jnp.where(sub == lanes, code_row, 0), axis=1, keepdims=True)
        token = jnp.where(
            long_col > 0, (long_col % 128 - 1) * 8 + iota((128, 1), 0) % 8, 512
        )
        pick[g * 128 : g * 128 + 128, :] = jnp.where(
            iota((128, 512), 1) == token, 1.0, 0.0
        ).astype(BF16)
    code_col = jnp.concatenate(code_cols, axis=0)
    valid = code_col > 0
    k_col = (code_col // 128) % 32
    row_col = code_col % 128 - 1
    square = iota((64, 64), 0) == iota((64, 64), 1)
    code_row64 = jnp.sum(jnp.where(square, code_col, 0), axis=0, keepdims=True)
    k_row = (code_row64 // 128) % 32
    row_row = code_row64 % 128 - 1

    states_copy.wait()

    def norm_pair(pair, carry):
        both = []
        for half in range(2):
            values = st[pair * 2 + half].astype(F32)
            mean_square = jnp.mean(values * values, axis=-1, keepdims=True)
            both.append(values * lax.rsqrt(mean_square + EPS) * gain_ref[...])
        rows = pl.ds(pl.multiple_of(pair * 16, 16), 16)
        stored[rows, :] = jnp.concatenate(both, axis=0).astype(BF16)
        return carry

    lax.fori_loop(0, 32, norm_pair, 0)

    def pick_step(n, carry):
        cols = pl.ds(pl.multiple_of(n * 256, 256), 256)
        nrm[:, cols] = nn(pick[...], stored[:, cols]).astype(BF16)
        return carry

    lax.fori_loop(0, 8, pick_step, 0)

    def project(begin, end):
        def step(n, carry):
            offset = pl.multiple_of(n * 256, 256)
            kv[:, pl.ds(offset, 256)] = nn(nrm[...], w[:, pl.ds(offset, 256)]).astype(BF16)
            return carry

        for n in range(begin, end):
            w_copies[n].wait()
        lax.fori_loop(begin * 2, end * 2, step, 0)

    for p in range(3):
        for step in (1, 2, 3):
            gather_wait(p, 0, step)
    gather_start(1)
    project(0, 2)
    for p in range(3):
        for step in (1, 2, 3):
            gather_wait(p, 1, step)
    gather_start(2)
    for p in range(3):
        forward(p, 0)
    project(2, 6)
    for step in (1, 3, 2):
        for p in range(3):
            gather_wait(p, 2, step)
            forward(p, step)
    project(6, 8)

    for step in (1, 2, 3):
        arrived(rqt.at[(my_group + 4 - step) % 4], RQ + step - 1)
    for g in range(4):
        match = rqt[g] == lane_ref[g : g + 1, :]
        row = jnp.sum(jnp.where(match, iota((32, 128), 0) + (g * 32 + 1), 0), axis=0, keepdims=True)
        ir_ref[g : g + 1, :] = row - 1

    for p in range(3):
        for back in range(4):
            first, second, third = ORDERS[p]
            begin = (1 - core) * 64 + ((at[third] + 4 - back) % 4) * 16
            arrived(qs[p].at[pl.ds(begin, 16)], AG_SIB + p * 4 + back)

    low = (lane < 64).astype(F32).astype(BF16)
    high = (lane >= 64).astype(F32).astype(BF16)

    def scores_of(p, tiles):
        def step(n, carry):
            g, cc = n // tiles, n % tiles
            inner = pl.multiple_of(cc * 128, 128)
            outer = pl.multiple_of((3 * p + cc) * 128, 128)
            slots = pl.ds(pl.multiple_of(g * 128, 128), 128)
            right = jnp.concatenate(
                [kv[slots, pl.ds(outer, 128)], kv[slots, pl.ds(outer + 1024, 128)]], axis=0
            )
            row = ir_ref[pl.ds(g, 1), :] - g * 32
            total = [jnp.zeros((8, 128), F32) for _ in range(4)]
            for jb in range(2):
                left = []
                for jj in range(16):
                    block = qs[p][block_of(p, g, jb * 16 + jj), :, pl.ds(inner, 128)]
                    left += [block * low, block * high]
                out = nt(jnp.concatenate(left, axis=0), right)
                for jj in range(16):
                    keep = jnp.broadcast_to(row == jb * 16 + jj, (8, 128))
                    for tile in range(4):
                        half = tile % 2
                        begin = jj * 32 + tile * 8
                        piece = out[begin : begin + 8, half * 128 : half * 128 + 128]
                        total[tile] = jnp.where(keep, piece, total[tile])
            rows = pl.ds(pl.multiple_of((3 * p + cc) * 32, 32), 32)
            s_buf[g, rows, :] = jnp.concatenate(total, axis=0) * (64 ** (-0.5))
            return carry

        lax.fori_loop(0, 4 * tiles, step, 0)

    scores_of(0, 3)
    scores_of(1, 3)
    scores_of(2, 2)

    peak_i = jnp.zeros((256, 128), F32)
    total_i = jnp.zeros((256, 128), F32)
    present = jnp.zeros((8, 128), F32)
    for g in range(4):
        scores = s_buf[g]
        u_row = lane_ref[g : g + 1, :]
        peak = scores
        for s in (1, 2, 4):
            bit = jnp.broadcast_to((lane // s) % 2 == 1, (256, 128))
            other = jnp.where(bit, pltpu.roll(peak, s, 1), pltpu.roll(peak, 128 - s, 1))
            peak = jnp.maximum(peak, other)
        u_rows = jnp.broadcast_to(u_row, (8, 128))
        before = pltpu.roll(u_rows, 8, 1)[0:1, :]
        for s in (8, 16, 32, 64):
            same = (pltpu.roll(u_rows, s, 1)[0:1, :] == u_row) & (lane >= s)
            other = jnp.where(jnp.broadcast_to(same, (256, 128)), pltpu.roll(peak, s, 1), ABSENT)
            peak = jnp.maximum(peak, other)
        for s in (8, 16, 32, 64):
            same = (pltpu.roll(u_rows, 128 - s, 1)[0:1, :] == u_row) & (lane < 128 - s)
            other = jnp.where(
                jnp.broadcast_to(same, (256, 128)), pltpu.roll(peak, 128 - s, 1), ABSENT
            )
            peak = jnp.maximum(peak, other)
        chosen = sub == ir_ref[g : g + 1, :]
        first = ((before != u_row) | (lane < 8)) & (lane % 8 == 0)
        lead = jnp.where(chosen & jnp.broadcast_to(first, (128, 128)), 1.0, 0.0)
        peak_i = peak_i + nt(peak, lead, HIGHEST)
        total_i = total_i + nt(jnp.exp(scores - peak), jnp.where(chosen, 1.0, 0.0), HIGHEST)
        present = present + nt(jnp.ones((8, 128), F32), lead)
    table = jnp.where(
        jnp.broadcast_to(present[0:1, :] > 0.5, (256, 128)),
        peak_i + jnp.log(jnp.maximum(total_i, 1e-30)),
        ABSENT,
    )
    t0[...] = table[0:128, :]
    t1[...] = table[128:256, :]

    lane64 = iota((64, 128), 1)
    i_cols = []
    for g in range(4):
        picked = jnp.where(slot16, ir_ref[g : g + 1, :] + 1, 0)
        i_cols.append(jnp.sum(picked, axis=1, keepdims=True))
    i_col = jnp.concatenate(i_cols, axis=0) - 1
    one_hot_i = lane64 == i_col
    hot_i = jnp.where(one_hot_i, 1.0, 0.0)
    decoder = jnp.maximum(i_col, 0)
    place = block_of(2, decoder // 32, decoder % 32) * 16
    flat = q2[:, :, 256:384].reshape(2048, 128)
    wide = iota((64, 2048), 1)
    emb = jnp.concatenate(
        [nn(jnp.where(wide == place + c, 1.0, 0.0).astype(BF16), flat) for c in range(6)], axis=1
    )
    hot_row = jnp.where(iota((64, 64), 1) == row_col, 1.0, 0.0).astype(BF16)
    keys = nn(hot_row, keys_ref[...])
    retrieval = jnp.sum(emb * keys, axis=1, keepdims=True) * (E ** (-0.5))
    retrieval_row = jnp.sum(jnp.where(square, retrieval, 0.0), axis=0, keepdims=True)
    by_k = jnp.where(iota((32, 64), 0) == k_row, retrieval_row, 0.0)
    t2[...] = nn(by_k, hot_i, HIGHEST)

    size = (64, 64, 16)

    def combine(p, values):
        if p == 2:
            total = values[0]
            for value in values[1:]:
                total = total + value
            return total
        top = values[0]
        for value in values[1:]:
            top = jnp.maximum(top, value)
        total = jnp.exp(values[0] - top)
        for value in values[1:]:
            total = total + jnp.exp(value - top)
        return top + jnp.log(total)

    for p in range(3):
        other = pl.ds(pl.multiple_of((1 - core) * size[p], size[p]), size[p])
        start(ts[p].at[other], acs[p], AR + p * 11, sibling)
    for p in range(3):
        own = pl.ds(pl.multiple_of(core * size[p], size[p]), size[p])
        arrived(acs[p], AR + p * 11)
        accs[p][0] = combine(p, [ts[p][own, :], acs[p][...]])
        for step in (1, 2, 3):
            start(
                accs[p].at[0],
                ars[p].at[step - 1],
                AR + p * 11 + step,
                peer(ORDERS[p][0], step),
            )
    for stage in range(3):
        for p in range(3):
            values = [accs[p][stage]]
            for step in (1, 2, 3):
                arrived(ars[p].at[stage * 3 + step - 1], AR + p * 11 + stage * 3 + step)
                values.append(ars[p][stage * 3 + step - 1])
            total = combine(p, values)
            own = pl.ds(pl.multiple_of(core * size[p], size[p]), size[p])
            if stage == 2:
                ls[p][own, :] = total
                ref = ls[p].at[own]
                start(ref, ref, AR + p * 11 + 10, sibling)
            else:
                accs[p][stage + 1] = total
                for step in (1, 2, 3):
                    start(
                        accs[p].at[stage + 1],
                        ars[p].at[(stage + 1) * 3 + step - 1],
                        AR + p * 11 + (stage + 1) * 3 + step,
                        peer(ORDERS[p][stage + 1], step),
                    )
    for p in range(3):
        other = pl.ds(pl.multiple_of((1 - core) * size[p], size[p]), size[p])
        arrived(ls[p].at[other], AR + p * 11 + 10)

    log_sum = jnp.concatenate([l0[...], l1[...]], axis=0)
    targets = []
    for g in range(4):
        chosen = jnp.where(sub == ir_ref[g : g + 1, :], 1.0, 0.0)
        weights = jnp.exp(s_buf[g] - nn(log_sum, chosen, HIGHEST))
        p_buf[g] = weights.astype(BF16)
        mass = jnp.sum(weights, axis=0, keepdims=True)
        own = iota((16, 128), 1) // 8 == iota((16, 128), 0)
        targets.append(jnp.sum(jnp.where(own, mass, 0.0), axis=1, keepdims=True))
    target = jnp.concatenate(targets, axis=0) * (1.0 / 256.0)
    raw = l2[...]
    top = jnp.max(raw, axis=0, keepdims=True)
    log_prob_all = raw - top - jnp.log(jnp.sum(jnp.exp(raw - top), axis=0, keepdims=True))
    hot_k = jnp.where(iota((64, 32), 1) == k_col, 1.0, 0.0)
    log_prob = jnp.sum(
        jnp.where(one_hot_i, nn(hot_k, log_prob_all, HIGHEST), 0.0), axis=1, keepdims=True
    )
    term = jnp.where(valid, target * (jnp.log(target) - log_prob), 0.0)
    loss_row = jnp.sum(jnp.where(one_hot_i, term, 0.0), axis=0, keepdims=True)
    loss_col = jnp.sum(jnp.where(sub == lanes, loss_row, 0.0), axis=1, keepdims=True)
    loss_t[...] = jnp.broadcast_to(loss_col, (128, 128))

    def loss_block(j, carry):
        for g in range(4):
            value = jnp.broadcast_to(loss_t[pl.ds(g * 32 + j, 1), :], (8, 128))
            top_half = value.astype(BF16).astype(F32)
            tile = jnp.concatenate([top_half, value - top_half], axis=0)
            c2[block_of(2, g, j), :, 256:384] = tile.astype(BF16)
        return carry

    lax.fori_loop(0, 32, loss_block, 0)

    keep_low = jnp.broadcast_to(lane < 64, (8, 128))

    def context_of(p, tiles):
        def step(n, carry):
            g, cc = n // tiles, n % tiles
            inner = pl.multiple_of(cc * 128, 128)
            outer = pl.multiple_of(D + (3 * p + cc) * 128, 128)
            slots = pl.ds(pl.multiple_of(g * 128, 128), 128)
            right = jnp.concatenate(
                [kv[slots, pl.ds(outer, 128)], kv[slots, pl.ds(outer + 1024, 128)]], axis=1
            )
            row = ir_ref[pl.ds(g, 1), :] - g * 32
            rows = pl.ds(pl.multiple_of((3 * p + cc) * 32, 32), 32)
            weights = p_buf[g, rows, :]
            for jb in range(2):
                left = []
                for jj in range(16):
                    keep = jnp.where(row == jb * 16 + jj, 1.0, 0.0).astype(BF16)
                    left.append(weights * keep)
                out = nn(jnp.concatenate(left, axis=0), right)
                for jj in range(16):
                    halves = []
                    for half in range(2):
                        cols = slice(half * 128, half * 128 + 128)
                        begin = jj * 32 + half * 8
                        halves.append(
                            jnp.where(
                                keep_low,
                                out[begin : begin + 8, cols],
                                out[begin + 16 : begin + 24, cols],
                            )
                        )
                    tile = jnp.concatenate(halves, axis=0).astype(BF16)
                    cs[p][block_of(p, g, jb * 16 + jj), :, pl.ds(inner, 128)] = tile
            return carry

        lax.fori_loop(0, 4 * tiles, step, 0)

    def swap_start(p):
        start(cs[p].at[pl.ds((1 - core) * 64, 64)], rcs[p], RS + p * 10, sibling)

    def reach(p, stage, to):
        first, second, third = ORDERS[p]
        if stage == 0:
            return core * 64 + to * 16, 16
        if stage == 1:
            return core * 64 + at[third] * 16 + to * 4, 4
        return core * 64 + at[third] * 16 + at[second] * 4 + to, 1

    def scatter_start(p, stage):
        axis = ORDERS[p][2 - stage]
        for step in (1, 2, 3):
            begin, count = reach(p, stage, (at[axis] + step) % 4)
            start(
                cs[p].at[pl.ds(begin, count)],
                rstage[stage][p].at[pl.ds((step - 1) * count, count)],
                RS + p * 10 + 1 + stage * 3 + step - 1,
                peer(axis, step),
            )

    def swap_finish(p):
        arrived(rcs[p], RS + p * 10)

        def step(b, carry):
            _, block = add_blocks(p, [cs[p][core * 64 + b], rcs[p][b]])
            cs[p][core * 64 + b] = block
            return carry

        lax.fori_loop(0, 64, step, 0)

    def scatter_wait(p, stage):
        count = (16, 4, 1)[stage]
        for step in (1, 2, 3):
            arrived(
                rstage[stage][p].at[pl.ds((step - 1) * count, count)],
                RS + p * 10 + 1 + stage * 3 + step - 1,
            )

    def scatter_add(p, stage):
        axis = ORDERS[p][2 - stage]
        begin, count = reach(p, stage, at[axis])
        scatter_wait(p, stage)

        def step(b, carry):
            parts = [rstage[stage][p][n * count + b] for n in range(3)]
            _, block = add_blocks(p, [cs[p][begin + b]] + parts)
            cs[p][begin + b] = block
            return carry

        lax.fori_loop(0, count, step, 0)

    context_of(0, 3)
    swap_start(0)
    context_of(1, 3)
    swap_start(1)
    swap_finish(0)
    scatter_start(0, 0)
    context_of(2, 2)
    swap_start(2)
    swap_finish(1)
    scatter_start(1, 0)
    swap_finish(2)
    scatter_start(2, 0)

    coefficient = (LOSS_WEIGHT * E ** (-0.5)) * (jnp.exp(log_prob) - target)
    grads = jnp.where(valid, coefficient * emb, 0.0).astype(BF16)
    hot_row_t = jnp.where(iota((64, 64), 0) == row_row, 1.0, 0.0).astype(BF16)
    grad_ref[...] = nn(hot_row_t, grads)

    for p in range(3):
        scatter_add(p, 0)
        scatter_start(p, 1)
    for p in range(3):
        scatter_add(p, 1)
        scatter_start(p, 2)
    for p in range(3):
        begin, _ = reach(p, 2, at[ORDERS[p][0]])
        scatter_wait(p, 2)
        total, _ = add_blocks(p, [cs[p][begin]] + [rstage[2][p][n] for n in range(3)])
        for cc in range(2 if p == 2 else 3):
            c = 3 * p + cc
            cols = total[:, cc * 128 : cc * 128 + 128].astype(BF16)
            ctx_ref[0, :, c * 128 : c * 128 + 128] = total[0:8, cc * 128 : cc * 128 + 128].astype(BF16)
            ctx_ref[0, :, 1024 + c * 128 : 1152 + c * 128] = total[
                8:16, cc * 128 : cc * 128 + 128
            ].astype(BF16)
        if p == 2:
            loss_ref[...] = total[0:8, 256:384] + total[8:16, 256:384]

    for copy in started:
        copy.wait_send()


def hand_over(ctx_ref, loss_ref, grad_ref, ctx_out, loss_out, grad_out):
    ctx_out[...] = ctx_ref[...]
    loss_out[0] = loss_ref[0, 0]
    grad_out[...] = grad_ref[...]


def body(
    store_states,
    store_keys,
    passage_ids,
    store_slot,
    row_question,
    queries,
    question_emb,
    enc_gain,
    key_weight,
    value_weight,
):
    vmem = pl.BlockSpec(memory_space=pltpu.VMEM)
    anywhere = pl.BlockSpec(memory_space=pl.ANY)
    scratch = [
        pltpu.VMEM((64, 8, D), BF16),
        pltpu.VMEM((D, 2 * D), BF16),
        pltpu.VMEM((512, D), BF16),
        pltpu.VMEM((512, 512), BF16),
        pltpu.VMEM((512, D), BF16),
        pltpu.VMEM((512, 2 * D), BF16),
    ]
    scratch += [pltpu.VMEM((128, 16, 384), BF16)] * 6
    scratch += [pltpu.VMEM((64, 16, 384), BF16)] * 3
    scratch += [pltpu.VMEM((48, 16, 384), BF16)] * 3
    scratch += [pltpu.VMEM((12, 16, 384), BF16)] * 3
    scratch += [pltpu.VMEM((3, 16, 384), BF16)] * 3
    scratch += [pltpu.VMEM((4, 256, 128), F32), pltpu.VMEM((4, 256, 128), BF16)]
    sizes = (64, 64, 16)
    scratch += [pltpu.VMEM((2 * n, 128), F32) for n in sizes]
    scratch += [pltpu.VMEM((n, 128), F32) for n in sizes]
    scratch += [pltpu.VMEM((9, n, 128), F32) for n in sizes]
    scratch += [pltpu.VMEM((3, n, 128), F32) for n in sizes]
    scratch += [pltpu.VMEM((2 * n, 128), F32) for n in sizes]
    scratch += [
        pltpu.VMEM((4, 32, 128), jnp.int32),
        pltpu.VMEM((8, 128), jnp.int32),
        pltpu.VMEM((8, 128), jnp.int32),
        pltpu.VMEM((128, 128), F32),
        pltpu.SemaphoreType.DMA((SEMS,)),
        pltpu.SemaphoreType.DMA((SEMS,)),
        pltpu.SemaphoreType.DMA((9,)),
    ]
    context, loss, grad = pl.pallas_call(
        kernel,
        out_shape=(
            jax.ShapeDtypeStruct((1, 8, D), BF16),
            jax.ShapeDtypeStruct((8, 128), F32),
            jax.ShapeDtypeStruct((STORE, E), F32),
        ),
        in_specs=[
            vmem,
            vmem,
            vmem,
            anywhere,
            vmem,
            vmem,
            vmem,
            vmem,
            anywhere,
            anywhere,
        ],
        out_specs=(vmem, vmem, vmem),
        scratch_shapes=scratch,
        compiler_params=pltpu.CompilerParams(
            collective_id=0, has_side_effects=True, vmem_limit_bytes=60 * 1024 * 1024
        ),
        cost_estimate=pl.CostEstimate(
            flops=12 * 10**9, bytes_accessed=20 * 10**6, transcendentals=10**6
        ),
    )(
        passage_ids.T,
        store_slot.reshape(64, 128),
        row_question,
        store_states,
        store_keys,
        queries,
        question_emb,
        enc_gain.reshape(1, D),
        key_weight,
        value_weight,
    )
    return pl.pallas_call(
        hand_over,
        out_shape=(
            jax.ShapeDtypeStruct((1, 8, D), BF16),
            jax.ShapeDtypeStruct((1,), F32),
            jax.ShapeDtypeStruct((STORE, E), F32),
        ),
        in_specs=[vmem, vmem, vmem],
        out_specs=(vmem, pl.BlockSpec(memory_space=pltpu.SMEM), vmem),
    )(context, loss, grad)


def solution(mesh):
    in_specs = (
        P(("group", "dev"), None, None),
        P(("group", "dev"), None),
        P(),
        P(),
        P("group", None),
        P(("group", "dev"), None, None),
        P(("group", "dev"), None),
        P(),
        P(),
        P(),
    )
    out_specs = (P(("group", "dev"), None, None), P(("group", "dev")), P(("group", "dev"), None))
    return jax.shard_map(body, mesh=mesh, in_specs=in_specs, out_specs=out_specs, check_vma=False)
```

```python
import functools

import jax
import jax.numpy as jnp
from jax import lax
from jax.experimental import pallas as pl
from jax.experimental.pallas import tpu as pltpu
from jax.sharding import PartitionSpec as P

MESH = pl.DeviceIdType.MESH
F32 = jnp.float32
BF16 = jnp.bfloat16
HIGHEST = lax.Precision.HIGHEST

D = 2048
E = 768
GROUPS = 4
PER_GROUP = 32
SLOTS = 16
LANES = 128
STORE = 64
EPS = 1e-06
LOSS_WEIGHT = 256.0
ABSENT = -1e30

ORDERS = (("x", "y", "z"), ("y", "z", "x"), ("z", "x", "y"))
AG, AG_SIB, RQ, AR, RS = 0, 27, 39, 42, 75
SEMS = 114


def nt(a, b, precision=None):
    return lax.dot_general(
        a, b, (((1,), (1,)), ((), ())), preferred_element_type=F32, precision=precision
    )


def nn(a, b, precision=None):
    return jnp.dot(a, b, preferred_element_type=F32, precision=precision)


def iota(shape, dim):
    return lax.broadcasted_iota(jnp.int32, shape, dim)


def block_of(part, g, j):
    y, x, core = j // 8, (j // 2) % 4, j % 2
    at = {"x": x, "y": y, "z": g}
    first, second, third = ORDERS[part]
    return core * 64 + at[third] * 16 + at[second] * 4 + at[first]


def add_blocks(part, blocks):
    total = blocks[0].astype(F32)
    for block in blocks[1:]:
        total = total + block.astype(F32)
    if part < 2:
        return total, total.astype(BF16)
    loss = total[0:8, 256:384] + total[8:16, 256:384]
    high = loss.astype(BF16).astype(F32)
    tile = jnp.concatenate([high, loss - high], axis=0)
    return total, jnp.concatenate([total[:, 0:256], tile], axis=1).astype(BF16)


def kernel(
    ids_ref,
    slot_ref,
    rq_ref,
    states_ref,
    keys_ref,
    queries_ref,
    emb_ref,
    gain_ref,
    kw_ref,
    vw_ref,
    ctx_ref,
    loss_ref,
    grad_ref,
    st,
    w,
    stored,
    pick,
    nrm,
    kv,
    q0,
    q1,
    q2,
    c0,
    c1,
    c2,
    rc0,
    rc1,
    rc2,
    ra0,
    ra1,
    ra2,
    rb0,
    rb1,
    rb2,
    rd0,
    rd1,
    rd2,
    s_buf,
    p_buf,
    t0,
    t1,
    t2,
    ac0,
    ac1,
    ac2,
    ar0,
    ar1,
    ar2,
    acc0,
    acc1,
    acc2,
    l0,
    l1,
    l2,
    rqt,
    lane_ref,
    ir_ref,
    block_ref,
    block_smem,
    loss_t,
    send_sem,
    recv_sem,
    local_sem,
):
    qs, cs, rcs = (q0, q1, q2), (c0, c1, c2), (rc0, rc1, rc2)
    rstage = ((ra0, ra1, ra2), (rb0, rb1, rb2), (rd0, rd1, rd2))
    ts, acs, ars, accs, ls = (
        (t0, t1, t2),
        (ac0, ac1, ac2),
        (ar0, ar1, ar2),
        (acc0, acc1, acc2),
        (l0, l1, l2),
    )
    my_group = lax.axis_index("group")
    my_dev = lax.axis_index("dev")
    core = my_dev % 2
    at = {"x": (my_dev // 2) % 4, "y": my_dev // 8, "z": my_group}
    sibling = (my_group, my_dev + 1 - 2 * core)

    def peer(axis, step):
        to = (at[axis] + step) % 4
        if axis == "z":
            return (to, my_dev)
        if axis == "y":
            return (my_group, to * 8 + at["x"] * 2 + core)
        return (my_group, at["y"] * 8 + to * 2 + core)

    started = []

    def remote(src, dst, number, device):
        copy = pltpu.make_async_remote_copy(
            src_ref=src,
            dst_ref=dst,
            send_sem=send_sem.at[number],
            recv_sem=recv_sem.at[number],
            device_id=device,
            device_id_type=MESH,
        )
        return copy

    def start(src, dst, number, device):
        copy = remote(src, dst, number, device)
        copy.start()
        started.append(copy)

    def arrived(dst, number):
        remote(dst, dst, number, sibling).wait_recv()

    states_copy = pltpu.make_async_copy(states_ref, st, local_sem.at[8])
    states_copy.start()
    w_copies = []
    for n in range(8):
        src = kw_ref if n < 4 else vw_ref
        copy = pltpu.make_async_copy(
            src.at[:, pl.ds((n % 4) * 512, 512)],
            w.at[:, pl.ds(n * 512, 512)],
            local_sem.at[n],
        )
        copy.start()
        w_copies.append(copy)

    mine = [
        core * 64 + at[ORDERS[p][2]] * 16 + at[ORDERS[p][1]] * 4 + at[ORDERS[p][0]]
        for p in range(3)
    ]
    for c in range(8):
        tile = jnp.concatenate(
            [
                queries_ref[0, :, c * 128 : c * 128 + 128].astype(F32),
                queries_ref[0, :, 1024 + c * 128 : 1152 + c * 128].astype(F32),
            ],
            axis=0,
        )
        qs[c // 3][mine[c // 3], :, (c % 3) * 128 : (c % 3) * 128 + 128] = tile.astype(BF16)
    emb_rows = [emb_ref[:, c * 128 : c * 128 + 128].astype(F32) for c in range(6)]
    emb_tile = jnp.concatenate(emb_rows + [jnp.zeros((10, 128), F32)], axis=0)
    q2[mine[2], :, 256:384] = emb_tile.astype(BF16)
    diagonal = iota((32, 32), 0) == iota((32, 32), 1)
    rq_col = jnp.sum(jnp.where(diagonal, rq_ref[...], 0), axis=1, keepdims=True)
    rqt[my_group] = jnp.broadcast_to(rq_col, (32, 128))

    barrier = pltpu.get_barrier_semaphore()
    pl.semaphore_signal(barrier, inc=1, device_id=sibling, device_id_type=MESH)
    for axis in ("x", "y", "z"):
        for step in (1, 2, 3):
            pl.semaphore_signal(barrier, inc=1, device_id=peer(axis, step), device_id_type=MESH)
    pl.semaphore_wait(barrier, 10)

    def span(p, stage, back):
        first, second, third = ORDERS[p]
        digit = (at[ORDERS[p][stage]] + 4 - back) % 4
        if stage == 0:
            return core * 64 + at[third] * 16 + at[second] * 4 + digit, 1
        if stage == 1:
            return core * 64 + at[third] * 16 + digit * 4, 4
        return core * 64 + digit * 16, 16

    def gather_start(stage):
        for p in range(3):
            begin, size = span(p, stage, 0)
            for step in (1, 2, 3):
                ref = qs[p].at[pl.ds(begin, size)]
                start(ref, ref, AG + (p * 3 + stage) * 3 + step - 1, peer(ORDERS[p][stage], step))

    def gather_wait(p, stage, step):
        begin, size = span(p, stage, step)
        arrived(qs[p].at[pl.ds(begin, size)], AG + (p * 3 + stage) * 3 + step - 1)

    def forward(p, back):
        begin, size = span(p, 2, back)
        ref = qs[p].at[pl.ds(begin, size)]
        start(ref, ref, AG_SIB + p * 4 + back, sibling)

    gather_start(0)
    for step in (1, 2, 3):
        start(rqt.at[my_group], rqt.at[my_group], RQ + step - 1, peer("z", step))

    lane = iota((1, 128), 1)
    sub = iota((128, 128), 0)
    lanes = iota((128, 128), 1)
    first_row = (my_group * PER_GROUP + my_dev) * STORE
    local = slot_ref[...] - first_row
    local = jnp.where((local >= 0) & (local < STORE), local + 1, 0).astype(F32)
    local_t = jnp.transpose(local).astype(BF16)
    ids_high = ids_ref[...] // 128
    ids_low = ids_ref[...] % 128
    high_sub = iota((64, 128), 0)
    lane32 = iota((128, 32), 1)
    held_rows = []
    for k in range(32):
        hot = jnp.where(high_sub == ids_high[k : k + 1, :], 1.0, 0.0).astype(BF16)
        found = jnp.where(sub == ids_low[k : k + 1, :], nn(local_t, hot), 0.0)
        held_rows.append(jnp.sum(found, axis=0, keepdims=True))
    held = jnp.transpose(jnp.concatenate(held_rows, axis=0))
    for p in range(3):
        for step in (1, 2, 3):
            gather_wait(p, 0, step)
    gather_start(1)

    held_int = held.astype(jnp.int32)
    mine_f = jnp.where(held_int > 0, 1.0, 0.0)
    mine_b = mine_f.astype(BF16)
    in_row = nn(mine_b, jnp.ones((32, 32), BF16))
    above = jnp.where((sub // 32 == lanes // 32) & (lanes < sub), 1.0, 0.0).astype(BF16)
    upto = jnp.where(iota((32, 32), 0) <= iota((32, 32), 1), 1.0, 0.0).astype(BF16)
    rank = nn(above, in_row.astype(BF16)) + nn(mine_b, upto)
    rank = jnp.where(held_int > 0, rank.astype(jnp.int32), 0)
    code = (iota((128, 32), 0) % 32) * 4096 + lane32 * 128 + held_int
    spread = jnp.zeros((128, 128), jnp.int32)
    for n in range(SLOTS):
        here = jnp.sum(jnp.where(rank == n + 1, code, 0), axis=1, keepdims=True)
        spread = jnp.where(lanes // 8 == n, here, spread)
    code_cols = []
    slot16 = iota((16, 128), 1) == iota((16, 128), 0) * 8
    for g in range(4):
        code_row = jnp.sum(spread[g * 32 : g * 32 + 32], axis=0, keepdims=True)
        lane_ref[g : g + 1, :] = jnp.where(code_row > 0, code_row // 4096, -1)
        code_cols.append(jnp.sum(jnp.where(slot16, code_row, 0), axis=1, keepdims=True))
        long_col = jnp.sum(jnp.where(sub == lanes, code_row, 0), axis=1, keepdims=True)
        token = jnp.where(
            long_col > 0, (long_col % 128 - 1) * 8 + iota((128, 1), 0) % 8, 512
        )
        pick[g * 128 : g * 128 + 128, :] = jnp.where(
            iota((128, 512), 1) == token, 1.0, 0.0
        ).astype(BF16)
    code_col = jnp.concatenate(code_cols, axis=0)
    valid = code_col > 0
    k_col = (code_col // 128) % 32
    row_col = code_col % 128 - 1
    square = iota((64, 64), 0) == iota((64, 64), 1)
    code_row64 = jnp.sum(jnp.where(square, code_col, 0), axis=0, keepdims=True)
    k_row = (code_row64 // 128) % 32
    row_row = code_row64 % 128 - 1

    states_copy.wait()

    def norm_pair(pair, carry):
        both = []
        for half in range(2):
            values = st[pair * 2 + half].astype(F32)
            mean_square = jnp.mean(values * values, axis=-1, keepdims=True)
            both.append(values * lax.rsqrt(mean_square + EPS) * gain_ref[...])
        rows = pl.ds(pl.multiple_of(pair * 16, 16), 16)
        stored[rows, :] = jnp.concatenate(both, axis=0).astype(BF16)
        return carry

    lax.fori_loop(0, 32, norm_pair, 0)

    for p in range(3):
        for step in (1, 2, 3):
            gather_wait(p, 1, step)
    gather_start(2)
    for p in range(3):
        forward(p, 0)

    for step in (1, 2, 3):
        arrived(rqt.at[(my_group + 4 - step) % 4], RQ + step - 1)
    for g in range(4):
        match = rqt[g] == lane_ref[g : g + 1, :]
        row = jnp.sum(jnp.where(match, iota((32, 128), 0) + (g * 32 + 1), 0), axis=0, keepdims=True)
        ir_ref[g : g + 1, :] = row - 1
    decoder_of = jnp.maximum(ir_ref[0:4, :], 0)
    for p in range(3):
        block_ref[p * 4 : p * 4 + 4, :] = block_of(p, decoder_of // 32, decoder_of % 32)
    block_copy = pltpu.make_async_copy(block_ref, block_smem, local_sem.at[9])
    block_copy.start()

    def pick_step(n, carry):
        cols = pl.ds(pl.multiple_of(n * 256, 256), 256)
        nrm[:, cols] = nn(pick[...], stored[:, cols]).astype(BF16)
        return carry

    lax.fori_loop(0, 8, pick_step, 0)

    def project(begin, end):
        def step(n, carry):
            offset = pl.multiple_of(n * 256, 256)
            kv[:, pl.ds(offset, 256)] = nn(nrm[...], w[:, pl.ds(offset, 256)]).astype(BF16)
            return carry

        for n in range(begin, end):
            w_copies[n].wait()
        lax.fori_loop(begin * 2, end * 2, step, 0)

    project(0, 6)
    for step in (1, 3, 2):
        for p in range(3):
            gather_wait(p, 2, step)
            forward(p, step)
    project(6, 8)
    block_copy.wait()

    for p in range(3):
        for back in range(4):
            first, second, third = ORDERS[p]
            begin = (1 - core) * 64 + ((at[third] + 4 - back) % 4) * 16
            arrived(qs[p].at[pl.ds(begin, 16)], AG_SIB + p * 4 + back)

    low = (lane < 64).astype(F32).astype(BF16)
    high = (lane >= 64).astype(F32).astype(BF16)

    def scores_of(p, tiles):
        def step(n, carry):
            g, cc = n // tiles, n % tiles
            inner = pl.multiple_of(cc * 128, 128)
            outer = pl.multiple_of((3 * p + cc) * 128, 128)
            slots = pl.ds(pl.multiple_of(g * 128, 128), 128)
            right = jnp.concatenate(
                [kv[slots, pl.ds(outer, 128)], kv[slots, pl.ds(outer + 1024, 128)]], axis=0
            )
            left = []
            for r in range(SLOTS):
                block = qs[p][block_smem[p * 4 + g, r * 8], :, pl.ds(inner, 128)]
                left += [block * low, block * high]
            out = nt(jnp.concatenate(left, axis=0), right)
            total = [jnp.zeros((8, 128), F32) for _ in range(4)]
            for r in range(SLOTS):
                keep = jnp.broadcast_to(lane // 8 == r, (8, 128))
                for tile in range(4):
                    half = tile % 2
                    begin = r * 32 + tile * 8
                    piece = out[begin : begin + 8, half * 128 : half * 128 + 128]
                    total[tile] = jnp.where(keep, piece, total[tile])
            rows = pl.ds(pl.multiple_of((3 * p + cc) * 32, 32), 32)
            s_buf[g, rows, :] = jnp.concatenate(total, axis=0) * (64 ** (-0.5))
            return carry

        lax.fori_loop(0, 4 * tiles, step, 0)

    scores_of(0, 3)
    scores_of(1, 3)
    scores_of(2, 2)

    peak_i = jnp.zeros((256, 128), F32)
    total_i = jnp.zeros((256, 128), F32)
    present = jnp.zeros((8, 128), F32)
    for g in range(4):
        scores = s_buf[g]
        u_row = lane_ref[g : g + 1, :]
        peak = scores
        for s in (1, 2, 4):
            bit = jnp.broadcast_to((lane // s) % 2 == 1, (256, 128))
            other = jnp.where(bit, pltpu.roll(peak, s, 1), pltpu.roll(peak, 128 - s, 1))
            peak = jnp.maximum(peak, other)
        u_rows = jnp.broadcast_to(u_row, (8, 128))
        before = pltpu.roll(u_rows, 8, 1)[0:1, :]
        for s in (8, 16, 32, 64):
            same = (pltpu.roll(u_rows, s, 1)[0:1, :] == u_row) & (lane >= s)
            other = jnp.where(jnp.broadcast_to(same, (256, 128)), pltpu.roll(peak, s, 1), ABSENT)
            peak = jnp.maximum(peak, other)
        for s in (8, 16, 32, 64):
            same = (pltpu.roll(u_rows, 128 - s, 1)[0:1, :] == u_row) & (lane < 128 - s)
            other = jnp.where(
                jnp.broadcast_to(same, (256, 128)), pltpu.roll(peak, 128 - s, 1), ABSENT
            )
            peak = jnp.maximum(peak, other)
        chosen = sub == ir_ref[g : g + 1, :]
        first = ((before != u_row) | (lane < 8)) & (lane % 8 == 0)
        lead = jnp.where(chosen & jnp.broadcast_to(first, (128, 128)), 1.0, 0.0)
        peak_i = peak_i + nt(peak, lead, HIGHEST)
        total_i = total_i + nt(jnp.exp(scores - peak), jnp.where(chosen, 1.0, 0.0), HIGHEST)
        present = present + nt(jnp.ones((8, 128), F32), lead)
    table = jnp.where(
        jnp.broadcast_to(present[0:1, :] > 0.5, (256, 128)),
        peak_i + jnp.log(jnp.maximum(total_i, 1e-30)),
        ABSENT,
    )
    t0[...] = table[0:128, :]
    t1[...] = table[128:256, :]

    lane64 = iota((64, 128), 1)
    i_cols = []
    for g in range(4):
        picked = jnp.where(slot16, ir_ref[g : g + 1, :] + 1, 0)
        i_cols.append(jnp.sum(picked, axis=1, keepdims=True))
    i_col = jnp.concatenate(i_cols, axis=0) - 1
    one_hot_i = lane64 == i_col
    hot_i = jnp.where(one_hot_i, 1.0, 0.0)
    decoder = jnp.maximum(i_col, 0)
    place = block_of(2, decoder // 32, decoder % 32) * 16
    flat = q2[:, :, 256:384].reshape(2048, 128)
    wide = iota((64, 2048), 1)
    emb = jnp.concatenate(
        [nn(jnp.where(wide == place + c, 1.0, 0.0).astype(BF16), flat) for c in range(6)], axis=1
    )
    hot_row = jnp.where(iota((64, 64), 1) == row_col, 1.0, 0.0).astype(BF16)
    keys = nn(hot_row, keys_ref[...])
    retrieval = jnp.sum(emb * keys, axis=1, keepdims=True) * (E ** (-0.5))
    retrieval_row = jnp.sum(jnp.where(square, retrieval, 0.0), axis=0, keepdims=True)
    by_k = jnp.where(iota((32, 64), 0) == k_row, retrieval_row, 0.0)
    t2[...] = nn(by_k, hot_i, HIGHEST)

    size = (64, 64, 16)

    def combine(p, values):
        if p == 2:
            total = values[0]
            for value in values[1:]:
                total = total + value
            return total
        top = values[0]
        for value in values[1:]:
            top = jnp.maximum(top, value)
        total = jnp.exp(values[0] - top)
        for value in values[1:]:
            total = total + jnp.exp(value - top)
        return top + jnp.log(total)

    for p in range(3):
        other = pl.ds(pl.multiple_of((1 - core) * size[p], size[p]), size[p])
        start(ts[p].at[other], acs[p], AR + p * 11, sibling)
    for p in range(3):
        own = pl.ds(pl.multiple_of(core * size[p], size[p]), size[p])
        arrived(acs[p], AR + p * 11)
        accs[p][0] = combine(p, [ts[p][own, :], acs[p][...]])
        for step in (1, 2, 3):
            start(
                accs[p].at[0],
                ars[p].at[step - 1],
                AR + p * 11 + step,
                peer(ORDERS[p][0], step),
            )
    for stage in range(3):
        for p in range(3):
            values = [accs[p][stage]]
            for step in (1, 2, 3):
                arrived(ars[p].at[stage * 3 + step - 1], AR + p * 11 + stage * 3 + step)
                values.append(ars[p][stage * 3 + step - 1])
            total = combine(p, values)
            own = pl.ds(pl.multiple_of(core * size[p], size[p]), size[p])
            if stage == 2:
                ls[p][own, :] = total
                ref = ls[p].at[own]
                start(ref, ref, AR + p * 11 + 10, sibling)
            else:
                accs[p][stage + 1] = total
                for step in (1, 2, 3):
                    start(
                        accs[p].at[stage + 1],
                        ars[p].at[(stage + 1) * 3 + step - 1],
                        AR + p * 11 + (stage + 1) * 3 + step,
                        peer(ORDERS[p][stage + 1], step),
                    )
    for p in range(3):
        other = pl.ds(pl.multiple_of((1 - core) * size[p], size[p]), size[p])
        arrived(ls[p].at[other], AR + p * 11 + 10)

    log_sum = jnp.concatenate([l0[...], l1[...]], axis=0)
    targets = []
    for g in range(4):
        chosen = jnp.where(sub == ir_ref[g : g + 1, :], 1.0, 0.0)
        weights = jnp.exp(s_buf[g] - nn(log_sum, chosen, HIGHEST))
        p_buf[g] = weights.astype(BF16)
        mass = jnp.sum(weights, axis=0, keepdims=True)
        own = iota((16, 128), 1) // 8 == iota((16, 128), 0)
        targets.append(jnp.sum(jnp.where(own, mass, 0.0), axis=1, keepdims=True))
    target = jnp.concatenate(targets, axis=0) * (1.0 / 256.0)
    raw = l2[...]
    top = jnp.max(raw, axis=0, keepdims=True)
    log_prob_all = raw - top - jnp.log(jnp.sum(jnp.exp(raw - top), axis=0, keepdims=True))
    hot_k = jnp.where(iota((64, 32), 1) == k_col, 1.0, 0.0)
    log_prob = jnp.sum(
        jnp.where(one_hot_i, nn(hot_k, log_prob_all, HIGHEST), 0.0), axis=1, keepdims=True
    )
    term = jnp.where(valid, target * (jnp.log(target) - log_prob), 0.0)
    loss_row = jnp.sum(jnp.where(one_hot_i, term, 0.0), axis=0, keepdims=True)
    loss_col = jnp.sum(jnp.where(sub == lanes, loss_row, 0.0), axis=1, keepdims=True)
    loss_t[...] = jnp.broadcast_to(loss_col, (128, 128))

    def loss_block(j, carry):
        for g in range(4):
            value = jnp.broadcast_to(loss_t[pl.ds(g * 32 + j, 1), :], (8, 128))
            top_half = value.astype(BF16).astype(F32)
            tile = jnp.concatenate([top_half, value - top_half], axis=0)
            c2[block_of(2, g, j), :, 256:384] = tile.astype(BF16)
        return carry

    lax.fori_loop(0, 32, loss_block, 0)

    keep_low = jnp.broadcast_to(lane < 64, (8, 128))

    def context_set(p, to):
        tiles = 2 if p == 2 else 3

        def tile_of(g, cc, decoders):
            inner = pl.multiple_of(cc * 128, 128)
            outer = pl.multiple_of(D + (3 * p + cc) * 128, 128)
            slots = pl.ds(pl.multiple_of(g * 128, 128), 128)
            right = jnp.concatenate(
                [kv[slots, pl.ds(outer, 128)], kv[slots, pl.ds(outer + 1024, 128)]], axis=1
            )
            row = ir_ref[pl.ds(g, 1), :] - g * 32
            rows = pl.ds(pl.multiple_of((3 * p + cc) * 32, 32), 32)
            weights = p_buf[g, rows, :]
            for first in range(0, len(decoders), 16):
                batch = decoders[first : first + 16]
                left = []
                for j in batch:
                    keep = jnp.where(row == j, 1.0, 0.0).astype(BF16)
                    left.append(weights * keep)
                out = nn(jnp.concatenate(left, axis=0), right)
                for n, j in enumerate(batch):
                    halves = []
                    for half in range(2):
                        cols = slice(half * 128, half * 128 + 128)
                        begin = n * 32 + half * 8
                        halves.append(
                            jnp.where(
                                keep_low,
                                out[begin : begin + 8, cols],
                                out[begin + 16 : begin + 24, cols],
                            )
                        )
                    tile = jnp.concatenate(halves, axis=0).astype(BF16)
                    cs[p][block_of(p, g, j), :, pl.ds(inner, 128)] = tile

        if p == 0:

            def step(cc, carry):
                tile_of(to, cc, list(range(32)))
                return carry

            lax.fori_loop(0, tiles, step, 0)
        else:

            def step(n, carry):
                if p == 1:
                    decoders = [y * 8 + to * 2 + c for y in range(4) for c in range(2)]
                else:
                    decoders = [to * 8 + x * 2 + c for x in range(4) for c in range(2)]
                tile_of(n // tiles, n % tiles, decoders)
                return carry

            lax.fori_loop(0, 4 * tiles, step, 0)

    def reach(p, stage, to):
        first, second, third = ORDERS[p]
        if stage == 0:
            return core * 64 + to * 16, 16
        if stage == 1:
            return core * 64 + at[third] * 16 + to * 4, 4
        return core * 64 + at[third] * 16 + at[second] * 4 + to, 1

    def set_of(p, n):
        return (at[ORDERS[p][2]] + n + 1) % 4

    def swap_copy(p, n):
        to = set_of(p, n)
        return remote(
            cs[p].at[pl.ds((1 - core) * 64 + to * 16, 16)],
            rcs[p].at[pl.ds(to * 16, 16)],
            RS + p * 13 + n,
            sibling,
        )

    def scatter_copy(p, stage, step):
        axis = ORDERS[p][2 - stage]
        begin, count = reach(p, stage, (at[axis] + step) % 4)
        return remote(
            cs[p].at[pl.ds(begin, count)],
            rstage[stage][p].at[pl.ds((step - 1) * count, count)],
            RS + p * 13 + 4 + stage * 3 + step - 1,
            peer(axis, step),
        )

    def scatter_start(p, stage):
        for step in (1, 2, 3):
            copy = scatter_copy(p, stage, step)
            copy.start()
            started.append(copy)

    def swap_finish(p, n):
        to = set_of(p, n)
        arrived(rcs[p].at[pl.ds(to * 16, 16)], RS + p * 13 + n)

        def step(b, carry):
            mine_at = core * 64 + to * 16 + b
            _, block = add_blocks(p, [cs[p][mine_at], rcs[p][to * 16 + b]])
            cs[p][mine_at] = block
            return carry

        lax.fori_loop(0, 16, step, 0)

        @pl.when(n < 3)
        def _():
            scatter_copy(p, 0, n + 1).start()

    def scatter_wait(p, stage):
        count = (16, 4, 1)[stage]
        for step in (1, 2, 3):
            arrived(
                rstage[stage][p].at[pl.ds((step - 1) * count, count)],
                RS + p * 13 + 4 + stage * 3 + step - 1,
            )

    def scatter_add(p, stage):
        axis = ORDERS[p][2 - stage]
        begin, count = reach(p, stage, at[axis])
        scatter_wait(p, stage)

        def step(b, carry):
            parts = [rstage[stage][p][n * count + b] for n in range(3)]
            _, block = add_blocks(p, [cs[p][begin + b]] + parts)
            cs[p][begin + b] = block
            return carry

        lax.fori_loop(0, count, step, 0)

    def scatter_set(n, carry):
        for p in range(3):
            context_set(p, set_of(p, n))
            swap_copy(p, n).start()
            if p > 0:
                swap_finish(p - 1, n)
            else:

                @pl.when(n > 0)
                def _():
                    swap_finish(2, n - 1)

        return carry

    lax.fori_loop(0, 4, scatter_set, 0)
    swap_finish(2, 3)
    for p in range(3):
        started.extend(swap_copy(p, n) for n in range(4))
        started.extend(scatter_copy(p, 0, step) for step in (1, 2, 3))

    coefficient = (LOSS_WEIGHT * E ** (-0.5)) * (jnp.exp(log_prob) - target)
    grads = jnp.where(valid, coefficient * emb, 0.0).astype(BF16)
    hot_row_t = jnp.where(iota((64, 64), 0) == row_row, 1.0, 0.0).astype(BF16)
    grad_ref[...] = nn(hot_row_t, grads)

    for p in range(3):
        scatter_add(p, 0)
        scatter_start(p, 1)
    for p in range(3):
        scatter_add(p, 1)
        scatter_start(p, 2)
    for p in range(3):
        begin, _ = reach(p, 2, at[ORDERS[p][0]])
        scatter_wait(p, 2)
        total, _ = add_blocks(p, [cs[p][begin]] + [rstage[2][p][n] for n in range(3)])
        for cc in range(2 if p == 2 else 3):
            c = 3 * p + cc
            cols = total[:, cc * 128 : cc * 128 + 128].astype(BF16)
            ctx_ref[0, :, c * 128 : c * 128 + 128] = total[0:8, cc * 128 : cc * 128 + 128].astype(BF16)
            ctx_ref[0, :, 1024 + c * 128 : 1152 + c * 128] = total[
                8:16, cc * 128 : cc * 128 + 128
            ].astype(BF16)
        if p == 2:
            loss_ref[...] = total[0:8, 256:384] + total[8:16, 256:384]

    for copy in started:
        copy.wait_send()


def hand_over(ctx_ref, loss_ref, grad_ref, ctx_out, loss_out, grad_out):
    ctx_out[...] = ctx_ref[...]
    loss_out[0] = loss_ref[0, 0]
    grad_out[...] = grad_ref[...]


def body(
    store_states,
    store_keys,
    passage_ids,
    store_slot,
    row_question,
    queries,
    question_emb,
    enc_gain,
    key_weight,
    value_weight,
):
    vmem = pl.BlockSpec(memory_space=pltpu.VMEM)
    anywhere = pl.BlockSpec(memory_space=pl.ANY)
    scratch = [
        pltpu.VMEM((64, 8, D), BF16),
        pltpu.VMEM((D, 2 * D), BF16),
        pltpu.VMEM((512, D), BF16),
        pltpu.VMEM((512, 512), BF16),
        pltpu.VMEM((512, D), BF16),
        pltpu.VMEM((512, 2 * D), BF16),
    ]
    scratch += [pltpu.VMEM((128, 16, 384), BF16)] * 6
    scratch += [pltpu.VMEM((64, 16, 384), BF16)] * 3
    scratch += [pltpu.VMEM((48, 16, 384), BF16)] * 3
    scratch += [pltpu.VMEM((12, 16, 384), BF16)] * 3
    scratch += [pltpu.VMEM((3, 16, 384), BF16)] * 3
    scratch += [pltpu.VMEM((4, 256, 128), F32), pltpu.VMEM((4, 256, 128), BF16)]
    sizes = (64, 64, 16)
    scratch += [pltpu.VMEM((2 * n, 128), F32) for n in sizes]
    scratch += [pltpu.VMEM((n, 128), F32) for n in sizes]
    scratch += [pltpu.VMEM((9, n, 128), F32) for n in sizes]
    scratch += [pltpu.VMEM((3, n, 128), F32) for n in sizes]
    scratch += [pltpu.VMEM((2 * n, 128), F32) for n in sizes]
    scratch += [
        pltpu.VMEM((4, 32, 128), jnp.int32),
        pltpu.VMEM((8, 128), jnp.int32),
        pltpu.VMEM((8, 128), jnp.int32),
        pltpu.VMEM((16, 128), jnp.int32),
        pltpu.SMEM((16, 128), jnp.int32),
        pltpu.VMEM((128, 128), F32),
        pltpu.SemaphoreType.DMA((SEMS,)),
        pltpu.SemaphoreType.DMA((SEMS,)),
        pltpu.SemaphoreType.DMA((10,)),
    ]
    context, loss, grad = pl.pallas_call(
        kernel,
        out_shape=(
            jax.ShapeDtypeStruct((1, 8, D), BF16),
            jax.ShapeDtypeStruct((8, 128), F32),
            jax.ShapeDtypeStruct((STORE, E), F32),
        ),
        in_specs=[
            vmem,
            vmem,
            vmem,
            anywhere,
            vmem,
            vmem,
            vmem,
            vmem,
            anywhere,
            anywhere,
        ],
        out_specs=(vmem, vmem, vmem),
        scratch_shapes=scratch,
        compiler_params=pltpu.CompilerParams(
            collective_id=0, has_side_effects=True, vmem_limit_bytes=60 * 1024 * 1024
        ),
        cost_estimate=pl.CostEstimate(
            flops=12 * 10**9, bytes_accessed=20 * 10**6, transcendentals=10**6
        ),
    )(
        passage_ids.T,
        store_slot.reshape(64, 128),
        row_question,
        store_states,
        store_keys,
        queries,
        question_emb,
        enc_gain.reshape(1, D),
        key_weight,
        value_weight,
    )
    return pl.pallas_call(
        hand_over,
        out_shape=(
            jax.ShapeDtypeStruct((1, 8, D), BF16),
            jax.ShapeDtypeStruct((1,), F32),
            jax.ShapeDtypeStruct((STORE, E), F32),
        ),
        in_specs=[vmem, vmem, vmem],
        out_specs=(vmem, pl.BlockSpec(memory_space=pltpu.SMEM), vmem),
    )(context, loss, grad)


def solution(mesh):
    in_specs = (
        P(("group", "dev"), None, None),
        P(("group", "dev"), None),
        P(),
        P(),
        P("group", None),
        P(("group", "dev"), None, None),
        P(("group", "dev"), None),
        P(),
        P(),
        P(),
    )
    out_specs = (P(("group", "dev"), None, None), P(("group", "dev")), P(("group", "dev"), None))
    return jax.shard_map(body, mesh=mesh, in_specs=in_specs, out_specs=out_specs, check_vma=False)
```

```python
import functools

import jax
import jax.numpy as jnp
from jax import lax
from jax.experimental import pallas as pl
from jax.experimental.pallas import tpu as pltpu
from jax.sharding import PartitionSpec as P

MESH = pl.DeviceIdType.MESH
F32 = jnp.float32
BF16 = jnp.bfloat16
HIGHEST = lax.Precision.HIGHEST

D = 2048
E = 768
GROUPS = 4
PER_GROUP = 32
SLOTS = 16
LANES = 128
STORE = 64
EPS = 1e-06
LOSS_WEIGHT = 256.0
ABSENT = -1e30

ORDERS = (("x", "y", "z"), ("y", "z", "x"), ("z", "x", "y"))
AG, AG_SIB, RQ, AR, RS = 0, 27, 39, 42, 75
SEMS = 114


def nt(a, b, precision=None):
    return lax.dot_general(
        a, b, (((1,), (1,)), ((), ())), preferred_element_type=F32, precision=precision
    )


def nn(a, b, precision=None):
    return jnp.dot(a, b, preferred_element_type=F32, precision=precision)


def iota(shape, dim):
    return lax.broadcasted_iota(jnp.int32, shape, dim)


def block_of(part, g, j):
    y, x, core = j // 8, (j // 2) % 4, j % 2
    at = {"x": x, "y": y, "z": g}
    first, second, third = ORDERS[part]
    return core * 64 + at[third] * 16 + at[second] * 4 + at[first]


def add_blocks(part, blocks):
    total = blocks[0].astype(F32)
    for block in blocks[1:]:
        total = total + block.astype(F32)
    if part < 2:
        return total, total.astype(BF16)
    loss = total[0:8, 256:384] + total[8:16, 256:384]
    high = loss.astype(BF16).astype(F32)
    tile = jnp.concatenate([high, loss - high], axis=0)
    return total, jnp.concatenate([total[:, 0:256], tile], axis=1).astype(BF16)


def kernel(
    ids_ref,
    slot_ref,
    rq_ref,
    states_ref,
    keys_ref,
    queries_ref,
    emb_ref,
    gain_ref,
    kw_ref,
    vw_ref,
    ctx_ref,
    loss_ref,
    grad_ref,
    st,
    w,
    stored,
    pick,
    nrm,
    kv,
    keys_t,
    q0,
    q1,
    q2,
    c0,
    c1,
    c2,
    rc0,
    rc1,
    rc2,
    ra0,
    ra1,
    ra2,
    rb0,
    rb1,
    rb2,
    rd0,
    rd1,
    rd2,
    s_buf,
    p_buf,
    t0,
    t1,
    t2,
    ac0,
    ac1,
    ac2,
    ar0,
    ar1,
    ar2,
    acc0,
    acc1,
    acc2,
    l0,
    l1,
    l2,
    rqt,
    lane_ref,
    ir_ref,
    block_ref,
    block_smem,
    loss_t,
    send_sem,
    recv_sem,
    local_sem,
):
    qs, cs, rcs = (q0, q1, q2), (c0, c1, c2), (rc0, rc1, rc2)
    rstage = ((ra0, ra1, ra2), (rb0, rb1, rb2), (rd0, rd1, rd2))
    ts, acs, ars, accs, ls = (
        (t0, t1, t2),
        (ac0, ac1, ac2),
        (ar0, ar1, ar2),
        (acc0, acc1, acc2),
        (l0, l1, l2),
    )
    my_group = lax.axis_index("group")
    my_dev = lax.axis_index("dev")
    core = my_dev % 2
    at = {"x": (my_dev // 2) % 4, "y": my_dev // 8, "z": my_group}
    sibling = (my_group, my_dev + 1 - 2 * core)

    def peer(axis, step):
        to = (at[axis] + step) % 4
        if axis == "z":
            return (to, my_dev)
        if axis == "y":
            return (my_group, to * 8 + at["x"] * 2 + core)
        return (my_group, at["y"] * 8 + to * 2 + core)

    started = []

    def remote(src, dst, number, device):
        copy = pltpu.make_async_remote_copy(
            src_ref=src,
            dst_ref=dst,
            send_sem=send_sem.at[number],
            recv_sem=recv_sem.at[number],
            device_id=device,
            device_id_type=MESH,
        )
        return copy

    def start(src, dst, number, device):
        copy = remote(src, dst, number, device)
        copy.start()
        started.append(copy)

    def arrived(dst, number):
        remote(dst, dst, number, sibling).wait_recv()

    states_copy = pltpu.make_async_copy(states_ref, st, local_sem.at[8])
    states_copy.start()
    w_copies = []
    for n in range(8):
        src = kw_ref if n < 4 else vw_ref
        copy = pltpu.make_async_copy(
            src.at[:, pl.ds((n % 4) * 512, 512)],
            w.at[:, pl.ds(n * 512, 512)],
            local_sem.at[n],
        )
        copy.start()
        w_copies.append(copy)

    mine = [
        core * 64 + at[ORDERS[p][2]] * 16 + at[ORDERS[p][1]] * 4 + at[ORDERS[p][0]]
        for p in range(3)
    ]
    for c in range(8):
        tile = jnp.concatenate(
            [
                queries_ref[0, :, c * 128 : c * 128 + 128].astype(F32),
                queries_ref[0, :, 1024 + c * 128 : 1152 + c * 128].astype(F32),
            ],
            axis=0,
        )
        qs[c // 3][mine[c // 3], :, (c % 3) * 128 : (c % 3) * 128 + 128] = tile.astype(BF16)
    emb_rows = [emb_ref[:, c * 128 : c * 128 + 128].astype(F32) for c in range(6)]
    emb_tile = jnp.concatenate(emb_rows + [jnp.zeros((10, 128), F32)], axis=0)
    q2[mine[2], :, 256:384] = emb_tile.astype(BF16)
    diagonal = iota((32, 32), 0) == iota((32, 32), 1)
    rq_col = jnp.sum(jnp.where(diagonal, rq_ref[...], 0), axis=1, keepdims=True)
    rqt[my_group] = jnp.broadcast_to(rq_col, (32, 128))

    barrier = pltpu.get_barrier_semaphore()
    pl.semaphore_signal(barrier, inc=1, device_id=sibling, device_id_type=MESH)
    for axis in ("x", "y", "z"):
        for step in (1, 2, 3):
            pl.semaphore_signal(barrier, inc=1, device_id=peer(axis, step), device_id_type=MESH)
    pl.semaphore_wait(barrier, 10)

    def span(p, stage, back):
        first, second, third = ORDERS[p]
        digit = (at[ORDERS[p][stage]] + 4 - back) % 4
        if stage == 0:
            return core * 64 + at[third] * 16 + at[second] * 4 + digit, 1
        if stage == 1:
            return core * 64 + at[third] * 16 + digit * 4, 4
        return core * 64 + digit * 16, 16

    def gather_start(stage):
        for p in range(3):
            begin, size = span(p, stage, 0)
            for step in (1, 2, 3):
                ref = qs[p].at[pl.ds(begin, size)]
                start(ref, ref, AG + (p * 3 + stage) * 3 + step - 1, peer(ORDERS[p][stage], step))

    def gather_wait(p, stage, step):
        begin, size = span(p, stage, step)
        arrived(qs[p].at[pl.ds(begin, size)], AG + (p * 3 + stage) * 3 + step - 1)

    def forward(p, back):
        begin, size = span(p, 2, back)
        ref = qs[p].at[pl.ds(begin, size)]
        start(ref, ref, AG_SIB + p * 4 + back, sibling)

    gather_start(0)
    for step in (1, 2, 3):
        start(rqt.at[my_group], rqt.at[my_group], RQ + step - 1, peer("z", step))

    lane = iota((1, 128), 1)
    sub = iota((128, 128), 0)
    lanes = iota((128, 128), 1)
    first_row = (my_group * PER_GROUP + my_dev) * STORE
    local = slot_ref[...] - first_row
    local = jnp.where((local >= 0) & (local < STORE), local + 1, 0).astype(F32)
    local_t = jnp.transpose(local).astype(BF16)
    ids_high = ids_ref[...] // 128
    ids_low = ids_ref[...] % 128
    high_sub = iota((64, 128), 0)
    lane32 = iota((128, 32), 1)
    held_rows = []
    for k in range(32):
        hot = jnp.where(high_sub == ids_high[k : k + 1, :], 1.0, 0.0).astype(BF16)
        found = jnp.where(sub == ids_low[k : k + 1, :], nn(local_t, hot), 0.0)
        held_rows.append(jnp.sum(found, axis=0, keepdims=True))
    held = jnp.transpose(jnp.concatenate(held_rows, axis=0))
    for p in range(3):
        for step in (1, 2, 3):
            gather_wait(p, 0, step)
    gather_start(1)

    held_int = held.astype(jnp.int32)
    mine_f = jnp.where(held_int > 0, 1.0, 0.0)
    mine_b = mine_f.astype(BF16)
    in_row = nn(mine_b, jnp.ones((32, 32), BF16))
    above = jnp.where((sub // 32 == lanes // 32) & (lanes < sub), 1.0, 0.0).astype(BF16)
    upto = jnp.where(iota((32, 32), 0) <= iota((32, 32), 1), 1.0, 0.0).astype(BF16)
    rank = nn(above, in_row.astype(BF16)) + nn(mine_b, upto)
    rank = jnp.where(held_int > 0, rank.astype(jnp.int32), 0)
    code = (iota((128, 32), 0) % 32) * 4096 + lane32 * 128 + held_int
    spread = jnp.zeros((128, 128), jnp.int32)
    for n in range(SLOTS):
        here = jnp.sum(jnp.where(rank == n + 1, code, 0), axis=1, keepdims=True)
        spread = jnp.where(lanes // 8 == n, here, spread)
    code_cols = []
    slot16 = iota((16, 128), 1) == iota((16, 128), 0) * 8
    for g in range(4):
        code_row = jnp.sum(spread[g * 32 : g * 32 + 32], axis=0, keepdims=True)
        lane_ref[g : g + 1, :] = jnp.where(code_row > 0, code_row // 4096, -1)
        code_cols.append(jnp.sum(jnp.where(slot16, code_row, 0), axis=1, keepdims=True))
        long_col = jnp.sum(jnp.where(sub == lanes, code_row, 0), axis=1, keepdims=True)
        token = jnp.where(
            long_col > 0, (long_col % 128 - 1) * 8 + iota((128, 1), 0) % 8, 512
        )
        pick[g * 128 : g * 128 + 128, :] = jnp.where(
            iota((128, 512), 1) == token, 1.0, 0.0
        ).astype(BF16)
    code_col = jnp.concatenate(code_cols, axis=0)
    valid = code_col > 0
    k_col = (code_col // 128) % 32
    row_col = code_col % 128 - 1
    square = iota((64, 64), 0) == iota((64, 64), 1)
    code_row64 = jnp.sum(jnp.where(square, code_col, 0), axis=0, keepdims=True)
    k_row = (code_row64 // 128) % 32
    row_row = code_row64 % 128 - 1

    for p in range(3):
        for step in (1, 2, 3):
            gather_wait(p, 1, step)
    gather_start(2)
    for p in range(3):
        forward(p, 0)

    for step in (1, 2, 3):
        arrived(rqt.at[(my_group + 4 - step) % 4], RQ + step - 1)
    for g in range(4):
        match = rqt[g] == lane_ref[g : g + 1, :]
        row = jnp.sum(jnp.where(match, iota((32, 128), 0) + (g * 32 + 1), 0), axis=0, keepdims=True)
        ir_ref[g : g + 1, :] = row - 1
    decoder_of = jnp.maximum(ir_ref[0:4, :], 0)
    for p in range(3):
        block_ref[p * 4 : p * 4 + 4, :] = block_of(p, decoder_of // 32, decoder_of % 32)
    block_copy = pltpu.make_async_copy(block_ref, block_smem, local_sem.at[9])
    block_copy.start()

    states_copy.wait()

    def norm_pair(pair, carry):
        both = []
        for half in range(2):
            values = st[pair * 2 + half].astype(F32)
            mean_square = jnp.mean(values * values, axis=-1, keepdims=True)
            both.append(values * lax.rsqrt(mean_square + EPS) * gain_ref[...])
        rows = pl.ds(pl.multiple_of(pair * 16, 16), 16)
        stored[rows, :] = jnp.concatenate(both, axis=0).astype(BF16)
        return carry

    lax.fori_loop(0, 32, norm_pair, 0)

    def pick_step(n, carry):
        cols = pl.ds(pl.multiple_of(n * 256, 256), 256)
        nrm[:, cols] = nn(pick[...], stored[:, cols]).astype(BF16)
        return carry

    lax.fori_loop(0, 8, pick_step, 0)

    def project(begin, end):
        def step(n, carry):
            offset = pl.multiple_of(n * 256, 256)
            kv[:, pl.ds(offset, 256)] = nn(nrm[...], w[:, pl.ds(offset, 256)]).astype(BF16)
            return carry

        for n in range(begin, end):
            w_copies[n].wait()
        lax.fori_loop(begin * 2, end * 2, step, 0)

    project(0, 4)
    for step in (1, 3, 2):
        for p in range(3):
            gather_wait(p, 2, step)
            forward(p, step)
    def turn(n, carry):
        rows = pl.ds(pl.multiple_of(n * 256, 256), 256)
        keys_t[rows, :] = jnp.transpose(kv[:, rows].astype(F32)).astype(BF16)
        return carry

    lax.fori_loop(0, 8, turn, 0)
    project(4, 6)
    block_copy.wait()

    for p in range(3):
        for back in range(4):
            first, second, third = ORDERS[p]
            begin = (1 - core) * 64 + ((at[third] + 4 - back) % 4) * 16
            arrived(qs[p].at[pl.ds(begin, 16)], AG_SIB + p * 4 + back)

    low = (lane < 64).astype(F32).astype(BF16)
    high = (lane >= 64).astype(F32).astype(BF16)

    def scores_of(p, tiles):
        def step(cc, carry):
            inner = pl.multiple_of(cc * 128, 128)
            outer = pl.multiple_of((3 * p + cc) * 128, 128)
            rows = pl.ds(pl.multiple_of((3 * p + cc) * 32, 32), 32)
            for g in range(4):
                slots = slice(g * 128, g * 128 + 128)
                right = jnp.concatenate(
                    [keys_t[pl.ds(outer, 128), slots], keys_t[pl.ds(outer + 1024, 128), slots]],
                    axis=1,
                )
                left = []
                for r in range(SLOTS):
                    block = qs[p][block_smem[p * 4 + g, r * 8], :, pl.ds(inner, 128)]
                    left += [block * low, block * high]
                out = nn(jnp.concatenate(left, axis=0), right)
                total = [jnp.zeros((8, 128), F32) for _ in range(4)]
                for r in range(SLOTS):
                    keep = jnp.broadcast_to(lane // 8 == r, (8, 128))
                    for tile in range(4):
                        half = tile % 2
                        begin = r * 32 + tile * 8
                        piece = out[begin : begin + 8, half * 128 : half * 128 + 128]
                        total[tile] = jnp.where(keep, piece, total[tile])
                s_buf[g, rows, :] = jnp.concatenate(total, axis=0) * (64 ** (-0.5))
            return carry

        lax.fori_loop(0, tiles, step, 0)

    scores_of(0, 3)
    scores_of(1, 3)
    scores_of(2, 2)

    peak_i = jnp.zeros((256, 128), F32)
    total_i = jnp.zeros((256, 128), F32)
    present = jnp.zeros((8, 128), F32)
    for g in range(4):
        scores = s_buf[g]
        u_row = lane_ref[g : g + 1, :]
        peak = scores
        for s in (1, 2, 4):
            bit = jnp.broadcast_to((lane // s) % 2 == 1, (256, 128))
            other = jnp.where(bit, pltpu.roll(peak, s, 1), pltpu.roll(peak, 128 - s, 1))
            peak = jnp.maximum(peak, other)
        u_rows = jnp.broadcast_to(u_row, (8, 128))
        before = pltpu.roll(u_rows, 8, 1)[0:1, :]
        for s in (8, 16, 32, 64):
            same = (pltpu.roll(u_rows, s, 1)[0:1, :] == u_row) & (lane >= s)
            other = jnp.where(jnp.broadcast_to(same, (256, 128)), pltpu.roll(peak, s, 1), ABSENT)
            peak = jnp.maximum(peak, other)
        for s in (8, 16, 32, 64):
            same = (pltpu.roll(u_rows, 128 - s, 1)[0:1, :] == u_row) & (lane < 128 - s)
            other = jnp.where(
                jnp.broadcast_to(same, (256, 128)), pltpu.roll(peak, 128 - s, 1), ABSENT
            )
            peak = jnp.maximum(peak, other)
        chosen = sub == ir_ref[g : g + 1, :]
        first = ((before != u_row) | (lane < 8)) & (lane % 8 == 0)
        lead = jnp.where(chosen & jnp.broadcast_to(first, (128, 128)), 1.0, 0.0)
        peak_i = peak_i + nt(peak, lead, HIGHEST)
        total_i = total_i + nt(jnp.exp(scores - peak), jnp.where(chosen, 1.0, 0.0), HIGHEST)
        present = present + nt(jnp.ones((8, 128), F32), lead)
    table = jnp.where(
        jnp.broadcast_to(present[0:1, :] > 0.5, (256, 128)),
        peak_i + jnp.log(jnp.maximum(total_i, 1e-30)),
        ABSENT,
    )
    t0[...] = table[0:128, :]
    t1[...] = table[128:256, :]
    size = (64, 64, 16)

    def table_swap(p):
        other = pl.ds(pl.multiple_of((1 - core) * size[p], size[p]), size[p])
        start(ts[p].at[other], acs[p], AR + p * 11, sibling)

    table_swap(0)
    table_swap(1)

    lane64 = iota((64, 128), 1)
    i_cols = []
    for g in range(4):
        picked = jnp.where(slot16, ir_ref[g : g + 1, :] + 1, 0)
        i_cols.append(jnp.sum(picked, axis=1, keepdims=True))
    i_col = jnp.concatenate(i_cols, axis=0) - 1
    one_hot_i = lane64 == i_col
    hot_i = jnp.where(one_hot_i, 1.0, 0.0)
    decoder = jnp.maximum(i_col, 0)
    place = block_of(2, decoder // 32, decoder % 32) * 16
    flat = q2[:, :, 256:384].reshape(2048, 128)
    wide = iota((64, 2048), 1)
    emb = jnp.concatenate(
        [nn(jnp.where(wide == place + c, 1.0, 0.0).astype(BF16), flat) for c in range(6)], axis=1
    )
    hot_row = jnp.where(iota((64, 64), 1) == row_col, 1.0, 0.0).astype(BF16)
    keys = nn(hot_row, keys_ref[...])
    retrieval = jnp.sum(emb * keys, axis=1, keepdims=True) * (E ** (-0.5))
    retrieval_row = jnp.sum(jnp.where(square, retrieval, 0.0), axis=0, keepdims=True)
    by_k = jnp.where(iota((32, 64), 0) == k_row, retrieval_row, 0.0)
    t2[...] = nn(by_k, hot_i, HIGHEST)
    table_swap(2)


    def combine(p, values):
        if p == 2:
            total = values[0]
            for value in values[1:]:
                total = total + value
            return total
        top = values[0]
        for value in values[1:]:
            top = jnp.maximum(top, value)
        total = jnp.exp(values[0] - top)
        for value in values[1:]:
            total = total + jnp.exp(value - top)
        return top + jnp.log(total)

    for p in range(3):
        own = pl.ds(pl.multiple_of(core * size[p], size[p]), size[p])
        arrived(acs[p], AR + p * 11)
        accs[p][0] = combine(p, [ts[p][own, :], acs[p][...]])
        for step in (1, 2, 3):
            start(
                accs[p].at[0],
                ars[p].at[step - 1],
                AR + p * 11 + step,
                peer(ORDERS[p][0], step),
            )
    for stage in range(3):
        if stage < 2:
            project(6 + stage, 7 + stage)
        for p in range(3):
            values = [accs[p][stage]]
            for step in (1, 2, 3):
                arrived(ars[p].at[stage * 3 + step - 1], AR + p * 11 + stage * 3 + step)
                values.append(ars[p][stage * 3 + step - 1])
            total = combine(p, values)
            own = pl.ds(pl.multiple_of(core * size[p], size[p]), size[p])
            if stage == 2:
                ls[p][own, :] = total
                ref = ls[p].at[own]
                start(ref, ref, AR + p * 11 + 10, sibling)
            else:
                accs[p][stage + 1] = total
                for step in (1, 2, 3):
                    start(
                        accs[p].at[stage + 1],
                        ars[p].at[(stage + 1) * 3 + step - 1],
                        AR + p * 11 + (stage + 1) * 3 + step,
                        peer(ORDERS[p][stage + 1], step),
                    )
    for p in range(3):
        other = pl.ds(pl.multiple_of((1 - core) * size[p], size[p]), size[p])
        arrived(ls[p].at[other], AR + p * 11 + 10)

    log_sum = jnp.concatenate([l0[...], l1[...]], axis=0)
    targets = []
    for g in range(4):
        chosen = jnp.where(sub == ir_ref[g : g + 1, :], 1.0, 0.0)
        weights = jnp.exp(s_buf[g] - nn(log_sum, chosen, HIGHEST))
        p_buf[g] = weights.astype(BF16)
        mass = jnp.sum(weights, axis=0, keepdims=True)
        own = iota((16, 128), 1) // 8 == iota((16, 128), 0)
        targets.append(jnp.sum(jnp.where(own, mass, 0.0), axis=1, keepdims=True))
    target = jnp.concatenate(targets, axis=0) * (1.0 / 256.0)
    raw = l2[...]
    top = jnp.max(raw, axis=0, keepdims=True)
    log_prob_all = raw - top - jnp.log(jnp.sum(jnp.exp(raw - top), axis=0, keepdims=True))
    hot_k = jnp.where(iota((64, 32), 1) == k_col, 1.0, 0.0)
    log_prob = jnp.sum(
        jnp.where(one_hot_i, nn(hot_k, log_prob_all, HIGHEST), 0.0), axis=1, keepdims=True
    )
    term = jnp.where(valid, target * (jnp.log(target) - log_prob), 0.0)
    loss_row = jnp.sum(jnp.where(one_hot_i, term, 0.0), axis=0, keepdims=True)
    loss_col = jnp.sum(jnp.where(sub == lanes, loss_row, 0.0), axis=1, keepdims=True)
    loss_t[...] = jnp.broadcast_to(loss_col, (128, 128))

    def loss_set(to):
        def step(g, carry):
            for x in range(4):
                for c in range(2):
                    j = to * 8 + x * 2 + c
                    value = jnp.broadcast_to(loss_t[pl.ds(g * 32 + j, 1), :], (8, 128))
                    top_half = value.astype(BF16).astype(F32)
                    tile = jnp.concatenate([top_half, value - top_half], axis=0)
                    c2[block_of(2, g, j), :, 256:384] = tile.astype(BF16)
            return carry

        lax.fori_loop(0, 4, step, 0)

    keep_low = jnp.broadcast_to(lane < 64, (8, 128))

    def context_set(p, to):
        tiles = 2 if p == 2 else 3

        def tile_of(g, cc, decoders):
            inner = cc * 128
            outer = D + (3 * p + cc) * 128
            slots = pl.ds(pl.multiple_of(g * 128, 128), 128)
            right = jnp.concatenate(
                [kv[slots, pl.ds(outer, 128)], kv[slots, pl.ds(outer + 1024, 128)]], axis=1
            )
            row = ir_ref[pl.ds(g, 1), :] - g * 32
            rows = pl.ds((3 * p + cc) * 32, 32)
            weights = p_buf[g, rows, :]
            for first in range(0, len(decoders), 16):
                batch = decoders[first : first + 16]
                left = []
                for j in batch:
                    keep = jnp.where(row == j, 1.0, 0.0).astype(BF16)
                    left.append(weights * keep)
                out = nn(jnp.concatenate(left, axis=0), right)
                for n, j in enumerate(batch):
                    halves = []
                    for half in range(2):
                        cols = slice(half * 128, half * 128 + 128)
                        begin = n * 32 + half * 8
                        halves.append(
                            jnp.where(
                                keep_low,
                                out[begin : begin + 8, cols],
                                out[begin + 16 : begin + 24, cols],
                            )
                        )
                    tile = jnp.concatenate(halves, axis=0).astype(BF16)
                    cs[p][block_of(p, g, j), :, pl.ds(inner, 128)] = tile

        if p == 0:

            for cc in range(tiles):
                tile_of(to, cc, list(range(32)))
        else:

            if p == 2:
                loss_set(to)

            def step(n, carry):
                if p == 1:
                    decoders = [y * 8 + to * 2 + c for y in range(4) for c in range(2)]
                else:
                    decoders = [to * 8 + x * 2 + c for x in range(4) for c in range(2)]
                for g in (2 * n, 2 * n + 1):
                    for cc in range(tiles):
                        tile_of(g, cc, decoders)
                return carry

            lax.fori_loop(0, 2, step, 0)

    def reach(p, stage, to):
        first, second, third = ORDERS[p]
        if stage == 0:
            return core * 64 + to * 16, 16
        if stage == 1:
            return core * 64 + at[third] * 16 + to * 4, 4
        return core * 64 + at[third] * 16 + at[second] * 4 + to, 1

    def set_of(p, n):
        return (at[ORDERS[p][2]] + n + 1) % 4

    def swap_copy(p, n):
        to = set_of(p, n)
        return remote(
            cs[p].at[pl.ds((1 - core) * 64 + to * 16, 16)],
            rcs[p].at[pl.ds(to * 16, 16)],
            RS + p * 13 + n,
            sibling,
        )

    def scatter_copy(p, stage, step):
        axis = ORDERS[p][2 - stage]
        begin, count = reach(p, stage, (at[axis] + step) % 4)
        return remote(
            cs[p].at[pl.ds(begin, count)],
            rstage[stage][p].at[pl.ds((step - 1) * count, count)],
            RS + p * 13 + 4 + stage * 3 + step - 1,
            peer(axis, step),
        )

    def scatter_start(p, stage):
        for step in (1, 2, 3):
            copy = scatter_copy(p, stage, step)
            copy.start()
            started.append(copy)

    def swap_finish(p, n):
        to = set_of(p, n)
        arrived(rcs[p].at[pl.ds(to * 16, 16)], RS + p * 13 + n)

        def step(four, carry):
            places = [four * 4 + n for n in range(4)]
            sums = [
                add_blocks(p, [cs[p][core * 64 + to * 16 + b], rcs[p][to * 16 + b]])[1]
                for b in places
            ]
            for b, block in zip(places, sums):
                cs[p][core * 64 + to * 16 + b] = block
            return carry

        lax.fori_loop(0, 4, step, 0)

        @pl.when(n < 3)
        def _():
            scatter_copy(p, 0, n + 1).start()

    def scatter_wait(p, stage):
        count = (16, 4, 1)[stage]
        for step in (1, 2, 3):
            arrived(
                rstage[stage][p].at[pl.ds((step - 1) * count, count)],
                RS + p * 13 + 4 + stage * 3 + step - 1,
            )

    def scatter_add(p, stage):
        axis = ORDERS[p][2 - stage]
        begin, count = reach(p, stage, at[axis])
        scatter_wait(p, stage)

        def step(four, carry):
            sums = []
            for n in range(4):
                b = four * 4 + n
                parts = [rstage[stage][p][n * count + b] for n in range(3)]
                sums.append((b, add_blocks(p, [cs[p][begin + b]] + parts)[1]))
            for b, block in sums:
                cs[p][begin + b] = block
            return carry

        lax.fori_loop(0, count // 4, step, 0)

    def scatter_set(n, carry):
        for p in range(3):
            context_set(p, set_of(p, n))
            swap_copy(p, n).start()
            if p > 0:
                swap_finish(p - 1, n)
            else:

                @pl.when(n > 0)
                def _():
                    swap_finish(2, n - 1)

        return carry

    lax.fori_loop(0, 4, scatter_set, 0)
    swap_finish(2, 3)
    for p in range(3):
        started.extend(swap_copy(p, n) for n in range(4))
        started.extend(scatter_copy(p, 0, step) for step in (1, 2, 3))

    coefficient = (LOSS_WEIGHT * E ** (-0.5)) * (jnp.exp(log_prob) - target)
    grads = jnp.where(valid, coefficient * emb, 0.0).astype(BF16)
    hot_row_t = jnp.where(iota((64, 64), 0) == row_row, 1.0, 0.0).astype(BF16)
    grad_ref[...] = nn(hot_row_t, grads)

    for p in range(3):
        scatter_add(p, 0)
        scatter_start(p, 1)
    for p in range(3):
        scatter_add(p, 1)
        scatter_start(p, 2)
    for p in range(3):
        begin, _ = reach(p, 2, at[ORDERS[p][0]])
        scatter_wait(p, 2)
        total, _ = add_blocks(p, [cs[p][begin]] + [rstage[2][p][n] for n in range(3)])
        for cc in range(2 if p == 2 else 3):
            c = 3 * p + cc
            cols = total[:, cc * 128 : cc * 128 + 128].astype(BF16)
            ctx_ref[0, :, c * 128 : c * 128 + 128] = total[0:8, cc * 128 : cc * 128 + 128].astype(BF16)
            ctx_ref[0, :, 1024 + c * 128 : 1152 + c * 128] = total[
                8:16, cc * 128 : cc * 128 + 128
            ].astype(BF16)
        if p == 2:
            loss_ref[...] = total[0:8, 256:384] + total[8:16, 256:384]

    for copy in started:
        copy.wait_send()


def hand_over(ctx_ref, loss_ref, grad_ref, ctx_out, loss_out, grad_out):
    ctx_out[...] = ctx_ref[...]
    loss_out[0] = loss_ref[0, 0]
    grad_out[...] = grad_ref[...]


def body(
    store_states,
    store_keys,
    passage_ids,
    store_slot,
    row_question,
    queries,
    question_emb,
    enc_gain,
    key_weight,
    value_weight,
):
    vmem = pl.BlockSpec(memory_space=pltpu.VMEM)
    anywhere = pl.BlockSpec(memory_space=pl.ANY)
    scratch = [
        pltpu.VMEM((64, 8, D), BF16),
        pltpu.VMEM((D, 2 * D), BF16),
        pltpu.VMEM((512, D), BF16),
        pltpu.VMEM((512, 512), BF16),
        pltpu.VMEM((512, D), BF16),
        pltpu.VMEM((512, 2 * D), BF16),
        pltpu.VMEM((D, 512), BF16),
    ]
    scratch += [pltpu.VMEM((128, 16, 384), BF16)] * 6
    scratch += [pltpu.VMEM((64, 16, 384), BF16)] * 3
    scratch += [pltpu.VMEM((48, 16, 384), BF16)] * 3
    scratch += [pltpu.VMEM((12, 16, 384), BF16)] * 3
    scratch += [pltpu.VMEM((3, 16, 384), BF16)] * 3
    scratch += [pltpu.VMEM((4, 256, 128), F32), pltpu.VMEM((4, 256, 128), BF16)]
    sizes = (64, 64, 16)
    scratch += [pltpu.VMEM((2 * n, 128), F32) for n in sizes]
    scratch += [pltpu.VMEM((n, 128), F32) for n in sizes]
    scratch += [pltpu.VMEM((9, n, 128), F32) for n in sizes]
    scratch += [pltpu.VMEM((3, n, 128), F32) for n in sizes]
    scratch += [pltpu.VMEM((2 * n, 128), F32) for n in sizes]
    scratch += [
        pltpu.VMEM((4, 32, 128), jnp.int32),
        pltpu.VMEM((8, 128), jnp.int32),
        pltpu.VMEM((8, 128), jnp.int32),
        pltpu.VMEM((16, 128), jnp.int32),
        pltpu.SMEM((16, 128), jnp.int32),
        pltpu.VMEM((128, 128), F32),
        pltpu.SemaphoreType.DMA((SEMS,)),
        pltpu.SemaphoreType.DMA((SEMS,)),
        pltpu.SemaphoreType.DMA((10,)),
    ]
    context, loss, grad = pl.pallas_call(
        kernel,
        out_shape=(
            jax.ShapeDtypeStruct((1, 8, D), BF16),
            jax.ShapeDtypeStruct((8, 128), F32),
            jax.ShapeDtypeStruct((STORE, E), F32),
        ),
        in_specs=[
            vmem,
            vmem,
            vmem,
            anywhere,
            vmem,
            vmem,
            vmem,
            vmem,
            anywhere,
            anywhere,
        ],
        out_specs=(vmem, vmem, vmem),
        scratch_shapes=scratch,
        compiler_params=pltpu.CompilerParams(
            collective_id=0, has_side_effects=True, vmem_limit_bytes=60 * 1024 * 1024
        ),
        cost_estimate=pl.CostEstimate(
            flops=12 * 10**9, bytes_accessed=20 * 10**6, transcendentals=10**6
        ),
    )(
        passage_ids.T,
        store_slot.reshape(64, 128),
        row_question,
        store_states,
        store_keys,
        queries,
        question_emb,
        enc_gain.reshape(1, D),
        key_weight,
        value_weight,
    )
    return pl.pallas_call(
        hand_over,
        out_shape=(
            jax.ShapeDtypeStruct((1, 8, D), BF16),
            jax.ShapeDtypeStruct((1,), F32),
            jax.ShapeDtypeStruct((STORE, E), F32),
        ),
        in_specs=[vmem, vmem, vmem],
        out_specs=(vmem, pl.BlockSpec(memory_space=pltpu.SMEM), vmem),
    )(context, loss, grad)


def solution(mesh):
    in_specs = (
        P(("group", "dev"), None, None),
        P(("group", "dev"), None),
        P(),
        P(),
        P("group", None),
        P(("group", "dev"), None, None),
        P(("group", "dev"), None),
        P(),
        P(),
        P(),
    )
    out_specs = (P(("group", "dev"), None, None), P(("group", "dev")), P(("group", "dev"), None))
    return jax.shard_map(body, mesh=mesh, in_specs=in_specs, out_specs=out_specs, check_vma=False)
```

```python
import functools

import jax
import jax.numpy as jnp
from jax import lax
from jax.experimental import pallas as pl
from jax.experimental.pallas import tpu as pltpu
from jax.sharding import PartitionSpec as P

MESH = pl.DeviceIdType.MESH
F32 = jnp.float32
BF16 = jnp.bfloat16
HIGHEST = lax.Precision.HIGHEST

D = 2048
E = 768
GROUPS = 4
PER_GROUP = 32
SLOTS = 16
LANES = 128
STORE = 64
EPS = 1e-06
LOSS_WEIGHT = 256.0
ABSENT = -1e30

ORDERS = (("x", "y", "z"), ("y", "z", "x"), ("z", "x", "y"))
AG, AG_SIB, RQ, SWAP, AR, FIN, RS, LOSS = 0, 27, 39, 42, 44, 71, 74, 113
SEMS = 126


def nt(a, b, precision=None):
    return lax.dot_general(
        a, b, (((1,), (1,)), ((), ())), preferred_element_type=F32, precision=precision
    )


def nn(a, b, precision=None):
    return jnp.dot(a, b, preferred_element_type=F32, precision=precision)


def iota(shape, dim):
    return lax.broadcasted_iota(jnp.int32, shape, dim)


def block_of(part, g, j):
    y, x, core = j // 8, (j // 2) % 4, j % 2
    at = {"x": x, "y": y, "z": g}
    first, second, third = ORDERS[part]
    return core * 64 + at[third] * 16 + at[second] * 4 + at[first]


def log_add(values):
    top = values[0]
    for value in values[1:]:
        top = jnp.maximum(top, value)
    total = jnp.exp(values[0] - top)
    for value in values[1:]:
        total = total + jnp.exp(value - top)
    return top + jnp.log(total)


def kernel(
    ids_ref,
    slot_ref,
    rq_ref,
    states_ref,
    keys_ref,
    queries_ref,
    emb_ref,
    gain_ref,
    kw_ref,
    vw_ref,
    ctx_ref,
    loss_ref,
    grad_ref,
    st,
    w,
    stored,
    pick,
    nrm,
    kv,
    keys_t,
    q0,
    q1,
    q2,
    c0,
    c1,
    c2,
    rc0,
    rc1,
    rc2,
    ra0,
    ra1,
    ra2,
    rb0,
    rb1,
    rb2,
    rd0,
    rd1,
    rd2,
    s_buf,
    p_buf,
    t_ref,
    o_ref,
    accs,
    ars,
    fin,
    e_ref,
    e_in,
    rqt,
    lane_ref,
    ir_ref,
    lam_ref,
    block_ref,
    block_smem,
    send_sem,
    recv_sem,
    local_sem,
):
    qs, cs, rcs = (q0, q1, q2), (c0, c1, c2), (rc0, rc1, rc2)
    rstage = ((ra0, ra1, ra2), (rb0, rb1, rb2), (rd0, rd1, rd2))
    my_group = lax.axis_index("group")
    my_dev = lax.axis_index("dev")
    core = my_dev % 2
    at = {"x": (my_dev // 2) % 4, "y": my_dev // 8, "z": my_group}
    sibling = (my_group, my_dev + 1 - 2 * core)

    def peer(axis, step):
        to = (at[axis] + step) % 4
        if axis == "z":
            return (to, my_dev)
        if axis == "y":
            return (my_group, to * 8 + at["x"] * 2 + core)
        return (my_group, at["y"] * 8 + to * 2 + core)

    started = []

    def remote(src, dst, number, device):
        copy = pltpu.make_async_remote_copy(
            src_ref=src,
            dst_ref=dst,
            send_sem=send_sem.at[number],
            recv_sem=recv_sem.at[number],
            device_id=device,
            device_id_type=MESH,
        )
        return copy

    def start(src, dst, number, device):
        copy = remote(src, dst, number, device)
        copy.start()
        started.append(copy)

    def arrived(dst, number):
        remote(dst, dst, number, sibling).wait_recv()

    def cross(step):
        return (my_group, at["y"] * 8 + (at["x"] + step) % 4 * 2 + 1 - core)

    barrier = pltpu.get_barrier_semaphore()
    pl.semaphore_signal(barrier, inc=1, device_id=sibling, device_id_type=MESH)
    for step in (1, 2, 3):
        for axis in ("x", "y", "z"):
            pl.semaphore_signal(barrier, inc=1, device_id=peer(axis, step), device_id_type=MESH)
        pl.semaphore_signal(barrier, inc=1, device_id=cross(step), device_id_type=MESH)

    states_copy = pltpu.make_async_copy(states_ref, st, local_sem.at[8])
    states_copy.start()
    w_copies = []
    for n in range(8):
        src = kw_ref if n < 4 else vw_ref
        copy = pltpu.make_async_copy(
            src.at[:, pl.ds((n % 4) * 512, 512)],
            w.at[:, pl.ds(n * 512, 512)],
            local_sem.at[n],
        )
        copy.start()
        w_copies.append(copy)

    mine = [
        core * 64 + at[ORDERS[p][2]] * 16 + at[ORDERS[p][1]] * 4 + at[ORDERS[p][0]]
        for p in range(3)
    ]
    for c in range(8):
        tile = jnp.concatenate(
            [
                queries_ref[0, :, c * 128 : c * 128 + 128].astype(F32),
                queries_ref[0, :, 1024 + c * 128 : 1152 + c * 128].astype(F32),
            ],
            axis=0,
        )
        qs[c // 3][mine[c // 3], :, (c % 3) * 128 : (c % 3) * 128 + 128] = tile.astype(BF16)
    emb_rows = [emb_ref[:, c * 128 : c * 128 + 128].astype(F32) for c in range(6)]
    emb_tile = jnp.concatenate(emb_rows + [jnp.zeros((10, 128), F32)], axis=0)
    q2[mine[2], :, 256:384] = emb_tile.astype(BF16)
    diagonal = iota((32, 32), 0) == iota((32, 32), 1)
    rq_col = jnp.sum(jnp.where(diagonal, rq_ref[...], 0), axis=1, keepdims=True)
    rqt[my_group] = jnp.broadcast_to(rq_col, (32, 128))

    pl.semaphore_wait(barrier, 13)

    def span(p, stage, back):
        first, second, third = ORDERS[p]
        digit = (at[ORDERS[p][stage]] + 4 - back) % 4
        if stage == 0:
            return core * 64 + at[third] * 16 + at[second] * 4 + digit, 1
        if stage == 1:
            return core * 64 + at[third] * 16 + digit * 4, 4
        return core * 64 + digit * 16, 16

    def gather_start(stage):
        for p in range(3):
            begin, size = span(p, stage, 0)
            for step in (1, 2, 3):
                ref = qs[p].at[pl.ds(begin, size)]
                start(ref, ref, AG + (p * 3 + stage) * 3 + step - 1, peer(ORDERS[p][stage], step))

    def gather_wait(p, stage, step):
        begin, size = span(p, stage, step)
        arrived(qs[p].at[pl.ds(begin, size)], AG + (p * 3 + stage) * 3 + step - 1)

    def forward(p, back):
        begin, size = span(p, 2, back)
        ref = qs[p].at[pl.ds(begin, size)]
        start(ref, ref, AG_SIB + p * 4 + back, sibling)

    gather_start(0)
    for step in (1, 2, 3):
        start(rqt.at[my_group], rqt.at[my_group], RQ + step - 1, peer("z", step))

    lane = iota((1, 128), 1)
    sub = iota((128, 128), 0)
    lanes = iota((128, 128), 1)
    first_row = (my_group * PER_GROUP + my_dev) * STORE
    local = slot_ref[...] - first_row
    local = jnp.where((local >= 0) & (local < STORE), local + 1, 0).astype(F32)
    local_t = jnp.transpose(local).astype(BF16)
    ids_high = ids_ref[...] // 128
    ids_low = ids_ref[...] % 128
    high_sub = iota((64, 128), 0)
    lane32 = iota((128, 32), 1)
    held_rows = []
    for k in range(32):
        hot = jnp.where(high_sub == ids_high[k : k + 1, :], 1.0, 0.0).astype(BF16)
        found = jnp.where(sub == ids_low[k : k + 1, :], nn(local_t, hot), 0.0)
        held_rows.append(jnp.sum(found, axis=0, keepdims=True))
    held = jnp.transpose(jnp.concatenate(held_rows, axis=0))
    for p in range(3):
        for step in (1, 2, 3):
            gather_wait(p, 0, step)
    gather_start(1)

    held_int = held.astype(jnp.int32)
    mine_f = jnp.where(held_int > 0, 1.0, 0.0)
    mine_b = mine_f.astype(BF16)
    in_row = nn(mine_b, jnp.ones((32, 32), BF16))
    above = jnp.where((sub // 32 == lanes // 32) & (lanes < sub), 1.0, 0.0).astype(BF16)
    upto = jnp.where(iota((32, 32), 0) <= iota((32, 32), 1), 1.0, 0.0).astype(BF16)
    rank = nn(above, in_row.astype(BF16)) + nn(mine_b, upto)
    rank = jnp.where(held_int > 0, rank.astype(jnp.int32), 0)
    code = (iota((128, 32), 0) % 32) * 4096 + lane32 * 128 + held_int
    spread = jnp.zeros((128, 128), jnp.int32)
    for n in range(SLOTS):
        here = jnp.sum(jnp.where(rank == n + 1, code, 0), axis=1, keepdims=True)
        spread = jnp.where(lanes // 8 == n, here, spread)
    code_cols = []
    slot16 = iota((16, 128), 1) == iota((16, 128), 0) * 8
    for g in range(4):
        code_row = jnp.sum(spread[g * 32 : g * 32 + 32], axis=0, keepdims=True)
        lane_ref[g : g + 1, :] = jnp.where(code_row > 0, code_row // 4096, -1)
        code_cols.append(jnp.sum(jnp.where(slot16, code_row, 0), axis=1, keepdims=True))
        long_col = jnp.sum(jnp.where(sub == lanes, code_row, 0), axis=1, keepdims=True)
        token = jnp.where(
            long_col > 0, (long_col % 128 - 1) * 8 + iota((128, 1), 0) % 8, 512
        )
        pick[g * 128 : g * 128 + 128, :] = jnp.where(
            iota((128, 512), 1) == token, 1.0, 0.0
        ).astype(BF16)
    code_col = jnp.concatenate(code_cols, axis=0)
    valid = code_col > 0
    k_col = (code_col // 128) % 32
    row_col = code_col % 128 - 1
    square = iota((64, 64), 0) == iota((64, 64), 1)
    code_row64 = jnp.sum(jnp.where(square, code_col, 0), axis=0, keepdims=True)
    k_row = (code_row64 // 128) % 32
    row_row = code_row64 % 128 - 1

    for p in range(3):
        for step in (1, 2, 3):
            gather_wait(p, 1, step)
    gather_start(2)
    for p in range(3):
        forward(p, 0)

    for step in (1, 2, 3):
        arrived(rqt.at[(my_group + 4 - step) % 4], RQ + step - 1)
    for g in range(4):
        match = rqt[g] == lane_ref[g : g + 1, :]
        row = jnp.sum(jnp.where(match, iota((32, 128), 0) + (g * 32 + 1), 0), axis=0, keepdims=True)
        ir_ref[g : g + 1, :] = row - 1
    decoder_of = jnp.maximum(ir_ref[0:4, :], 0)
    for p in range(3):
        block_ref[p * 4 : p * 4 + 4, :] = block_of(p, decoder_of // 32, decoder_of % 32)
    lam_ref[0:4, :] = jnp.where(ir_ref[0:4, :] >= 0, block_ref[0:4, :], -1)
    block_copy = pltpu.make_async_copy(block_ref, block_smem, local_sem.at[9])
    block_copy.start()

    states_copy.wait()

    def norm_pair(pair, carry):
        both = []
        for half in range(2):
            values = st[pair * 2 + half].astype(F32)
            mean_square = jnp.mean(values * values, axis=-1, keepdims=True)
            both.append(values * lax.rsqrt(mean_square + EPS) * gain_ref[...])
        rows = pl.ds(pl.multiple_of(pair * 16, 16), 16)
        stored[rows, :] = jnp.concatenate(both, axis=0).astype(BF16)
        return carry

    lax.fori_loop(0, 32, norm_pair, 0)

    def pick_step(n, carry):
        cols = pl.ds(pl.multiple_of(n * 256, 256), 256)
        nrm[:, cols] = nn(pick[...], stored[:, cols]).astype(BF16)
        return carry

    lax.fori_loop(0, 8, pick_step, 0)

    def project(begin, end):
        def step(n, carry):
            offset = pl.multiple_of(n * 256, 256)
            kv[:, pl.ds(offset, 256)] = nn(nrm[...], w[:, pl.ds(offset, 256)]).astype(BF16)
            return carry

        for n in range(begin, end):
            w_copies[n].wait()
        lax.fori_loop(begin * 2, end * 2, step, 0)

    project(0, 4)
    for step in (1, 3, 2):
        for p in range(3):
            gather_wait(p, 2, step)
            forward(p, step)
    def turn(n, carry):
        rows = pl.ds(pl.multiple_of(n * 256, 256), 256)
        keys_t[rows, :] = jnp.transpose(kv[:, rows].astype(F32)).astype(BF16)
        return carry

    lax.fori_loop(0, 8, turn, 0)
    project(4, 7)
    block_copy.wait()

    for p in range(3):
        for back in range(4):
            first, second, third = ORDERS[p]
            begin = (1 - core) * 64 + ((at[third] + 4 - back) % 4) * 16
            arrived(qs[p].at[pl.ds(begin, 16)], AG_SIB + p * 4 + back)

    low = (lane < 64).astype(F32).astype(BF16)
    high = (lane >= 64).astype(F32).astype(BF16)

    def scores_of(p, tiles):
        def step(cc, carry):
            inner = pl.multiple_of(cc * 128, 128)
            outer = pl.multiple_of((3 * p + cc) * 128, 128)
            rows = pl.ds(pl.multiple_of((3 * p + cc) * 16, 16), 16)
            high_rows = pl.ds(pl.multiple_of((3 * p + cc) * 16 + 128, 16), 16)
            for g in range(4):
                slots = slice(g * 128, g * 128 + 128)
                right = jnp.concatenate(
                    [keys_t[pl.ds(outer, 128), slots], keys_t[pl.ds(outer + 1024, 128), slots]],
                    axis=1,
                )
                left = []
                for r in range(SLOTS):
                    block = qs[p][block_smem[p * 4 + g, r * 8], :, pl.ds(inner, 128)]
                    left += [block * low, block * high]
                out = nn(jnp.concatenate(left, axis=0), right)
                total = [jnp.zeros((8, 128), F32) for _ in range(4)]
                for r in range(SLOTS):
                    keep = jnp.broadcast_to(lane // 8 == r, (8, 128))
                    for tile in range(4):
                        half = tile % 2
                        begin = r * 32 + tile * 8
                        piece = out[begin : begin + 8, half * 128 : half * 128 + 128]
                        total[tile] = jnp.where(keep, piece, total[tile])
                s_buf[g, rows, :] = jnp.concatenate(total[0:2], axis=0) * (64 ** (-0.5))
                s_buf[g, high_rows, :] = jnp.concatenate(total[2:4], axis=0) * (64 ** (-0.5))
            return carry

        lax.fori_loop(0, tiles, step, 0)

    scores_of(0, 3)
    scores_of(1, 3)
    scores_of(2, 2)

    peak_i = jnp.zeros((256, 128), F32)
    total_i = jnp.zeros((256, 128), F32)
    present = jnp.zeros((8, 128), F32)
    for g in range(4):
        scores = s_buf[g]
        u_row = lane_ref[g : g + 1, :]
        peak = scores
        for s in (1, 2, 4):
            bit = jnp.broadcast_to((lane // s) % 2 == 1, (256, 128))
            other = jnp.where(bit, pltpu.roll(peak, s, 1), pltpu.roll(peak, 128 - s, 1))
            peak = jnp.maximum(peak, other)
        u_rows = jnp.broadcast_to(u_row, (8, 128))
        before = pltpu.roll(u_rows, 8, 1)[0:1, :]
        for s in (8, 16, 32, 64):
            same = (pltpu.roll(u_rows, s, 1)[0:1, :] == u_row) & (lane >= s)
            other = jnp.where(jnp.broadcast_to(same, (256, 128)), pltpu.roll(peak, s, 1), ABSENT)
            peak = jnp.maximum(peak, other)
        for s in (8, 16, 32, 64):
            same = (pltpu.roll(u_rows, 128 - s, 1)[0:1, :] == u_row) & (lane < 128 - s)
            other = jnp.where(
                jnp.broadcast_to(same, (256, 128)), pltpu.roll(peak, 128 - s, 1), ABSENT
            )
            peak = jnp.maximum(peak, other)
        chosen = sub == lam_ref[g : g + 1, :]
        first = ((before != u_row) | (lane < 8)) & (lane % 8 == 0)
        lead = jnp.where(chosen & jnp.broadcast_to(first, (128, 128)), 1.0, 0.0)
        peak_i = peak_i + nt(peak, lead, HIGHEST)
        total_i = total_i + nt(jnp.exp(scores - peak), jnp.where(chosen, 1.0, 0.0), HIGHEST)
        present = present + nt(jnp.ones((8, 128), F32), lead)
    table = jnp.where(
        jnp.broadcast_to(present[0:1, :] > 0.5, (256, 128)),
        peak_i + jnp.log(jnp.maximum(total_i, 1e-30)),
        ABSENT,
    )
    t_ref[0:256, :] = table
    start(t_ref.at[pl.ds(0, 256)], o_ref.at[pl.ds(0, 256)], SWAP, sibling)

    lane64 = iota((64, 128), 1)
    i_cols, lam_cols = [], []
    for g in range(4):
        picked = jnp.where(slot16, ir_ref[g : g + 1, :] + 1, 0)
        i_cols.append(jnp.sum(picked, axis=1, keepdims=True))
        picked = jnp.where(slot16, lam_ref[g : g + 1, :] + 1, 0)
        lam_cols.append(jnp.sum(picked, axis=1, keepdims=True))
    i_col = jnp.concatenate(i_cols, axis=0) - 1
    one_hot_i = lane64 == jnp.concatenate(lam_cols, axis=0) - 1
    hot_i = jnp.where(one_hot_i, 1.0, 0.0)
    decoder = jnp.maximum(i_col, 0)
    place = block_of(2, decoder // 32, decoder % 32) * 16
    flat = q2[:, :, 256:384].reshape(2048, 128)
    wide = iota((64, 2048), 1)
    emb = jnp.concatenate(
        [nn(jnp.where(wide == place + c, 1.0, 0.0).astype(BF16), flat) for c in range(6)], axis=1
    )
    hot_row = jnp.where(iota((64, 64), 1) == row_col, 1.0, 0.0).astype(BF16)
    keys = nn(hot_row, keys_ref[...])
    retrieval = jnp.sum(emb * keys, axis=1, keepdims=True) * (E ** (-0.5))
    retrieval_row = jnp.sum(jnp.where(square, retrieval, 0.0), axis=0, keepdims=True)
    by_k = jnp.where(iota((32, 64), 0) == k_row, retrieval_row, 0.0)
    t_ref[256:288, :] = nn(by_k, hot_i, HIGHEST)
    start(t_ref.at[pl.ds(256, 32)], o_ref.at[pl.ds(256, 32)], SWAP + 1, sibling)
    project(7, 8)

    low_lanes = lane < 64

    def pack(first, second, of):
        zero = jnp.where(low_lanes, first, pltpu.roll(second, 64, 1))
        one = jnp.where(low_lanes, pltpu.roll(first, 64, 1), second)
        return jnp.where(of == 0, zero, one)

    arrived(o_ref.at[pl.ds(0, 256)], SWAP)
    arrived(o_ref.at[pl.ds(256, 32)], SWAP + 1)
    pair = log_add([t_ref[0:256, :], o_ref[0:256, :]])
    pair_raw = t_ref[256:288, :] + o_ref[256:288, :]
    packed = pack(pair[0:128], pair[128:256], core)
    accs[0, 0] = packed[0:48]
    accs[1, 0] = packed[48:96]
    accs[2, 0] = jnp.concatenate([packed[96:128], pack(pair_raw[0:16], pair_raw[16:32], core)], axis=0)

    def table_copy(p, stage, step):
        return remote(
            accs.at[p, stage],
            ars.at[p, stage * 3 + step - 1],
            AR + p * 9 + stage * 3 + step - 1,
            peer(ORDERS[p][2 - stage], step),
        )

    def table_start(stage):
        for p in range(3):
            for step in (1, 2, 3):
                table_copy(p, stage, step).start()

    def table_finish(stage):
        for p in range(3):
            values = [accs[p, stage]]
            for step in (1, 2, 3):
                arrived(ars.at[p, stage * 3 + step - 1], AR + p * 9 + stage * 3 + step - 1)
                values.append(ars[p, stage * 3 + step - 1])
            if p < 2:
                accs[p, stage + 1] = log_add(values)
            else:
                raw = values[0][32:48] + values[1][32:48] + values[2][32:48] + values[3][32:48]
                total = log_add([value[0:32] for value in values])
                accs[p, stage + 1] = jnp.concatenate([total, raw], axis=0)

    table_start(0)
    while started:
        started.pop(0).wait_send()

    for g in range(4):
        chosen = jnp.where(sub == lam_ref[g : g + 1, :], 1.0, 0.0)
        p_buf[g] = jnp.exp(s_buf[g] - nn(pair, chosen, HIGHEST)).astype(BF16)

    keep_low = jnp.broadcast_to(lane < 64, (8, 128))

    def context_set(p, to):
        tiles = 2 if p == 2 else 3

        def tile_of(g, cc, decoders):
            inner = cc * 128
            outer = D + (3 * p + cc) * 128
            slots = pl.ds(pl.multiple_of(g * 128, 128), 128)
            right = jnp.concatenate(
                [kv[slots, pl.ds(outer, 128)], kv[slots, pl.ds(outer + 1024, 128)]], axis=1
            )
            row = ir_ref[pl.ds(g, 1), :] - g * 32
            c = 3 * p + cc
            weights = jnp.concatenate(
                [p_buf[g, pl.ds(c * 16, 16), :], p_buf[g, pl.ds(128 + c * 16, 16), :]], axis=0
            )
            for first in range(0, len(decoders), 16):
                batch = decoders[first : first + 16]
                left = []
                for j in batch:
                    keep = jnp.where(row == j, 1.0, 0.0).astype(BF16)
                    left.append(weights * keep)
                out = nn(jnp.concatenate(left, axis=0), right)
                for n, j in enumerate(batch):
                    halves = []
                    for half in range(2):
                        cols = slice(half * 128, half * 128 + 128)
                        begin = n * 32 + half * 8
                        halves.append(
                            jnp.where(
                                keep_low,
                                out[begin : begin + 8, cols],
                                out[begin + 16 : begin + 24, cols],
                            )
                        )
                    tile = jnp.concatenate(halves, axis=0).astype(BF16)
                    cs[p][block_of(p, g, j), :, pl.ds(inner, 128)] = tile

        if p == 0:

            for cc in range(tiles):
                tile_of(to, cc, list(range(32)))
        else:

            def step(n, carry):
                if p == 1:
                    decoders = [y * 8 + to * 2 + c for y in range(4) for c in range(2)]
                else:
                    decoders = [to * 8 + x * 2 + c for x in range(4) for c in range(2)]
                for g in (2 * n, 2 * n + 1):
                    for cc in range(tiles):
                        tile_of(g, cc, decoders)
                return carry

            lax.fori_loop(0, 2, step, 0)

    def reach(p, stage, to):
        first, second, third = ORDERS[p]
        if stage == 0:
            return core * 64 + to * 16, 16
        if stage == 1:
            return core * 64 + at[third] * 16 + to * 4, 4
        return core * 64 + at[third] * 16 + at[second] * 4 + to, 1

    def set_of(p, n):
        return (at[ORDERS[p][2]] + n + 1) % 4

    def swap_copy(p, n):
        to = set_of(p, n)
        return remote(
            cs[p].at[pl.ds((1 - core) * 64 + to * 16, 16)],
            rcs[p].at[pl.ds(to * 16, 16)],
            RS + p * 13 + n,
            sibling,
        )

    def scatter_copy(p, stage, step):
        axis = ORDERS[p][2 - stage]
        begin, count = reach(p, stage, (at[axis] + step) % 4)
        return remote(
            cs[p].at[pl.ds(begin, count)],
            rstage[stage][p].at[pl.ds((step - 1) * count, count)],
            RS + p * 13 + 4 + stage * 3 + step - 1,
            peer(axis, step),
        )

    def scatter_start(p, stage):
        for step in (1, 2, 3):
            copy = scatter_copy(p, stage, step)
            copy.start()
            started.append(copy)

    def swap_finish(p, n):
        to = set_of(p, n)
        arrived(rcs[p].at[pl.ds(to * 16, 16)], RS + p * 13 + n)

        def step(four, carry):
            places = [four * 4 + n for n in range(4)]
            sums = [
                (
                    cs[p][core * 64 + to * 16 + b].astype(F32) + rcs[p][to * 16 + b].astype(F32)
                ).astype(BF16)
                for b in places
            ]
            for b, block in zip(places, sums):
                cs[p][core * 64 + to * 16 + b] = block
            return carry

        lax.fori_loop(0, 4, step, 0)

        @pl.when(n < 3)
        def _():
            scatter_copy(p, 0, n + 1).start()

    def scatter_wait(p, stage):
        count = (16, 4, 1)[stage]
        for step in (1, 2, 3):
            arrived(
                rstage[stage][p].at[pl.ds((step - 1) * count, count)],
                RS + p * 13 + 4 + stage * 3 + step - 1,
            )

    def scatter_sum(p, stage):
        axis = ORDERS[p][2 - stage]
        tiles = 2 if p == 2 else 3
        begin, count = reach(p, stage, at[axis])
        scatter_wait(p, stage)
        after = accs[p, stage + 1][0 : tiles * 16]
        tables = [accs[p, stage]] + [ars[p, stage * 3 + n] for n in range(3)]
        wide_lane = iota((1, count * 128), 1)
        place_of = begin - core * 64 + wide_lane // 128
        digits = {
            ORDERS[p][2]: place_of // 16,
            ORDERS[p][1]: (place_of // 4) % 4,
            ORDERS[p][0]: place_of % 4,
        }
        packed_lane = (wide_lane % 128) // 64 * 64 + digits["z"] * 16 + digits["y"] * 4 + digits["x"]
        spread_hot = jnp.where(iota((128, count * 128), 0) == packed_lane, 1.0, 0.0).astype(BF16)
        factors = [
            nn(jnp.exp(table[0 : tiles * 16] - after).astype(BF16), spread_hot) for table in tables
        ]
        sums = []
        for b in range(count):
            blocks = [cs[p][begin + b]] + [rstage[stage][p][n * count + b] for n in range(3)]
            cols = []
            for cc in range(tiles):
                total = jnp.zeros((16, 128), F32)
                for block, factor in zip(blocks, factors):
                    part = factor[cc * 16 : cc * 16 + 16, b * 128 : b * 128 + 128]
                    total = total + block[:, cc * 128 : cc * 128 + 128].astype(F32) * part
                cols.append(total)
            sums.append(cols)
        return begin, sums

    def scatter_add(p, stage):
        begin, sums = scatter_sum(p, stage)
        for b, cols in enumerate(sums):
            cs[p][begin + b] = jnp.concatenate(cols, axis=1).astype(BF16)

    def final_copy(p):
        return remote(accs.at[p, 3], fin.at[p], FIN + p, sibling)

    def scatter_set(n, carry):
        for p in range(3):
            context_set(p, set_of(p, n))
            swap_copy(p, n).start()
            if p > 0:
                swap_finish(p - 1, n)
            else:

                @pl.when(n > 0)
                def _():
                    swap_finish(2, n - 1)

        for stage in range(3):

            @pl.when(n == stage)
            def _(stage=stage):
                table_finish(stage)
                if stage < 2:
                    table_start(stage + 1)
                else:
                    for p in range(3):
                        final_copy(p).start()

        return carry

    lax.fori_loop(0, 4, scatter_set, 0)
    swap_finish(2, 3)
    for p in range(3):
        started.extend(swap_copy(p, n) for n in range(4))
        started.extend(scatter_copy(p, 0, step) for step in (1, 2, 3))

    for p in range(3):
        started.extend(table_copy(p, stage, step) for stage in range(3) for step in (1, 2, 3))
        started.append(final_copy(p))

    for p in range(3):
        arrived(fin.at[p], FIN + p)
    own_sum = jnp.concatenate([accs[0, 3], accs[1, 3], accs[2, 3]], axis=0)
    other_sum = jnp.concatenate([fin[0], fin[1], fin[2]], axis=0)
    zero_sum = jnp.where(core == 0, own_sum, other_sum)
    one_sum = jnp.where(core == 0, other_sum, own_sum)
    first_half = jnp.where(low_lanes, zero_sum, pltpu.roll(one_sum, 64, 1))
    second_half = jnp.where(low_lanes, pltpu.roll(zero_sum, 64, 1), one_sum)
    log_sum = jnp.concatenate([first_half[0:128], second_half[0:128]], axis=0)
    raw = jnp.concatenate([first_half[128:144], second_half[128:144]], axis=0)
    targets = []
    for g in range(4):
        chosen = jnp.where(sub == lam_ref[g : g + 1, :], 1.0, 0.0)
        mass = jnp.exp(s_buf[g] - nn(log_sum, chosen, HIGHEST))
        mass = jnp.sum(mass, axis=0, keepdims=True)
        own = iota((16, 128), 1) // 8 == iota((16, 128), 0)
        targets.append(jnp.sum(jnp.where(own, mass, 0.0), axis=1, keepdims=True))
    target = jnp.concatenate(targets, axis=0) * (1.0 / 256.0)
    top = jnp.max(raw, axis=0, keepdims=True)
    log_prob_all = raw - top - jnp.log(jnp.sum(jnp.exp(raw - top), axis=0, keepdims=True))
    hot_k = jnp.where(iota((64, 32), 1) == k_col, 1.0, 0.0)
    log_prob = jnp.sum(
        jnp.where(one_hot_i, nn(hot_k, log_prob_all, HIGHEST), 0.0), axis=1, keepdims=True
    )
    term = jnp.where(valid, target * (jnp.log(target) - log_prob), 0.0)
    loss_row = jnp.sum(jnp.where(one_hot_i, term, 0.0), axis=0, keepdims=True)

    def loss_start(stage):
        if stage == 0:
            start(e_ref.at[0], e_in.at[0], LOSS, sibling)
            for step in (1, 2, 3):
                start(e_ref.at[0], e_in.at[step], LOSS + step, peer("x", step))
                start(e_ref.at[0], e_in.at[3 + step], LOSS + 3 + step, cross(step))
        else:
            for step in (1, 2, 3):
                n = 3 + stage * 3 + step
                start(e_ref.at[stage], e_in.at[n], LOSS + n, peer("xyz"[stage], step))

    def loss_sum(stage):
        total = e_ref[stage]
        for n in range(7) if stage == 0 else range(4 + stage * 3, 7 + stage * 3):
            arrived(e_in.at[n], LOSS + n)
            total = total + e_in[n]
        return total

    e_ref[0] = jnp.broadcast_to(loss_row, (8, 128))
    loss_start(0)
    for p in range(3):
        scatter_add(p, 0)
        scatter_start(p, 1)
    e_ref[1] = loss_sum(0)
    loss_start(1)

    coefficient = (LOSS_WEIGHT * E ** (-0.5)) * (jnp.exp(log_prob) - target)
    grads = jnp.where(valid, coefficient * emb, 0.0).astype(BF16)
    hot_row_t = jnp.where(iota((64, 64), 0) == row_row, 1.0, 0.0).astype(BF16)
    grad_ref[...] = nn(hot_row_t, grads)

    for p in range(3):
        scatter_add(p, 1)
        scatter_start(p, 2)
    e_ref[2] = loss_sum(1)
    loss_start(2)
    for p in range(3):
        _, sums = scatter_sum(p, 2)
        for cc, total in enumerate(sums[0]):
            c = 3 * p + cc
            ctx_ref[0, :, c * 128 : c * 128 + 128] = total[0:8].astype(BF16)
            ctx_ref[0, :, 1024 + c * 128 : 1152 + c * 128] = total[8:16].astype(BF16)
    loss_all = jnp.sum(jnp.where(lane == mine[0], loss_sum(2)[0:1, :], 0.0), axis=1, keepdims=True)
    loss_ref[...] = jnp.broadcast_to(loss_all, (8, 128))

    for copy in started:
        copy.wait_send()


def hand_over(ctx_ref, loss_ref, grad_ref, ctx_out, loss_out, grad_out):
    ctx_out[...] = ctx_ref[...]
    loss_out[0] = loss_ref[0, 0]
    grad_out[...] = grad_ref[...]


def body(
    store_states,
    store_keys,
    passage_ids,
    store_slot,
    row_question,
    queries,
    question_emb,
    enc_gain,
    key_weight,
    value_weight,
):
    vmem = pl.BlockSpec(memory_space=pltpu.VMEM)
    anywhere = pl.BlockSpec(memory_space=pl.ANY)
    scratch = [
        pltpu.VMEM((64, 8, D), BF16),
        pltpu.VMEM((D, 2 * D), BF16),
        pltpu.VMEM((512, D), BF16),
        pltpu.VMEM((512, 512), BF16),
        pltpu.VMEM((512, D), BF16),
        pltpu.VMEM((512, 2 * D), BF16),
        pltpu.VMEM((D, 512), BF16),
    ]
    scratch += [pltpu.VMEM((128, 16, 384), BF16)] * 3
    for blocks in (128, 64, 48, 12, 3):
        scratch += [pltpu.VMEM((blocks, 16, lanes), BF16) for lanes in (384, 384, 256)]
    scratch += [pltpu.VMEM((4, 256, 128), F32), pltpu.VMEM((4, 256, 128), BF16)]
    scratch += [
        pltpu.VMEM((288, 128), F32),
        pltpu.VMEM((288, 128), F32),
        pltpu.VMEM((3, 4, 48, 128), F32),
        pltpu.VMEM((3, 9, 48, 128), F32),
        pltpu.VMEM((3, 48, 128), F32),
        pltpu.VMEM((3, 8, 128), F32),
        pltpu.VMEM((13, 8, 128), F32),
        pltpu.VMEM((4, 32, 128), jnp.int32),
        pltpu.VMEM((8, 128), jnp.int32),
        pltpu.VMEM((8, 128), jnp.int32),
        pltpu.VMEM((8, 128), jnp.int32),
        pltpu.VMEM((16, 128), jnp.int32),
        pltpu.SMEM((16, 128), jnp.int32),
        pltpu.SemaphoreType.DMA((SEMS,)),
        pltpu.SemaphoreType.DMA((SEMS,)),
        pltpu.SemaphoreType.DMA((10,)),
    ]
    context, loss, grad = pl.pallas_call(
        kernel,
        out_shape=(
            jax.ShapeDtypeStruct((1, 8, D), BF16),
            jax.ShapeDtypeStruct((8, 128), F32),
            jax.ShapeDtypeStruct((STORE, E), F32),
        ),
        in_specs=[
            vmem,
            vmem,
            vmem,
            anywhere,
            vmem,
            vmem,
            vmem,
            vmem,
            anywhere,
            anywhere,
        ],
        out_specs=(vmem, vmem, vmem),
        scratch_shapes=scratch,
        compiler_params=pltpu.CompilerParams(
            collective_id=0, has_side_effects=True, vmem_limit_bytes=60 * 1024 * 1024
        ),
        cost_estimate=pl.CostEstimate(
            flops=12 * 10**9, bytes_accessed=20 * 10**6, transcendentals=10**6
        ),
    )(
        passage_ids.T,
        store_slot.reshape(64, 128),
        row_question,
        store_states,
        store_keys,
        queries,
        question_emb,
        enc_gain.reshape(1, D),
        key_weight,
        value_weight,
    )
    return pl.pallas_call(
        hand_over,
        out_shape=(
            jax.ShapeDtypeStruct((1, 8, D), BF16),
            jax.ShapeDtypeStruct((1,), F32),
            jax.ShapeDtypeStruct((STORE, E), F32),
        ),
        in_specs=[vmem, vmem, vmem],
        out_specs=(vmem, pl.BlockSpec(memory_space=pltpu.SMEM), vmem),
    )(context, loss, grad)


def solution(mesh):
    in_specs = (
        P(("group", "dev"), None, None),
        P(("group", "dev"), None),
        P(),
        P(),
        P("group", None),
        P(("group", "dev"), None, None),
        P(("group", "dev"), None),
        P(),
        P(),
        P(),
    )
    out_specs = (P(("group", "dev"), None, None), P(("group", "dev")), P(("group", "dev"), None))
    return jax.shard_map(body, mesh=mesh, in_specs=in_specs, out_specs=out_specs, check_vma=False)
```

```python
import functools

import jax
import jax.numpy as jnp
from jax import lax
from jax.experimental import pallas as pl
from jax.experimental.pallas import tpu as pltpu
from jax.sharding import PartitionSpec as P

MESH = pl.DeviceIdType.MESH
F32 = jnp.float32
BF16 = jnp.bfloat16
HIGHEST = lax.Precision.HIGHEST

D = 2048
E = 768
GROUPS = 4
PER_GROUP = 32
SLOTS = 16
LANES = 128
STORE = 64
EPS = 1e-06
LOSS_WEIGHT = 256.0
ABSENT = -1e30

ORDERS = (("x", "y", "z"), ("y", "z", "x"), ("z", "x", "y"))
AG, AG_SIB, RQ, SWAP, AR, FIN, RS, LOSS = 0, 27, 39, 42, 44, 71, 74, 113
SEMS = 126


def nt(a, b, precision=None):
    return lax.dot_general(
        a, b, (((1,), (1,)), ((), ())), preferred_element_type=F32, precision=precision
    )


def nn(a, b, precision=None):
    return jnp.dot(a, b, preferred_element_type=F32, precision=precision)


def iota(shape, dim):
    return lax.broadcasted_iota(jnp.int32, shape, dim)


def block_of(part, g, j):
    y, x, core = j // 8, (j // 2) % 4, j % 2
    at = {"x": x, "y": y, "z": g}
    first, second, third = ORDERS[part]
    return core * 64 + at[third] * 16 + at[second] * 4 + at[first]


def log_add(values):
    top = values[0]
    for value in values[1:]:
        top = jnp.maximum(top, value)
    total = jnp.exp(values[0] - top)
    for value in values[1:]:
        total = total + jnp.exp(value - top)
    return top + jnp.log(total)


def kernel(
    ids_ref,
    slot_ref,
    rq_ref,
    states_ref,
    keys_ref,
    queries_ref,
    emb_ref,
    gain_ref,
    kw_ref,
    vw_ref,
    ctx_ref,
    loss_ref,
    grad_ref,
    st,
    w,
    row_ref,
    row_smem,
    nrm,
    kv,
    keys_t,
    q0,
    q1,
    q2,
    c0,
    c1,
    c2,
    rc0,
    rc1,
    rc2,
    ra0,
    ra1,
    ra2,
    rb0,
    rb1,
    rb2,
    rd0,
    rd1,
    rd2,
    s_buf,
    p_buf,
    t_ref,
    o_ref,
    accs,
    ars,
    fin,
    e_ref,
    e_in,
    rqt,
    lane_ref,
    ir_ref,
    lam_ref,
    block_ref,
    block_smem,
    send_sem,
    recv_sem,
    local_sem,
):
    qs, cs, rcs = (q0, q1, q2), (c0, c1, c2), (rc0, rc1, rc2)
    rstage = ((ra0, ra1, ra2), (rb0, rb1, rb2), (rd0, rd1, rd2))
    my_group = lax.axis_index("group")
    my_dev = lax.axis_index("dev")
    core = my_dev % 2
    at = {"x": (my_dev // 2) % 4, "y": my_dev // 8, "z": my_group}
    sibling = (my_group, my_dev + 1 - 2 * core)

    def peer(axis, step):
        to = (at[axis] + step) % 4
        if axis == "z":
            return (to, my_dev)
        if axis == "y":
            return (my_group, to * 8 + at["x"] * 2 + core)
        return (my_group, at["y"] * 8 + to * 2 + core)

    started = []

    def remote(src, dst, number, device):
        copy = pltpu.make_async_remote_copy(
            src_ref=src,
            dst_ref=dst,
            send_sem=send_sem.at[number],
            recv_sem=recv_sem.at[number],
            device_id=device,
            device_id_type=MESH,
        )
        return copy

    def start(src, dst, number, device):
        copy = remote(src, dst, number, device)
        copy.start()
        started.append(copy)

    def arrived(dst, number):
        remote(dst, dst, number, sibling).wait_recv()

    def cross(step):
        return (my_group, at["y"] * 8 + (at["x"] + step) % 4 * 2 + 1 - core)

    barrier = pltpu.get_barrier_semaphore()
    pl.semaphore_signal(barrier, inc=1, device_id=sibling, device_id_type=MESH)
    for step in (1, 2, 3):
        for axis in ("x", "y", "z"):
            pl.semaphore_signal(barrier, inc=1, device_id=peer(axis, step), device_id_type=MESH)
        pl.semaphore_signal(barrier, inc=1, device_id=cross(step), device_id_type=MESH)

    states_copy = pltpu.make_async_copy(states_ref, st, local_sem.at[8])
    states_copy.start()
    w_copies = []
    for n in range(8):
        src = kw_ref if n < 4 else vw_ref
        copy = pltpu.make_async_copy(
            src.at[:, pl.ds((n % 4) * 512, 512)],
            w.at[:, pl.ds(n * 512, 512)],
            local_sem.at[n],
        )
        copy.start()
        w_copies.append(copy)

    mine = [
        core * 64 + at[ORDERS[p][2]] * 16 + at[ORDERS[p][1]] * 4 + at[ORDERS[p][0]]
        for p in range(3)
    ]
    for c in range(8):
        tile = jnp.concatenate(
            [
                queries_ref[0, :, c * 128 : c * 128 + 128].astype(F32),
                queries_ref[0, :, 1024 + c * 128 : 1152 + c * 128].astype(F32),
            ],
            axis=0,
        )
        qs[c // 3][mine[c // 3], :, (c % 3) * 128 : (c % 3) * 128 + 128] = tile.astype(BF16)
    emb_rows = [emb_ref[:, c * 128 : c * 128 + 128].astype(F32) for c in range(6)]
    emb_tile = jnp.concatenate(emb_rows + [jnp.zeros((10, 128), F32)], axis=0)
    q2[mine[2], :, 256:384] = emb_tile.astype(BF16)
    diagonal = iota((32, 32), 0) == iota((32, 32), 1)
    rq_col = jnp.sum(jnp.where(diagonal, rq_ref[...], 0), axis=1, keepdims=True)
    rqt[my_group] = jnp.broadcast_to(rq_col, (32, 128))

    pl.semaphore_wait(barrier, 13)

    def span(p, stage, back):
        first, second, third = ORDERS[p]
        digit = (at[ORDERS[p][stage]] + 4 - back) % 4
        if stage == 0:
            return core * 64 + at[third] * 16 + at[second] * 4 + digit, 1
        if stage == 1:
            return core * 64 + at[third] * 16 + digit * 4, 4
        return core * 64 + digit * 16, 16

    def gather_start(stage):
        for p in range(3):
            begin, size = span(p, stage, 0)
            for step in (1, 2, 3):
                ref = qs[p].at[pl.ds(begin, size)]
                start(ref, ref, AG + (p * 3 + stage) * 3 + step - 1, peer(ORDERS[p][stage], step))

    def gather_wait(p, stage, step):
        begin, size = span(p, stage, step)
        arrived(qs[p].at[pl.ds(begin, size)], AG + (p * 3 + stage) * 3 + step - 1)

    def forward(p, back):
        begin, size = span(p, 2, back)
        ref = qs[p].at[pl.ds(begin, size)]
        start(ref, ref, AG_SIB + p * 4 + back, sibling)

    gather_start(0)
    for step in (1, 2, 3):
        start(rqt.at[my_group], rqt.at[my_group], RQ + step - 1, peer("z", step))

    lane = iota((1, 128), 1)
    sub = iota((128, 128), 0)
    lanes = iota((128, 128), 1)
    first_row = (my_group * PER_GROUP + my_dev) * STORE
    local = slot_ref[...] - first_row
    local = jnp.where((local >= 0) & (local < STORE), local + 1, 0).astype(F32)
    local_t = jnp.transpose(local).astype(BF16)
    ids_high = ids_ref[...] // 128
    ids_low = ids_ref[...] % 128
    high_sub = iota((64, 128), 0)
    lane32 = iota((128, 32), 1)
    held_rows = []
    for k in range(32):
        hot = jnp.where(high_sub == ids_high[k : k + 1, :], 1.0, 0.0).astype(BF16)
        found = jnp.where(sub == ids_low[k : k + 1, :], nn(local_t, hot), 0.0)
        held_rows.append(jnp.sum(found, axis=0, keepdims=True))
    held = jnp.transpose(jnp.concatenate(held_rows, axis=0))
    for p in range(3):
        for step in (1, 2, 3):
            gather_wait(p, 0, step)
    gather_start(1)

    held_int = held.astype(jnp.int32)
    mine_f = jnp.where(held_int > 0, 1.0, 0.0)
    mine_b = mine_f.astype(BF16)
    in_row = nn(mine_b, jnp.ones((32, 32), BF16))
    above = jnp.where((sub // 32 == lanes // 32) & (lanes < sub), 1.0, 0.0).astype(BF16)
    upto = jnp.where(iota((32, 32), 0) <= iota((32, 32), 1), 1.0, 0.0).astype(BF16)
    rank = nn(above, in_row.astype(BF16)) + nn(mine_b, upto)
    rank = jnp.where(held_int > 0, rank.astype(jnp.int32), 0)
    code = (iota((128, 32), 0) % 32) * 4096 + lane32 * 128 + held_int
    spread = jnp.zeros((128, 128), jnp.int32)
    for n in range(SLOTS):
        here = jnp.sum(jnp.where(rank == n + 1, code, 0), axis=1, keepdims=True)
        spread = jnp.where(lanes // 8 == n, here, spread)
    code_cols = []
    slot16 = iota((16, 128), 1) == iota((16, 128), 0) * 8
    for g in range(4):
        code_row = jnp.sum(spread[g * 32 : g * 32 + 32], axis=0, keepdims=True)
        lane_ref[g : g + 1, :] = jnp.where(code_row > 0, code_row // 4096, -1)
        code_cols.append(jnp.sum(jnp.where(slot16, code_row, 0), axis=1, keepdims=True))
        row_ref[g : g + 1, :] = jnp.maximum(code_row % 128 - 1, 0)
    row_copy = pltpu.make_async_copy(row_ref, row_smem, local_sem.at[10])
    row_copy.start()
    code_col = jnp.concatenate(code_cols, axis=0)
    valid = code_col > 0
    k_col = (code_col // 128) % 32
    row_col = code_col % 128 - 1
    square = iota((64, 64), 0) == iota((64, 64), 1)
    code_row64 = jnp.sum(jnp.where(square, code_col, 0), axis=0, keepdims=True)
    k_row = (code_row64 // 128) % 32
    row_row = code_row64 % 128 - 1

    states_copy.wait()

    row_copy.wait()

    def norm_slots(four, carry):
        both = []
        for n in range(4):
            values = st[row_smem[four // 4, (four % 4) * 32 + n * 8]].astype(F32)
            mean_square = jnp.mean(values * values, axis=-1, keepdims=True)
            both.append(values * lax.rsqrt(mean_square + EPS) * gain_ref[...])
        rows = pl.ds(pl.multiple_of(four * 32, 32), 32)
        nrm[rows, :] = jnp.concatenate(both, axis=0).astype(BF16)
        return carry

    lax.fori_loop(0, 16, norm_slots, 0)

    for p in range(3):
        for step in (1, 2, 3):
            gather_wait(p, 1, step)
    gather_start(2)
    for p in range(3):
        forward(p, 0)

    for step in (1, 2, 3):
        arrived(rqt.at[(my_group + 4 - step) % 4], RQ + step - 1)
    for g in range(4):
        match = rqt[g] == lane_ref[g : g + 1, :]
        row = jnp.sum(jnp.where(match, iota((32, 128), 0) + (g * 32 + 1), 0), axis=0, keepdims=True)
        ir_ref[g : g + 1, :] = row - 1
    decoder_of = jnp.maximum(ir_ref[0:4, :], 0)
    for p in range(3):
        block_ref[p * 4 : p * 4 + 4, :] = block_of(p, decoder_of // 32, decoder_of % 32)
    lam_ref[0:4, :] = jnp.where(ir_ref[0:4, :] >= 0, block_ref[0:4, :], -1)
    block_copy = pltpu.make_async_copy(block_ref, block_smem, local_sem.at[9])
    block_copy.start()

    def project(begin, end):
        def step(n, carry):
            offset = pl.multiple_of(n * 256, 256)
            kv[:, pl.ds(offset, 256)] = nn(nrm[...], w[:, pl.ds(offset, 256)]).astype(BF16)
            return carry

        for n in range(begin, end):
            w_copies[n].wait()
        lax.fori_loop(begin * 2, end * 2, step, 0)

    project(0, 4)
    for step in (1, 3, 2):
        for p in range(3):
            gather_wait(p, 2, step)
            forward(p, step)
    def turn(n, carry):
        rows = pl.ds(pl.multiple_of(n * 256, 256), 256)
        keys_t[rows, :] = jnp.transpose(kv[:, rows])
        return carry

    lax.fori_loop(0, 8, turn, 0)
    project(4, 7)
    block_copy.wait()

    for p in range(3):
        for back in range(4):
            first, second, third = ORDERS[p]
            begin = (1 - core) * 64 + ((at[third] + 4 - back) % 4) * 16
            arrived(qs[p].at[pl.ds(begin, 16)], AG_SIB + p * 4 + back)

    low = (lane < 64).astype(F32).astype(BF16)
    high = (lane >= 64).astype(F32).astype(BF16)

    def scores_of(p, tiles):
        def step(cc, carry):
            inner = pl.multiple_of(cc * 128, 128)
            outer = pl.multiple_of((3 * p + cc) * 128, 128)
            rows = pl.ds(pl.multiple_of((3 * p + cc) * 16, 16), 16)
            high_rows = pl.ds(pl.multiple_of((3 * p + cc) * 16 + 128, 16), 16)
            for g in range(4):
                slots = slice(g * 128, g * 128 + 128)
                right = jnp.concatenate(
                    [keys_t[pl.ds(outer, 128), slots], keys_t[pl.ds(outer + 1024, 128), slots]],
                    axis=1,
                )
                left = []
                for r in range(SLOTS):
                    block = qs[p][block_smem[p * 4 + g, r * 8], :, pl.ds(inner, 128)]
                    left += [block * low, block * high]
                out = nn(jnp.concatenate(left, axis=0), right)
                total = [jnp.zeros((8, 128), F32) for _ in range(4)]
                for r in range(SLOTS):
                    keep = jnp.broadcast_to(lane // 8 == r, (8, 128))
                    for tile in range(4):
                        half = tile % 2
                        begin = r * 32 + tile * 8
                        piece = out[begin : begin + 8, half * 128 : half * 128 + 128]
                        total[tile] = jnp.where(keep, piece, total[tile])
                s_buf[g, rows, :] = jnp.concatenate(total[0:2], axis=0) * (64 ** (-0.5))
                s_buf[g, high_rows, :] = jnp.concatenate(total[2:4], axis=0) * (64 ** (-0.5))
            return carry

        lax.fori_loop(0, tiles, step, 0)

    scores_of(0, 3)
    scores_of(1, 3)
    scores_of(2, 2)

    peak_i = jnp.zeros((256, 128), F32)
    total_i = jnp.zeros((256, 128), F32)
    present = jnp.zeros((8, 128), F32)
    for g in range(4):
        scores = s_buf[g]
        u_row = lane_ref[g : g + 1, :]
        peak = scores
        for s in (1, 2, 4):
            bit = jnp.broadcast_to((lane // s) % 2 == 1, (256, 128))
            other = jnp.where(bit, pltpu.roll(peak, s, 1), pltpu.roll(peak, 128 - s, 1))
            peak = jnp.maximum(peak, other)
        u_rows = jnp.broadcast_to(u_row, (8, 128))
        before = pltpu.roll(u_rows, 8, 1)[0:1, :]
        for s in (8, 16, 32, 64):
            same = (pltpu.roll(u_rows, s, 1)[0:1, :] == u_row) & (lane >= s)
            other = jnp.where(jnp.broadcast_to(same, (256, 128)), pltpu.roll(peak, s, 1), ABSENT)
            peak = jnp.maximum(peak, other)
        for s in (8, 16, 32, 64):
            same = (pltpu.roll(u_rows, 128 - s, 1)[0:1, :] == u_row) & (lane < 128 - s)
            other = jnp.where(
                jnp.broadcast_to(same, (256, 128)), pltpu.roll(peak, 128 - s, 1), ABSENT
            )
            peak = jnp.maximum(peak, other)
        chosen = sub == lam_ref[g : g + 1, :]
        first = ((before != u_row) | (lane < 8)) & (lane % 8 == 0)
        lead = jnp.where(chosen & jnp.broadcast_to(first, (128, 128)), 1.0, 0.0)
        peak_i = peak_i + nt(peak, lead, HIGHEST)
        total_i = total_i + nt(jnp.exp(scores - peak), jnp.where(chosen, 1.0, 0.0), HIGHEST)
        present = present + nt(jnp.ones((8, 128), F32), lead)
    table = jnp.where(
        jnp.broadcast_to(present[0:1, :] > 0.5, (256, 128)),
        peak_i + jnp.log(jnp.maximum(total_i, 1e-30)),
        ABSENT,
    )
    t_ref[0:256, :] = table
    start(t_ref.at[pl.ds(0, 256)], o_ref.at[pl.ds(0, 256)], SWAP, sibling)

    lane64 = iota((64, 128), 1)
    i_cols, lam_cols = [], []
    for g in range(4):
        picked = jnp.where(slot16, ir_ref[g : g + 1, :] + 1, 0)
        i_cols.append(jnp.sum(picked, axis=1, keepdims=True))
        picked = jnp.where(slot16, lam_ref[g : g + 1, :] + 1, 0)
        lam_cols.append(jnp.sum(picked, axis=1, keepdims=True))
    i_col = jnp.concatenate(i_cols, axis=0) - 1
    one_hot_i = lane64 == jnp.concatenate(lam_cols, axis=0) - 1
    hot_i = jnp.where(one_hot_i, 1.0, 0.0)
    decoder = jnp.maximum(i_col, 0)
    place = block_of(2, decoder // 32, decoder % 32) * 16
    flat = q2[:, :, 256:384].reshape(2048, 128)
    wide = iota((64, 2048), 1)
    emb = jnp.concatenate(
        [nn(jnp.where(wide == place + c, 1.0, 0.0).astype(BF16), flat) for c in range(6)], axis=1
    )
    hot_row = jnp.where(iota((64, 64), 1) == row_col, 1.0, 0.0).astype(BF16)
    keys = nn(hot_row, keys_ref[...])
    retrieval = jnp.sum(emb * keys, axis=1, keepdims=True) * (E ** (-0.5))
    retrieval_row = jnp.sum(jnp.where(square, retrieval, 0.0), axis=0, keepdims=True)
    by_k = jnp.where(iota((32, 64), 0) == k_row, retrieval_row, 0.0)
    t_ref[256:288, :] = nn(by_k, hot_i, HIGHEST)
    start(t_ref.at[pl.ds(256, 32)], o_ref.at[pl.ds(256, 32)], SWAP + 1, sibling)
    project(7, 8)

    low_lanes = lane < 64

    def pack(first, second, of):
        zero = jnp.where(low_lanes, first, pltpu.roll(second, 64, 1))
        one = jnp.where(low_lanes, pltpu.roll(first, 64, 1), second)
        return jnp.where(of == 0, zero, one)

    arrived(o_ref.at[pl.ds(0, 256)], SWAP)
    arrived(o_ref.at[pl.ds(256, 32)], SWAP + 1)
    pair = log_add([t_ref[0:256, :], o_ref[0:256, :]])
    pair_raw = t_ref[256:288, :] + o_ref[256:288, :]
    packed = pack(pair[0:128], pair[128:256], core)
    accs[0, 0] = packed[0:48]
    accs[1, 0] = packed[48:96]
    accs[2, 0] = jnp.concatenate([packed[96:128], pack(pair_raw[0:16], pair_raw[16:32], core)], axis=0)

    def table_copy(p, stage, step):
        return remote(
            accs.at[p, stage],
            ars.at[p, stage * 3 + step - 1],
            AR + p * 9 + stage * 3 + step - 1,
            peer(ORDERS[p][2 - stage], step),
        )

    def table_start(stage):
        for p in range(3):
            for step in (1, 2, 3):
                table_copy(p, stage, step).start()

    def table_finish(stage):
        for p in range(3):
            values = [accs[p, stage]]
            for step in (1, 2, 3):
                arrived(ars.at[p, stage * 3 + step - 1], AR + p * 9 + stage * 3 + step - 1)
                values.append(ars[p, stage * 3 + step - 1])
            if p < 2:
                accs[p, stage + 1] = log_add(values)
            else:
                raw = values[0][32:48] + values[1][32:48] + values[2][32:48] + values[3][32:48]
                total = log_add([value[0:32] for value in values])
                accs[p, stage + 1] = jnp.concatenate([total, raw], axis=0)

    table_start(0)
    while started:
        started.pop(0).wait_send()

    for g in range(4):
        chosen = jnp.where(sub == lam_ref[g : g + 1, :], 1.0, 0.0)
        used = jnp.broadcast_to(lam_ref[g : g + 1, :] >= 0, (256, 128))
        p_buf[g] = jnp.where(used, jnp.exp(s_buf[g] - nn(pair, chosen, HIGHEST)), 0.0).astype(BF16)

    keep_low = jnp.broadcast_to(lane < 64, (8, 128))

    def context_set(p, to):
        tiles = 2 if p == 2 else 3

        def tile_of(g, cc, decoders):
            inner = cc * 128
            outer = D + (3 * p + cc) * 128
            slots = pl.ds(pl.multiple_of(g * 128, 128), 128)
            right = jnp.concatenate(
                [kv[slots, pl.ds(outer, 128)], kv[slots, pl.ds(outer + 1024, 128)]], axis=1
            )
            row = ir_ref[pl.ds(g, 1), :] - g * 32
            c = 3 * p + cc
            weights = jnp.concatenate(
                [p_buf[g, pl.ds(c * 16, 16), :], p_buf[g, pl.ds(128 + c * 16, 16), :]], axis=0
            )
            for first in range(0, len(decoders), 16):
                batch = decoders[first : first + 16]
                left = []
                for j in batch:
                    keep = jnp.where(row == j, 1.0, 0.0).astype(BF16)
                    left.append(weights * keep)
                out = nn(jnp.concatenate(left, axis=0), right)
                for n, j in enumerate(batch):
                    halves = []
                    for half in range(2):
                        cols = slice(half * 128, half * 128 + 128)
                        begin = n * 32 + half * 8
                        halves.append(
                            jnp.where(
                                keep_low,
                                out[begin : begin + 8, cols],
                                out[begin + 16 : begin + 24, cols],
                            )
                        )
                    tile = jnp.concatenate(halves, axis=0).astype(BF16)
                    cs[p][block_of(p, g, j), :, pl.ds(inner, 128)] = tile

        if p == 0:

            for cc in range(tiles):
                tile_of(to, cc, list(range(32)))
        else:

            def step(n, carry):
                if p == 1:
                    decoders = [y * 8 + to * 2 + c for y in range(4) for c in range(2)]
                else:
                    decoders = [to * 8 + x * 2 + c for x in range(4) for c in range(2)]
                for g in (2 * n, 2 * n + 1):
                    for cc in range(tiles):
                        tile_of(g, cc, decoders)
                return carry

            lax.fori_loop(0, 2, step, 0)

    def reach(p, stage, to):
        first, second, third = ORDERS[p]
        if stage == 0:
            return core * 64 + to * 16, 16
        if stage == 1:
            return core * 64 + at[third] * 16 + to * 4, 4
        return core * 64 + at[third] * 16 + at[second] * 4 + to, 1

    def set_of(p, n):
        return (at[ORDERS[p][2]] + n + 1) % 4

    def swap_copy(p, n):
        to = set_of(p, n)
        return remote(
            cs[p].at[pl.ds((1 - core) * 64 + to * 16, 16)],
            rcs[p].at[pl.ds(to * 16, 16)],
            RS + p * 13 + n,
            sibling,
        )

    def scatter_copy(p, stage, step):
        axis = ORDERS[p][2 - stage]
        begin, count = reach(p, stage, (at[axis] + step) % 4)
        return remote(
            cs[p].at[pl.ds(begin, count)],
            rstage[stage][p].at[pl.ds((step - 1) * count, count)],
            RS + p * 13 + 4 + stage * 3 + step - 1,
            peer(axis, step),
        )

    def scatter_start(p, stage):
        for step in (1, 2, 3):
            copy = scatter_copy(p, stage, step)
            copy.start()
            started.append(copy)

    def swap_finish(p, n):
        to = set_of(p, n)
        arrived(rcs[p].at[pl.ds(to * 16, 16)], RS + p * 13 + n)

        def step(four, carry):
            places = [four * 4 + n for n in range(4)]
            sums = [
                (
                    cs[p][core * 64 + to * 16 + b].astype(F32) + rcs[p][to * 16 + b].astype(F32)
                ).astype(BF16)
                for b in places
            ]
            for b, block in zip(places, sums):
                cs[p][core * 64 + to * 16 + b] = block
            return carry

        lax.fori_loop(0, 4, step, 0)

        @pl.when(n < 3)
        def _():
            scatter_copy(p, 0, n + 1).start()

    def scatter_wait(p, stage):
        count = (16, 4, 1)[stage]
        for step in (1, 2, 3):
            arrived(
                rstage[stage][p].at[pl.ds((step - 1) * count, count)],
                RS + p * 13 + 4 + stage * 3 + step - 1,
            )

    def scatter_sum(p, stage):
        axis = ORDERS[p][2 - stage]
        tiles = 2 if p == 2 else 3
        begin, count = reach(p, stage, at[axis])
        scatter_wait(p, stage)
        after = accs[p, stage + 1][0 : tiles * 16]
        tables = [accs[p, stage]] + [ars[p, stage * 3 + n] for n in range(3)]
        wide_lane = iota((1, count * 128), 1)
        place_of = begin - core * 64 + wide_lane // 128
        digits = {
            ORDERS[p][2]: place_of // 16,
            ORDERS[p][1]: (place_of // 4) % 4,
            ORDERS[p][0]: place_of % 4,
        }
        packed_lane = (wide_lane % 128) // 64 * 64 + digits["z"] * 16 + digits["y"] * 4 + digits["x"]
        spread_hot = jnp.where(iota((128, count * 128), 0) == packed_lane, 1.0, 0.0).astype(BF16)
        factors = [
            nn(jnp.exp(table[0 : tiles * 16] - after).astype(BF16), spread_hot) for table in tables
        ]
        sums = []
        for b in range(count):
            blocks = [cs[p][begin + b]] + [rstage[stage][p][n * count + b] for n in range(3)]
            cols = []
            for cc in range(tiles):
                total = jnp.zeros((16, 128), F32)
                for block, factor in zip(blocks, factors):
                    part = factor[cc * 16 : cc * 16 + 16, b * 128 : b * 128 + 128]
                    total = total + block[:, cc * 128 : cc * 128 + 128].astype(F32) * part
                cols.append(total)
            sums.append(cols)
        return begin, sums

    def scatter_add(p, stage):
        begin, sums = scatter_sum(p, stage)
        for b, cols in enumerate(sums):
            cs[p][begin + b] = jnp.concatenate(cols, axis=1).astype(BF16)

    def final_copy(p):
        return remote(accs.at[p, 3], fin.at[p], FIN + p, sibling)

    def scatter_set(n, carry):
        for p in range(3):
            context_set(p, set_of(p, n))
            swap_copy(p, n).start()
            if p > 0:
                swap_finish(p - 1, n)
            else:

                @pl.when(n > 0)
                def _():
                    swap_finish(2, n - 1)

        for stage in range(3):

            @pl.when(n == stage)
            def _(stage=stage):
                table_finish(stage)
                if stage < 2:
                    table_start(stage + 1)
                else:
                    for p in range(3):
                        final_copy(p).start()

        return carry

    lax.fori_loop(0, 4, scatter_set, 0)
    swap_finish(2, 3)
    for p in range(3):
        started.extend(swap_copy(p, n) for n in range(4))
        started.extend(scatter_copy(p, 0, step) for step in (1, 2, 3))

    for p in range(3):
        started.extend(table_copy(p, stage, step) for stage in range(3) for step in (1, 2, 3))
        started.append(final_copy(p))

    for p in range(3):
        arrived(fin.at[p], FIN + p)
    own_sum = jnp.concatenate([accs[0, 3], accs[1, 3], accs[2, 3]], axis=0)
    other_sum = jnp.concatenate([fin[0], fin[1], fin[2]], axis=0)
    zero_sum = jnp.where(core == 0, own_sum, other_sum)
    one_sum = jnp.where(core == 0, other_sum, own_sum)
    first_half = jnp.where(low_lanes, zero_sum, pltpu.roll(one_sum, 64, 1))
    second_half = jnp.where(low_lanes, pltpu.roll(zero_sum, 64, 1), one_sum)
    log_sum = jnp.concatenate([first_half[0:128], second_half[0:128]], axis=0)
    raw = jnp.concatenate([first_half[128:144], second_half[128:144]], axis=0)
    targets = []
    for g in range(4):
        chosen = jnp.where(sub == lam_ref[g : g + 1, :], 1.0, 0.0)
        mass = jnp.exp(s_buf[g] - nn(log_sum, chosen, HIGHEST))
        mass = jnp.sum(mass, axis=0, keepdims=True)
        own = iota((16, 128), 1) // 8 == iota((16, 128), 0)
        targets.append(jnp.sum(jnp.where(own, mass, 0.0), axis=1, keepdims=True))
    target = jnp.concatenate(targets, axis=0) * (1.0 / 256.0)
    top = jnp.max(raw, axis=0, keepdims=True)
    log_prob_all = raw - top - jnp.log(jnp.sum(jnp.exp(raw - top), axis=0, keepdims=True))
    hot_k = jnp.where(iota((64, 32), 1) == k_col, 1.0, 0.0)
    log_prob = jnp.sum(
        jnp.where(one_hot_i, nn(hot_k, log_prob_all, HIGHEST), 0.0), axis=1, keepdims=True
    )
    term = jnp.where(valid, target * (jnp.log(target) - log_prob), 0.0)
    loss_row = jnp.sum(jnp.where(one_hot_i, term, 0.0), axis=0, keepdims=True)

    def loss_start(stage):
        if stage == 0:
            start(e_ref.at[0], e_in.at[0], LOSS, sibling)
            for step in (1, 2, 3):
                start(e_ref.at[0], e_in.at[step], LOSS + step, peer("x", step))
                start(e_ref.at[0], e_in.at[3 + step], LOSS + 3 + step, cross(step))
        else:
            for step in (1, 2, 3):
                n = 3 + stage * 3 + step
                start(e_ref.at[stage], e_in.at[n], LOSS + n, peer("xyz"[stage], step))

    def loss_sum(stage):
        total = e_ref[stage]
        for n in range(7) if stage == 0 else range(4 + stage * 3, 7 + stage * 3):
            arrived(e_in.at[n], LOSS + n)
            total = total + e_in[n]
        return total

    e_ref[0] = jnp.broadcast_to(loss_row, (8, 128))
    loss_start(0)
    for p in range(3):
        scatter_add(p, 0)
        scatter_start(p, 1)
    e_ref[1] = loss_sum(0)
    loss_start(1)

    coefficient = (LOSS_WEIGHT * E ** (-0.5)) * (jnp.exp(log_prob) - target)
    grads = jnp.where(valid, coefficient * emb, 0.0).astype(BF16)
    hot_row_t = jnp.where(iota((64, 64), 0) == row_row, 1.0, 0.0).astype(BF16)
    grad_ref[...] = nn(hot_row_t, grads)

    for p in range(3):
        scatter_add(p, 1)
        scatter_start(p, 2)
    e_ref[2] = loss_sum(1)
    loss_start(2)
    for p in range(3):
        _, sums = scatter_sum(p, 2)
        for cc, total in enumerate(sums[0]):
            c = 3 * p + cc
            ctx_ref[0, :, c * 128 : c * 128 + 128] = total[0:8].astype(BF16)
            ctx_ref[0, :, 1024 + c * 128 : 1152 + c * 128] = total[8:16].astype(BF16)
    loss_all = jnp.sum(jnp.where(lane == mine[0], loss_sum(2)[0:1, :], 0.0), axis=1, keepdims=True)
    loss_ref[...] = jnp.broadcast_to(loss_all, (8, 128))

    for copy in started:
        copy.wait_send()


def hand_over(ctx_ref, loss_ref, grad_ref, ctx_out, loss_out, grad_out):
    ctx_out[...] = ctx_ref[...]
    loss_out[0] = loss_ref[0, 0]
    grad_out[...] = grad_ref[...]


def body(
    store_states,
    store_keys,
    passage_ids,
    store_slot,
    row_question,
    queries,
    question_emb,
    enc_gain,
    key_weight,
    value_weight,
):
    vmem = pl.BlockSpec(memory_space=pltpu.VMEM)
    anywhere = pl.BlockSpec(memory_space=pl.ANY)
    scratch = [
        pltpu.VMEM((64, 8, D), BF16),
        pltpu.VMEM((D, 2 * D), BF16),
        pltpu.VMEM((8, 128), jnp.int32),
        pltpu.SMEM((8, 128), jnp.int32),
        pltpu.VMEM((512, D), BF16),
        pltpu.VMEM((512, 2 * D), BF16),
        pltpu.VMEM((D, 512), BF16),
    ]
    scratch += [pltpu.VMEM((128, 16, 384), BF16)] * 3
    for blocks in (128, 64, 48, 12, 3):
        scratch += [pltpu.VMEM((blocks, 16, lanes), BF16) for lanes in (384, 384, 256)]
    scratch += [pltpu.VMEM((4, 256, 128), F32), pltpu.VMEM((4, 256, 128), BF16)]
    scratch += [
        pltpu.VMEM((288, 128), F32),
        pltpu.VMEM((288, 128), F32),
        pltpu.VMEM((3, 4, 48, 128), F32),
        pltpu.VMEM((3, 9, 48, 128), F32),
        pltpu.VMEM((3, 48, 128), F32),
        pltpu.VMEM((3, 8, 128), F32),
        pltpu.VMEM((13, 8, 128), F32),
        pltpu.VMEM((4, 32, 128), jnp.int32),
        pltpu.VMEM((8, 128), jnp.int32),
        pltpu.VMEM((8, 128), jnp.int32),
        pltpu.VMEM((8, 128), jnp.int32),
        pltpu.VMEM((16, 128), jnp.int32),
        pltpu.SMEM((16, 128), jnp.int32),
        pltpu.SemaphoreType.DMA((SEMS,)),
        pltpu.SemaphoreType.DMA((SEMS,)),
        pltpu.SemaphoreType.DMA((11,)),
    ]
    context, loss, grad = pl.pallas_call(
        kernel,
        out_shape=(
            jax.ShapeDtypeStruct((1, 8, D), BF16),
            jax.ShapeDtypeStruct((8, 128), F32),
            jax.ShapeDtypeStruct((STORE, E), F32),
        ),
        in_specs=[
            vmem,
            vmem,
            vmem,
            anywhere,
            vmem,
            vmem,
            vmem,
            vmem,
            anywhere,
            anywhere,
        ],
        out_specs=(vmem, vmem, vmem),
        scratch_shapes=scratch,
        compiler_params=pltpu.CompilerParams(
            collective_id=0, has_side_effects=True, vmem_limit_bytes=60 * 1024 * 1024
        ),
        cost_estimate=pl.CostEstimate(
            flops=12 * 10**9, bytes_accessed=20 * 10**6, transcendentals=10**6
        ),
    )(
        passage_ids.T,
        store_slot.reshape(64, 128),
        row_question,
        store_states,
        store_keys,
        queries,
        question_emb,
        enc_gain.reshape(1, D),
        key_weight,
        value_weight,
    )
    return pl.pallas_call(
        hand_over,
        out_shape=(
            jax.ShapeDtypeStruct((1, 8, D), BF16),
            jax.ShapeDtypeStruct((1,), F32),
            jax.ShapeDtypeStruct((STORE, E), F32),
        ),
        in_specs=[vmem, vmem, vmem],
        out_specs=(vmem, pl.BlockSpec(memory_space=pltpu.SMEM), vmem),
    )(context, loss, grad)


def solution(mesh):
    in_specs = (
        P(("group", "dev"), None, None),
        P(("group", "dev"), None),
        P(),
        P(),
        P("group", None),
        P(("group", "dev"), None, None),
        P(("group", "dev"), None),
        P(),
        P(),
        P(),
    )
    out_specs = (P(("group", "dev"), None, None), P(("group", "dev")), P(("group", "dev"), None))
    return jax.shard_map(body, mesh=mesh, in_specs=in_specs, out_specs=out_specs, check_vma=False)
```
